32 devices in a mesh: dp: 8 (over z, x), tensor: 4 (over y, core).
Axes of the slice: x: 2, y: 2, z: 4, core: 2. Of those that a mesh axis runs over, the one named last changes fastest.
Arguments:
- decoder_layer_input: bfloat16 [16, 1024, 512], P('dp'), may hold values from -6 to 6
- encoder_state_rows: bfloat16 [16, 1024, 512], P('dp'), may hold values from -6 to 6
- target_segments: int32 [16, 1024], P('dp'), may hold values from 0 to 3, never falling along the last dimension, each value on 1 to 800 neighbouring positions
- source_segments: int32 [16, 1024], P('dp'), may hold values from 0 to 3, never falling along the last dimension, each value on 1 to 800 neighbouring positions
- valid_mask: int32 [16, 1024], P('dp', 'tensor'), may hold values 0 or 1
- cotangent: float32 [16, 1024, 512], P('dp', 'tensor'), may hold values from -6 to 6
- self_input_projection: bfloat16 [3, 512, 512], P(None, None, 'tensor'), may hold values from -0.25 to 0.25
- self_in_bias: float32 [2, 512], P(None, 'tensor'), may hold values from -3 to 3
- self_out_proj: bfloat16 [512, 512], P('tensor'), may hold values from -1.5 to 1.5
- cross_input_projection: bfloat16 [3, 512, 512], P(None, None, 'tensor'), may hold values from -0.25 to 0.25
- cross_in_bias: float32 [2, 512], P(None, 'tensor'), may hold values from -3 to 3
- cross_out_proj: bfloat16 [512, 512], P('tensor'), may hold values from -1.5 to 1.5
- feed_in_proj: bfloat16 [512, 2048], P(None, 'tensor'), may hold values from -0.25 to 0.25
- feed_in_bias: float32 [2048], P('tensor'), may hold values from -3 to 3
- feed_out_proj: bfloat16 [2048, 512], P('tensor'), may hold values from -0.1875 to 0.1875
- out_bias: float32 [3, 512], replicated, may hold values from -2 to 2
- norm_gain: float32 [3, 512], replicated, may hold values from 0.1 to 1.9
- norm_bias: float32 [3, 512], replicated, may hold values from -2 to 2
Outputs:
- layer_output: bfloat16 [16, 1024, 512], P('dp', 'tensor')
- input_grad: float32 [16, 1024, 512], P('dp', 'tensor')
- encoder_grad: float32 [16, 1024, 512], P('dp', 'tensor')
- self_in_proj_grad: float32 [3, 512, 512], P(None, None, 'tensor')
- self_in_bias_grad: float32 [2, 512], P(None, 'tensor')
- self_out_proj_grad: float32 [512, 512], P('tensor')
- cross_in_proj_grad: float32 [3, 512, 512], P(None, None, 'tensor')
- cross_in_bias_grad: float32 [2, 512], P(None, 'tensor')
- cross_out_proj_grad: float32 [512, 512], P('tensor')
- feed_in_proj_grad: float32 [512, 2048], P(None, 'tensor')
- feed_in_bias_grad: float32 [2048], P('tensor')
- feed_out_proj_grad: float32 [2048, 512], P('tensor')
- out_bias_grad: float32 [3, 512], replicated
- norm_gain_grad: float32 [3, 512], replicated
- norm_bias_grad: float32 [3, 512], replicated
- rms_values: float32 [4], replicated
The draws below stay inside these ranges and needn't reach their ends.
Inputs may be any that keep to these rules, and one draw needn't show every extreme that they name: `target_segments`: document ids of a sequence never fall; each of the 4 ids occurs, at most 800 tokens each, and some document has exactly that many. `source_segments`: document ids of a sequence never fall; each of the 4 ids occurs, at most 800 slots each, and some document has exactly that many.
All inputs are finite; a program needn't handle non-finite values. No bound on the sum of `valid_mask` on one device may be relied on, other than what follows from the above.
Results may differ from the reference program's by a relative error of at most 0.028.
Values may be sent and summed in bfloat16 or wider, within the bound.
No kernel may reach another device: no remote copies, remote signals or barrier semaphores. Data moves between devices by JAX's collectives and lax.ppermute only.
A program may use at most 192 MiB of HBM per device.

```python
import math
import jax
import jax.numpy as jnp
import numpy as np
from jax import lax

D = 512
HEADS = 8
HEAD = 64
FF = 2048
TLEN = 1024
SLEN = 1024
HD = 512
NSEQ = 16
DOCS = 4


def set_ends(drawn, stream_key, least, top_value):
    longest = drawn.shape.index(max(drawn.shape))
    spots = []
    for shift in (0, 1):
        where = [jax.random.randint(jax.random.fold_in(stream_key, axis), (), 0, length) for axis, length in enumerate(drawn.shape)]
        where[longest] = (where[longest] + shift) % drawn.shape[longest]
        spots.append(tuple(where))
    return drawn.at[spots[0]].set(least).at[spots[1]].set(top_value)


def levels(rng, extent, split, smallest, top_value):
    factor_of = 1.0
    for dim, shards_of in split:
        steps = jax.random.uniform(jax.random.fold_in(jax.random.fold_in(rng, 6), dim), (shards_of,), jnp.float32, smallest / len(split), top_value / len(split))
        factor_of = factor_of * jnp.repeat(jnp.exp(steps), extent[dim] // shards_of).reshape((-1,) + (1,) * (len(extent) - 1 - dim))
    return factor_of


def length_profile(count, total, limit, skew):
    weights = [(1 << 20) // math.isqrt(standing ** skew) + 1 for standing in range(2, count + 1)]
    rest, given = total - limit - (count - 1), [1] * (count - 1)
    while rest > 0:
        movable = [i for i in range(count - 1) if given[i] < limit]
        pool, remaining = sum([weights[i] for i in movable]), rest
        for i in movable:
            extra = min(limit - given[i], max(1, remaining * weights[i] // pool), rest)
            given[i] = given[i] + extra
            rest = rest - extra
    return np.array([limit] + given)


def uneven(rng, count, total, reach, lean):
    if count == 2:
        one = jax.random.randint(rng, (), max(1, total - reach), min(reach, total - 1) + 1)
        return jnp.stack([one, total - one])
    tallies = jnp.asarray(length_profile(count, total, reach, lean), jnp.int32)
    twos = (count - 1) // 2
    source_of, taker = tallies[1:1 + 2 * twos:2], tallies[2:2 + 2 * twos:2]
    room = jnp.minimum(source_of - 1, reach - taker)
    shifted = jax.random.randint(jax.random.fold_in(rng, 1), (twos,), 0, 1 << 20) % (room + 1)
    tallies = tallies.at[1:1 + 2 * twos:2].set(source_of - shifted).at[2:2 + 2 * twos:2].set(taker + shifted)
    return tallies[jax.random.permutation(jax.random.fold_in(rng, 2), count)]


def scatter_about(own_key, shape, width, reach, cuts=(), kind=jnp.bfloat16):
    entries = width * jax.random.normal(own_key, shape, jnp.float32)
    if cuts:
        entries = entries * levels(own_key, shape, cuts, -0.22, 0.18)
    return jnp.clip(entries, -reach, reach).astype(kind)


def setup_inputs(seed: int = 0) -> dict:
    splits = jax.random.split(jax.random.key(seed), 19)
    decoder_layer_input = scatter_about(splits[0], (NSEQ, TLEN, D), 1.0, 6.0, ((0, 8),))
    encoder_state_rows = scatter_about(splits[1], (NSEQ, SLEN, D), 1.0, 6.0, ((0, 8),))
    target_segments = jax.vmap(lambda own: jnp.searchsorted(jnp.cumsum(uneven(own, DOCS, TLEN, TLEN * 25 // 32, 1)), jnp.arange(TLEN), side="right"))(jax.random.split(splits[2], NSEQ)).reshape((NSEQ, TLEN)).astype(jnp.int32)
    source_segments = jax.vmap(lambda own: jnp.searchsorted(jnp.cumsum(uneven(own, DOCS, SLEN, SLEN * 25 // 32, 1)), jnp.arange(SLEN), side="right"))(jax.random.split(splits[3], NSEQ)).reshape((NSEQ, SLEN)).astype(jnp.int32)
    valid_mask = set_ends((jax.random.randint(splits[4], (NSEQ, TLEN), 0, 4) < 3).astype(jnp.int32), jax.random.fold_in(splits[4], 1), 0, 1)
    cotangent = scatter_about(splits[5], (NSEQ, TLEN, D), 1.0, 6.0, ((0, 8), (1, 4)), jnp.float32)
    self_input_projection = scatter_about(splits[6], (3, D, HD), D ** -0.5, 0.25, ((2, 4),))
    self_in_bias = scatter_about(splits[7], (2, HD), 0.5, 3.0, ((1, 4),), jnp.float32)
    self_out_proj = scatter_about(splits[8], (HD, D), (HD // 32) ** -0.5, 1.5, ((0, 4),))
    cross_input_projection = scatter_about(splits[9], (3, D, HD), D ** -0.5, 0.25, ((2, 4),))
    cross_in_bias = scatter_about(splits[10], (2, HD), 0.5, 3.0, ((1, 4),), jnp.float32)
    cross_out_proj = scatter_about(splits[11], (HD, D), (HD // 32) ** -0.5, 1.5, ((0, 4),))
    feed_in_proj = scatter_about(splits[12], (D, FF), D ** -0.5, 0.25, ((1, 4),))
    feed_in_bias = scatter_about(splits[13], (FF,), 0.5, 3.0, ((0, 4),), jnp.float32)
    feed_out_proj = scatter_about(splits[14], (FF, D), (FF // 2) ** -0.5, 0.1875, ((0, 4),))
    out_bias = scatter_about(splits[15], (3, D), 0.3, 2.0, (), jnp.float32)
    norm_gain = jnp.clip(1.0 + 0.18 * jax.random.normal(splits[16], (3, D), jnp.float32), 0.1, 1.9)
    norm_bias = scatter_about(splits[17], (3, D), 0.3, 2.0, (), jnp.float32)
    return dict(decoder_layer_input=decoder_layer_input, encoder_state_rows=encoder_state_rows, target_segments=target_segments, source_segments=source_segments, valid_mask=valid_mask, cotangent=cotangent, self_input_projection=self_input_projection, self_in_bias=self_in_bias, self_out_proj=self_out_proj, cross_input_projection=cross_input_projection, cross_in_bias=cross_in_bias, cross_out_proj=cross_out_proj, feed_in_proj=feed_in_proj, feed_in_bias=feed_in_bias, feed_out_proj=feed_out_proj, out_bias=out_bias, norm_gain=norm_gain, norm_bias=norm_bias)


@jax.custom_vjp
def low(v):
    return lax.optimization_barrier(v.astype(jnp.bfloat16)).astype(jnp.float32)

@jax.custom_vjp
def low_back(v):
    return v

def low_keep(v):
    return (low(v), None)

def low_pass(kept, grad):
    return (grad,)

def back_keep(v):
    return (v, None)

def back_low(kept, grad):
    return (low(grad),)
low.defvjp(low_keep, low_pass)
low_back.defvjp(back_keep, back_low)
EPSILON = 1e-05
HIGHEST = lax.Precision.HIGHEST

def layer_norm(summed_in, gain_vec, shift_vec):
    row_mean = lax.optimization_barrier(jnp.mean(summed_in, axis=-1, keepdims=True))
    centred = summed_in - row_mean
    variance = lax.optimization_barrier(jnp.mean(centred * centred, axis=-1, keepdims=True))
    return centred * lax.rsqrt(variance + EPSILON) * gain_vec + shift_vec

def matmul(inputs, matrix):
    return jnp.dot(inputs, matrix, precision=HIGHEST)

def attend(queries, key_rows, value_rows, query_ids, key_ids):
    row_count, row_width = queries.shape
    block_rows = min(512, row_count)
    query_blocks = queries.reshape(row_count // block_rows, block_rows, HEADS, HEAD)
    id_blocks = query_ids.reshape(row_count // block_rows, block_rows)
    key_heads = key_rows.reshape(key_rows.shape[0], HEADS, HEAD)
    value_heads = value_rows.reshape(value_rows.shape[0], HEADS, HEAD)

    def one_block(block_args):
        query_block, block_ids = block_args
        scores = jnp.einsum('qhe,khe->hqk', query_block, key_heads, precision=HIGHEST) * HEAD ** (-0.5)
        allowed = block_ids[:, None] == key_ids[None, :]
        scores = low_back(jnp.where(allowed[None], scores, -1e+30))
        probs = jax.nn.softmax(scores, axis=-1)
        return jnp.einsum('hqk,khe->qhe', low(probs), value_heads, precision=HIGHEST)
    output = lax.map(jax.checkpoint(one_block), (query_blocks, id_blocks))
    return output.reshape(row_count, row_width)

def block_layer(layer_in, enc_in, target_ids, source_ids, weights):
    self_input_projection, self_in_bias, self_out_proj, cross_input_projection, cross_in_bias, cross_out_proj, feed_in_proj, feed_in_bias, feed_out_proj, out_bias, norm_gain, norm_bias = weights
    self_q = low(low_back(matmul(layer_in, self_input_projection[0])) + self_in_bias[0])
    self_k = low(low_back(matmul(layer_in, self_input_projection[1])))
    self_v = low(low_back(matmul(layer_in, self_input_projection[2])) + self_in_bias[1])
    self_attn = low(low_back(attend(self_q, self_k, self_v, target_ids, target_ids)))
    branch_one = low_back(matmul(self_attn, self_out_proj)) + out_bias[0]
    stream_one = low(layer_norm(layer_in + branch_one, norm_gain[0], norm_bias[0]))
    cross_q = low(low_back(matmul(stream_one, cross_input_projection[0])) + cross_in_bias[0])
    cross_k = low(low_back(matmul(enc_in, cross_input_projection[1])))
    cross_v = low(low_back(matmul(enc_in, cross_input_projection[2])) + cross_in_bias[1])
    cross_attn = low(low_back(attend(cross_q, cross_k, cross_v, target_ids, source_ids)))
    branch_two = low_back(matmul(cross_attn, cross_out_proj)) + out_bias[1]
    stream_two = low(layer_norm(stream_one + branch_two, norm_gain[1], norm_bias[1]))
    pre_act = low_back(matmul(stream_two, feed_in_proj)) + feed_in_bias
    hidden = low(jax.nn.gelu(pre_act, approximate=True))
    branch_three = low_back(matmul(hidden, feed_out_proj)) + out_bias[2]
    final_norm = layer_norm(stream_two + branch_three, norm_gain[2], norm_bias[2])
    return (final_norm, branch_one, branch_two, branch_three)

def reference(decoder_layer_input, encoder_state_rows, target_segments, source_segments, valid_mask, cotangent, self_input_projection, self_in_bias, self_out_proj, cross_input_projection, cross_in_bias, cross_out_proj, feed_in_proj, feed_in_bias, feed_out_proj, out_bias, norm_gain, norm_bias):
    params = tuple((array_in.astype(jnp.float32) for array_in in (self_input_projection, self_in_bias, self_out_proj, cross_input_projection, cross_in_bias, cross_out_proj, feed_in_proj, feed_in_bias, feed_out_proj, out_bias, norm_gain, norm_bias)))
    zero_grads = tuple((jnp.zeros_like(array_in) for array_in in params))

    def one_sequence(carry, seq_item):
        grad_sums, stat_sums = carry
        seq_input, seq_enc, seq_target, seq_source, seq_valid, seq_cot = seq_item

        def forward(input_rows, enc_rows, weights):
            return block_layer(input_rows, enc_rows, seq_target, seq_source, weights)
        results, pullback = jax.vjp(forward, seq_input.astype(jnp.float32), seq_enc.astype(jnp.float32), params)
        final_norm, branch_one, branch_two, branch_three = results
        mask_col = seq_valid.astype(jnp.float32)[:, None]
        nothing = jnp.zeros_like(final_norm)
        input_grad, enc_grad, weight_grads = pullback((seq_cot * mask_col, nothing, nothing, nothing))
        grad_sums = jax.tree.map(jnp.add, grad_sums, weight_grads)
        new_stats = jnp.stack([jnp.sum(mask_col * branch_one * branch_one), jnp.sum(mask_col * branch_two * branch_two), jnp.sum(mask_col * branch_three * branch_three), jnp.sum(mask_col * final_norm * final_norm), jnp.sum(mask_col)])
        return ((grad_sums, stat_sums + new_stats), (final_norm.astype(jnp.bfloat16), input_grad, enc_grad))
    start_carry = (zero_grads, jnp.zeros((5,), jnp.float32))
    (grad_sums, stat_sums), (layer_output, input_grad, encoder_grad) = lax.scan(one_sequence, start_carry, (decoder_layer_input, encoder_state_rows, target_segments, source_segments, valid_mask, cotangent))
    rms_values = jnp.sqrt(stat_sums[:4] / (stat_sums[4] * D))
    return (layer_output, input_grad, encoder_grad, grad_sums[0], grad_sums[1], grad_sums[2], grad_sums[3], grad_sums[4], grad_sums[5], grad_sums[6], grad_sums[7], grad_sums[8], grad_sums[9], grad_sums[10], grad_sums[11], rms_values)
```

```python
import jax
import jax.numpy as jnp
from jax import lax
from jax.experimental import pallas as pl
from jax.experimental.pallas import tpu as pltpu
from jax.sharding import PartitionSpec as P

D = 512
HEAD = 64
EPSILON = 1e-05
PAIR = 2 * HEAD
FAR = 2.0**100
SCALE = HEAD ** (-0.5)
bf16, f32 = jnp.bfloat16, jnp.float32


def partner(array_in, bit):
    count = lax.axis_size("tensor")
    return lax.ppermute(array_in, "tensor", [(i, i ^ bit) for i in range(count)])


def partner_dp(array_in, bit):
    count = lax.axis_size("dp")
    return lax.ppermute(array_in, "dp", [(i, i ^ bit) for i in range(count)])


def gather_relative(shard):
    across = partner(shard, 2)
    return [shard, partner(shard, 1), across, partner(across, 1)]


def dp_bits():
    bits = []
    bit = 1
    while bit < lax.axis_size("dp"):
        bits.append(bit)
        bit *= 2
    return bits


def reduce_tensor(sent, kept):
    kept = kept + partner(sent, 1).astype(f32)
    return kept[0] + partner(kept[1].astype(bf16), 2).astype(f32)


def reduce_dp(total):
    rank = lax.axis_index("dp")
    for bit in dp_bits():
        upper = (rank & bit) != 0
        half = total.shape[0] // 2
        first, second = total[:half], total[half:]
        sent = jnp.where(upper, first, second).astype(bf16)
        kept = jnp.where(upper, second, first)
        total = kept + partner_dp(sent, bit).astype(f32)
    low = total.astype(bf16)
    for bit in reversed(dp_bits()):
        upper = (rank & bit) != 0
        other = partner_dp(low, bit)
        low = jnp.concatenate([jnp.where(upper, other, low), jnp.where(upper, low, other)], axis=0)
    return low


def reduce_small(common, sharded):
    many = common.shape[0]
    for bit in (1, 2):
        packed = jnp.concatenate([common, sharded.reshape(-1, D)], axis=0) if many else sharded.reshape(-1, D)
        other = partner(packed, bit)
        common = common + other[:many]
        other_chunks = other[many:].reshape(sharded.shape)
        sharded = sharded + jnp.stack([other_chunks[i ^ bit] for i in range(4)])
    packed = jnp.concatenate([common, sharded[0]], axis=0)
    for bit in dp_bits():
        packed = packed + partner_dp(packed, bit)
    return packed[:many], packed[many:]


def dot_nn(a, b):
    return lax.dot_general(a, b, (((1,), (0,)), ((), ())), preferred_element_type=f32)


def dot_nt(a, b):
    return lax.dot_general(a, b, (((1,), (1,)), ((), ())), preferred_element_type=f32)


def dot_tn(a, b):
    return lax.dot_general(a, b, (((0,), (0,)), ((), ())), preferred_element_type=f32)


def lane_in_head(count):
    return lax.broadcasted_iota(jnp.int32, (count, PAIR), 1) & (HEAD - 1)


def lane_low(count):
    return lax.broadcasted_iota(jnp.int32, (count, PAIR), 1) < HEAD


def as_columns(row):
    return jnp.broadcast_to(row.astype(f32), (PAIR, row.shape[1])).T


def minus_pieces(column, lane):
    high = column.astype(bf16).astype(f32)
    rest = column - high
    middle = rest.astype(bf16).astype(f32)
    low = rest - middle
    return jnp.where(lane == 4, -high, jnp.where(lane == 5, -middle, jnp.where(lane == 6, -low, 0.0)))


def query_extra(ids):
    lane = lane_in_head(ids.shape[0])
    return jnp.where((lane < 4) & (lane.astype(f32) != ids), -FAR, 0.0)


def key_extra(ids):
    lane = lane_in_head(ids.shape[0])
    ones = (lane >= 4) & (lane < 7)
    return jnp.where((lane.astype(f32) == ids) | ones, 1.0, 0.0).astype(bf16)


def attend(pairs, q_ref, k_ref, v_ref, q_extra, k_extra, o_ref, lse_ref):
    n_q, n_k = q_ref.shape[0], k_ref.shape[0]
    low_q, low_k = lane_low(n_q), lane_low(n_k)
    lane = lax.broadcasted_iota(jnp.int32, (n_q, PAIR), 1)
    extra = q_extra.astype(bf16)
    lse_all = jnp.zeros((n_q, PAIR), f32)
    for i in range(pairs):
        c = slice(i * PAIR, (i + 1) * PAIR)
        q2, k2, v2 = q_ref[:, c] * bf16(SCALE), k_ref[:, c], v_ref[:, c]
        scores = [
            dot_nt(jnp.where(low_q, q2, extra), jnp.where(low_k, k2, k_extra)),
            dot_nt(jnp.where(low_q, extra, q2), jnp.where(low_k, k_extra, k2)),
        ]
        outs = []
        for h in range(2):
            top = jnp.max(scores[h], axis=1, keepdims=True)
            terms = jnp.exp(scores[h] - top)
            total = jnp.sum(terms, axis=1, keepdims=True)
            outs.append(dot_nn(terms.astype(bf16), v2) * (1.0 / total))
            lse_all = jnp.where(lane == 2 * i + h, top + jnp.log(total), lse_all)
        o_ref[:, c] = jnp.where(low_q, outs[0], outs[1]).astype(bf16)
    lse_ref[...] = lse_all


def attend_back(pairs, base, q_ref, k_ref, v_ref, o_ref, g_ref, lse_ref, q_extra, k_extra, gq_ref, store):
    n_q, n_k = q_ref.shape[0], k_ref.shape[0]
    low_q, low_k = lane_low(n_q), lane_low(n_k)
    lane = lax.broadcasted_iota(jnp.int32, (n_q, PAIR), 1)
    head_lane = lane_in_head(n_q)
    key_lane = lane_in_head(n_k)
    v_extra = jnp.where((key_lane >= 4) & (key_lane < 7), 1.0, 0.0).astype(bf16)
    nothing = jnp.zeros((n_q, PAIR), bf16)
    lse_all = lse_ref[...]
    for i in range(pairs):
        c = slice(i * PAIR, (i + 1) * PAIR)
        q2, k2, v2, g2 = q_ref[:, c] * bf16(SCALE), k_ref[:, c], v_ref[:, c], g_ref[:, c]
        product = g2.astype(f32) * o_ref[:, c].astype(f32)
        gk, gv, gq = [], [], []
        for h in range(2):
            own_q = low_q if h == 0 else ~low_q
            own_k = low_k if h == 0 else ~low_k
            dots = jnp.sum(jnp.where(own_q, product, 0.0), axis=1, keepdims=True)
            lse = jnp.sum(jnp.where(lane == base + 2 * i + h, lse_all, 0.0), axis=1, keepdims=True)
            q_more = jnp.where(own_q, q2, (q_extra + minus_pieces(lse, head_lane)).astype(bf16))
            g_more = jnp.where(own_q, g2, minus_pieces(dots, head_lane).astype(bf16))
            probs = jnp.exp(dot_nt(jnp.where(own_k, k2, k_extra), q_more))
            g_scores = (probs * dot_nt(jnp.where(own_k, v2, v_extra), g_more)).astype(bf16)
            gv.append(dot_nn(probs.astype(bf16), jnp.where(own_q, g2, nothing)))
            gk.append(dot_nn(g_scores, jnp.where(own_q, q2, nothing)))
            gq.append(dot_tn(g_scores, k2))
        store(i, gk[0] + gk[1], gv[0] + gv[1])
        gq_ref[:, c] = jnp.where(low_q, gq[0], gq[1]) * SCALE


def normed(z):
    centred = z - jnp.mean(z, axis=-1, keepdims=True)
    r = lax.rsqrt(jnp.mean(centred * centred, axis=-1, keepdims=True) + EPSILON)
    return centred * r, r


def norm_back(z, gain, upstream):
    xhat, r = normed(z)
    inner = gain * upstream
    grad = r * (
        inner
        - jnp.mean(inner, axis=-1, keepdims=True)
        - xhat * jnp.mean(inner * xhat, axis=-1, keepdims=True)
    )
    return grad, column_sum(upstream * xhat), column_sum(upstream)


def column_sum(array_in):
    return jnp.sum(array_in, axis=0, keepdims=True)


def lanes(refs, index=None):
    return jnp.concatenate([r[...] if index is None else r[index] for r in refs], axis=1)


def stacked(refs):
    return jnp.concatenate([r[...] for r in refs], axis=0)


def sequence_rows(spots, ref, blocks):
    size = ref.shape[1] // 4
    return jnp.concatenate(
        [
            ref[spots[0], pl.ds(pl.multiple_of(spots[1 + j] * size, size), size), :]
            for j in range(blocks)
        ],
        axis=0,
    )


def kernel_call(body, name, out_shape, operands, smem=1, scratch=(), flops=0, limit=48):
    vmem = pl.BlockSpec(memory_space=pltpu.VMEM)
    scalar = pl.BlockSpec(memory_space=pltpu.SMEM)
    moved = sum(a.size * a.dtype.itemsize for a in list(operands) + list(out_shape))
    return pl.pallas_call(
        body,
        name=name,
        out_shape=out_shape,
        in_specs=[scalar] * smem + [vmem] * (len(operands) - smem),
        out_specs=[vmem] * len(out_shape),
        scratch_shapes=scratch,
        compiler_params=pltpu.CompilerParams(vmem_limit_bytes=limit * 2**20),
        cost_estimate=pl.CostEstimate(flops=flops, bytes_accessed=moved, transcendentals=0),
    )(*operands)


def shape(dims, dtype):
    return jax.ShapeDtypeStruct(dims, dtype)


def self_forward(spots, x, w_a, w_b, b_a, b_b, ids, q_ref, k_ref, v_ref, o_ref, lse_ref):
    rows = sequence_rows(spots, x, 4)
    own = q_ref.shape[0]
    bias = jnp.concatenate([b_a[:, 0:PAIR], b_b[:, 0:PAIR]], axis=1)
    q_ref[...] = (dot_nn(rows[:own], lanes([w_a, w_b], 0)) + bias).astype(bf16)
    k_ref[...] = dot_nn(rows, lanes([w_a, w_b], 1)).astype(bf16)
    bias = jnp.concatenate([b_a[:, PAIR : 2 * PAIR], b_b[:, PAIR : 2 * PAIR]], axis=1)
    v_ref[...] = (dot_nn(rows, lanes([w_a, w_b], 2)) + bias).astype(bf16)
    columns = as_columns(ids[0:1, :])
    attend(2, q_ref, k_ref, v_ref, query_extra(columns[:own]), key_extra(columns), o_ref, lse_ref)


def cross_forward(
    spots, o_a, o_b, so0, so1, so2, so3, x, e, ci0, ci1, ci2, ci3, co0, co1, co2, co3, b0, b1, b2, b3,
    ids, mask, out_bias, gain, shift,
    s1_ref, z1_ref, q_ref, k_ref, v_ref, o_ref, lse_ref, s2_ref, z2_ref, sums_ref,
):
    own = q_ref.shape[0]
    valid = as_columns(mask[...])[:, 0:1]
    branch = dot_nn(lanes([o_a, o_b]), stacked([so0, so1, so2, so3])) + out_bias[0:1, :]
    sums_ref[...] = jnp.zeros_like(sums_ref)
    sums_ref[0:1, :] = column_sum(valid * branch * branch)
    z = sequence_rows(spots, x, 2).astype(f32) + branch
    z1_ref[...] = z
    stream = (normed(z)[0] * gain[0:1, :] + shift[0:1, :]).astype(bf16)
    s1_ref[...] = stream
    rows = sequence_rows(spots, e, 4)
    shards = [ci0, ci1, ci2, ci3]
    bias = jnp.concatenate([b[:, 2 * PAIR : 3 * PAIR] for b in (b0, b1, b2, b3)], axis=1)
    q_ref[...] = (dot_nn(stream, lanes(shards, 0)) + bias).astype(bf16)
    k_ref[...] = dot_nn(rows, lanes(shards, 1)).astype(bf16)
    bias = jnp.concatenate([b[:, 3 * PAIR : 4 * PAIR] for b in (b0, b1, b2, b3)], axis=1)
    v_ref[...] = (dot_nn(rows, lanes(shards, 2)) + bias).astype(bf16)
    queries = query_extra(as_columns(ids[0:1, :own]))
    attend(4, q_ref, k_ref, v_ref, queries, key_extra(as_columns(ids[1:2, :])), o_ref, lse_ref)
    branch = dot_nn(o_ref[...], stacked([co0, co1, co2, co3])) + out_bias[1:2, :]
    sums_ref[1:2, :] = column_sum(valid * branch * branch)
    z = stream.astype(f32) + branch
    z2_ref[...] = z
    s2_ref[...] = (normed(z)[0] * gain[1:2, :] + shift[1:2, :]).astype(bf16)


def feed(
    spots, s2, z2, fi0, fi1, fi2, fi3, fo0, fo1, fo2, fo3, b0, b1, b2, b3, out_bias, gain, shift, cot, cot_other,
    mask, co0, co1, co2, co3, o2,
    kept_out, sent_out, sent_parts, kept_parts, g2_ref, gc_ref, out_t, sums_ref, bias_ref,
    slope, hidden,
):
    curve = (2.0 / 3.141592653589793) ** 0.5
    stream = s2[...]
    rows, width = stream.shape[0], fi0.shape[1]
    valid = as_columns(mask[...])[:, 0:1]
    branch = jnp.zeros((rows, D), f32) + out_bias[2:3, :]
    ins, outs, offsets = [fi0, fi1, fi2, fi3], [fo0, fo1, fo2, fo3], [b0, b1, b2, b3]
    for j in range(4):
        pre = dot_nn(stream, ins[j][...]) + offsets[j][:, 4 * PAIR :]
        square = pre * pre
        bend = jnp.tanh(curve * pre * (1.0 + 0.044715 * square))
        half = 0.5 * (1.0 + bend)
        slope[j] = half + 0.5 * pre * (1.0 - bend * bend) * (curve * (1.0 + 3.0 * 0.044715 * square))
        units = (pre * half).astype(bf16)
        hidden[j] = units
        branch = branch + dot_nn(units, outs[j][...])
    z = stream.astype(f32) + branch
    final = normed(z)[0] * gain[2:3, :] + shift[2:3, :]
    low = final.astype(bf16)
    kept_out[...] = low[: rows // 2]
    sent_out[...] = low[rows // 2 :]
    sums_ref[0:1, :] = column_sum(valid * branch * branch)
    sums_ref[1:2, :] = column_sum(valid * final * final)
    upstream = jnp.concatenate([cot[spots[0]], cot_other[...].astype(f32)], axis=0) * valid
    g3, row_gain, row_shift = norm_back(z, gain[2:3, :], upstream)
    sums_ref[2:3, :] = row_gain
    sums_ref[3:4, :] = row_shift
    sums_ref[4:5, :] = column_sum(g3)
    g_low = g3.astype(bf16)
    up = g3
    for j in range(4):
        g_pre = dot_nt(g_low, outs[j][...]) * slope[j]
        bias_ref[j : j + 1, :] = column_sum(g_pre)
        pre_low = g_pre.astype(bf16)
        up = up + dot_nt(pre_low, ins[j][...])
        part_in, part_out = dot_tn(stream, pre_low), dot_tn(hidden[j], g_low)
        if j % 2:
            sent_parts[j // 2, 0:D, :] = part_in.astype(bf16)
            sent_parts[j // 2, D : D + width, :] = part_out.astype(bf16)
        else:
            kept_parts[j // 2, 0:D, :] = part_in
            kept_parts[j // 2, D : D + width, :] = part_out
    g2, row_gain, row_shift = norm_back(z2[...], gain[1:2, :], up)
    sums_ref[5:6, :] = row_gain
    sums_ref[6:7, :] = row_shift
    sums_ref[7:8, :] = column_sum(g2)
    g2_ref[...] = g2
    g_low = g2.astype(bf16)
    gc_ref[...] = dot_nt(g_low, stacked([co0, co1, co2, co3])).astype(bf16)
    out_t[...] = dot_tn(g_low, o2[...])


def kv_store(sent_ref, kept_ref, first, sums_ref):
    own, width = kept_ref.shape[0], kept_ref.shape[1] // 2

    def store(i, gk, gv):
        here = (first + i) * PAIR
        there = ((first + i) ^ 1) * PAIR
        kept_ref[:, here : here + PAIR] = gk[:own]
        kept_ref[:, width + here : width + here + PAIR] = gv[:own]
        sent_ref[:, there : there + PAIR] = gk[own:].astype(bf16)
        sent_ref[:, width + there : width + there + PAIR] = gv[own:].astype(bf16)
        sums_ref[1:2, here : here + PAIR] = column_sum(gv)

    return store


def cross_backward(
    q, k, v, o, lse, g, ids, s1, g2, ci0, ci1, ci2, ci3, z1, gain, o_a, o_b, so0, so1, so2, so3,
    sent_ref, kept_ref, part_q, g1_ref, gs_ref, out_t, sums_ref, gq_ref,
):
    own = q.shape[0]
    sums_ref[...] = jnp.zeros_like(sums_ref)
    queries = query_extra(as_columns(ids[0:1, :own]))
    keys = key_extra(as_columns(ids[1:2, :]))
    store = kv_store(sent_ref, kept_ref, 0, sums_ref)
    attend_back(4, 0, q, k, v, o, g, lse, queries, keys, gq_ref, store)
    gq = gq_ref[...]
    sums_ref[0:1, :] = column_sum(gq)
    low = gq.astype(bf16)
    part_q[...] = dot_tn(s1[...], low)
    up = g2[...] + dot_nt(low, lanes([ci0, ci1, ci2, ci3], 0))
    g1, row_gain, row_shift = norm_back(z1[...], gain[0:1, :], up)
    sums_ref[2:3, :] = row_gain
    sums_ref[3:4, :] = row_shift
    sums_ref[4:5, :] = column_sum(g1)
    g1_ref[...] = g1
    g_low = g1.astype(bf16)
    gs_ref[...] = dot_nt(g_low, stacked([so0, so1, so2, so3])).astype(bf16)
    out_t[...] = dot_tn(g_low, lanes([o_a, o_b]))


def self_backward(
    spots, q_a, k_a, v_a, o_a, lse_a, q_b, k_b, v_b, o_b, lse_b, g, ids, x, g1, w0, w1, w2, w3,
    sent_ref, kept_ref, part_q, base_ref, sums_ref, gq_ref,
):
    own = q_a.shape[0]
    sums_ref[...] = jnp.zeros_like(sums_ref)
    columns = as_columns(ids[0:1, :])
    queries, keys = query_extra(columns[:own]), key_extra(columns)
    for part, (q, k, v, o, lse) in enumerate([(q_a, k_a, v_a, o_a, lse_a), (q_b, k_b, v_b, o_b, lse_b)]):
        c = slice(part * 2 * PAIR, (part + 1) * 2 * PAIR)
        store = kv_store(sent_ref, kept_ref, 2 * part, sums_ref)
        attend_back(2, 0, q, k, v, o, g.at[:, c], lse, queries, keys, gq_ref.at[:, c], store)
    gq = gq_ref[...]
    sums_ref[0:1, :] = column_sum(gq)
    low = gq.astype(bf16)
    part_q[...] = dot_tn(sequence_rows(spots, x, 2), low)
    base_ref[...] = g1[...] + dot_nt(low, lanes([w0, w1, w2, w3], 0))


def finish(has_base, *refs):
    if has_base:
        spots, kept, other, rows_ref, w0, w1, w2, w3, part_q, out_t, base, *outs = refs
    else:
        spots, kept, other, rows_ref, w0, w1, w2, w3, part_q, out_t, *outs = refs
    sent_parts, kept_parts, res_kept, res_sent = outs
    both = (kept[...] + other[...].astype(f32)).astype(bf16)
    gk, gv = both[:, :D], both[:, D:]
    rows = sequence_rows(spots, rows_ref, 2)
    shards = [w0, w1, w2, w3]
    res = dot_nt(gk, lanes(shards, 1)) + dot_nt(gv, lanes(shards, 2))
    if has_base:
        res = res + base[...]
    half = res.shape[0] // 2
    res_kept[...] = res[:half]
    res_sent[...] = res[half:].astype(bf16)
    part_kv = dot_tn(rows, both)
    parts = [part_q[...], part_kv[:, :D], part_kv[:, D:], out_t[...]]
    for n, part in enumerate(parts):
        for j in range(4):
            chunk = part[:, j * PAIR : (j + 1) * PAIR]
            if j % 2:
                sent_parts[j // 2, n * D : (n + 1) * D, :] = chunk.astype(bf16)
            else:
                kept_parts[j // 2, n * D : (n + 1) * D, :] = chunk


def own_first(ids, mine, rank):
    row = lax.dynamic_index_in_dim(ids, mine, 0, True)
    size = ids.shape[1] // 4
    parts = [
        lax.dynamic_slice_in_dim(row, (rank ^ step) * size, size, 1) for step in (0, 2, 1, 3)
    ]
    return jnp.concatenate(parts, axis=1)


def per_device(
    decoder_layer_input,
    encoder_state_rows,
    target_segments,
    source_segments,
    valid_mask,
    cotangent,
    self_input_projection,
    self_in_bias,
    self_out_proj,
    cross_input_projection,
    cross_in_bias,
    cross_out_proj,
    feed_in_proj,
    feed_in_bias,
    feed_out_proj,
    out_bias,
    norm_gain,
    norm_bias,
):
    rank = lax.axis_index("tensor")
    mine = rank // 2
    length = decoder_layer_input.shape[1]
    own = length // 2
    width = self_out_proj.shape[0]
    units = feed_in_proj.shape[1]
    spots = jnp.stack([mine, rank, rank ^ 2, rank ^ 1, rank ^ 3]).astype(jnp.int32)

    biases = jnp.concatenate(
        [self_in_bias.reshape(-1), cross_in_bias.reshape(-1), feed_in_bias]
    ).reshape(1, -1)
    bias = gather_relative(biases)
    self_in = gather_relative(self_input_projection)
    self_out = gather_relative(self_out_proj)
    cross_in = gather_relative(cross_input_projection)
    cross_out = gather_relative(cross_out_proj)
    feed_in = gather_relative(feed_in_proj)
    feed_out = gather_relative(feed_out_proj)

    ids = jnp.concatenate(
        [own_first(target_segments, mine, rank), own_first(source_segments, mine, rank)], axis=0
    )
    mask_kept = lax.dynamic_index_in_dim(valid_mask, mine, 0, True)
    mask_sent = lax.dynamic_index_in_dim(valid_mask, 1 - mine, 0, True)
    mask = jnp.concatenate([mask_kept, partner(mask_sent, 2)], axis=1).astype(f32)
    cot_other = partner(lax.dynamic_index_in_dim(cotangent, 1 - mine, 0, False).astype(bf16), 2)

    def self_half(first):
        return kernel_call(
            self_forward,
            "self_forward",
            [
                shape((own, 2 * PAIR), bf16),
                shape((length, 2 * PAIR), bf16),
                shape((length, 2 * PAIR), bf16),
                shape((own, 2 * PAIR), bf16),
                shape((own, PAIR), f32),
            ],
            [spots, decoder_layer_input, self_in[first], self_in[first + 1], bias[first], bias[first + 1], ids],
            flops=4_000_000_000,
        )

    q_a, k_a, v_a, o_a, lse_a = self_half(0)
    q_b, k_b, v_b, o_b, lse_b = self_half(2)

    full, wide = (own, D), (length, D)
    s1, z1, q2, k2, v2, o2, lse2, s2, z2, sums_two = kernel_call(
        cross_forward,
        "cross_forward",
        [
            shape(full, bf16), shape(full, f32), shape(full, bf16), shape(wide, bf16), shape(wide, bf16),
            shape(full, bf16), shape((own, PAIR), f32), shape(full, bf16), shape(full, f32), shape((8, D), f32),
        ],
        [spots, o_a, o_b, *self_out, decoder_layer_input, encoder_state_rows, *cross_in, *cross_out, *bias,
         ids, mask, out_bias, norm_gain, norm_bias],
        flops=10_000_000_000,
    )

    out_kept, out_sent, feed_sent, feed_kept, g2, g_cross, cross_out_t, sums_three, bias_rows = kernel_call(
        feed,
        "feed",
        [
            shape((own // 2, D), bf16), shape((own // 2, D), bf16),
            shape((2, D + units, D), bf16), shape((2, D + units, D), f32),
            shape(full, f32), shape(full, bf16), shape((D, D), f32), shape((8, D), f32), shape((4, units), f32),
        ],
        [spots, s2, z2, *feed_in, *feed_out, *bias, out_bias, norm_gain, norm_bias, cotangent, cot_other, mask,
         *cross_out, o2],
        scratch=[pltpu.VMEM((4, own, units), f32), pltpu.VMEM((4, own, units), bf16)],
        flops=15_000_000_000,
    )
    feed_total = reduce_dp(reduce_tensor(feed_sent, feed_kept))

    kv_shapes = [shape((own, 2 * D), bf16), shape((own, 2 * D), f32), shape((D, D), f32)]
    gkv_sent, gkv_kept, part_q, g1, g_self, self_out_t, sums_four = kernel_call(
        cross_backward,
        "cross_backward",
        kv_shapes + [shape(full, f32), shape(full, bf16), shape((D, D), f32), shape((8, D), f32)],
        [q2, k2, v2, o2, lse2, g_cross, ids, s1, g2, *cross_in, z1, norm_gain, o_a, o_b, *self_out],
        smem=0,
        scratch=[pltpu.VMEM(full, f32)],
        flops=18_000_000_000,
    )

    def finished(sent, kept, rows_in, shards, part, out_t, base):
        return kernel_call(
            lambda *refs: finish(base is not None, *refs),
            "finish",
            [
                shape((2, 4 * D, width), bf16), shape((2, 4 * D, width), f32),
                shape((own // 2, D), f32), shape((own // 2, D), bf16),
            ],
            [spots, kept, partner(sent, 1), rows_in, *shards, part, out_t] + ([] if base is None else [base]),
            flops=3_000_000_000,
        )

    cross_sent, cross_kept, enc_kept, enc_sent = finished(
        gkv_sent, gkv_kept, encoder_state_rows, cross_in, part_q, cross_out_t, None
    )
    cross_total = reduce_dp(reduce_tensor(cross_sent, cross_kept))

    gkv_sent, gkv_kept, part_q, base, sums_five = kernel_call(
        self_backward,
        "self_backward",
        kv_shapes + [shape(full, f32), shape((8, D), f32)],
        [spots, q_a, k_a, v_a, o_a, lse_a, q_b, k_b, v_b, o_b, lse_b, g_self, ids, decoder_layer_input, g1, *self_in],
        scratch=[pltpu.VMEM(full, f32)],
        flops=18_000_000_000,
    )
    self_sent, self_kept, in_kept, in_sent = finished(
        gkv_sent, gkv_kept, decoder_layer_input, self_in, part_q, self_out_t, base
    )
    self_total = reduce_dp(reduce_tensor(self_sent, self_kept))

    def to_owner(kept, sent):
        other = partner(sent, 2).astype(kept.dtype)
        first = mine == 0
        return jnp.stack([jnp.where(first, kept, other), jnp.where(first, other, kept)])

    def by_chunk(row):
        return row.reshape(4, width)

    mask_row = jnp.concatenate([mask[:, :D], jnp.zeros((1, D - mask.shape[1]), f32)], axis=1) if mask.shape[1] < D else mask
    common = jnp.concatenate([sums_two[0:2], sums_three, sums_four[2:5], mask_row], axis=0)
    sharded = jnp.concatenate(
        [
            by_chunk(sums_five[0]), by_chunk(sums_five[1]), by_chunk(sums_four[0]), by_chunk(sums_four[1]),
            bias_rows,
        ],
        axis=1,
    ).reshape(4, -1, D)
    common, own_sums = reduce_small(common, sharded)
    totals = jnp.sum(common, axis=1)
    rms_values = jnp.sqrt(totals[0:4] / (totals[13] * D))
    pair_sums = own_sums[0].reshape(2, 2, width)

    def in_grad(total):
        return total[: 3 * D].reshape(3, D, width).astype(f32)

    def out_grad(total):
        return total[3 * D :].T.astype(f32)

    return (
        to_owner(out_kept, out_sent),
        to_owner(in_kept, in_sent),
        to_owner(enc_kept, enc_sent),
        in_grad(self_total),
        pair_sums[0],
        out_grad(self_total),
        in_grad(cross_total),
        pair_sums[1],
        out_grad(cross_total),
        feed_total[:D].astype(f32),
        own_sums[1],
        feed_total[D:].astype(f32),
        jnp.stack([common[12], common[9], common[6]]),
        jnp.stack([common[10], common[7], common[4]]),
        jnp.stack([common[11], common[8], common[5]]),
        rms_values,
    )


def solution(mesh):
    return jax.shard_map(
        per_device,
        mesh=mesh,
        in_specs=(
            P("dp", None, None),
            P("dp", None, None),
            P("dp", None),
            P("dp", None),
            P("dp", "tensor"),
            P("dp", "tensor", None),
            P(None, None, "tensor"),
            P(None, "tensor"),
            P("tensor", None),
            P(None, None, "tensor"),
            P(None, "tensor"),
            P("tensor", None),
            P(None, "tensor"),
            P("tensor"),
            P("tensor", None),
            P(),
            P(),
            P(),
        ),
        out_specs=(
            P("dp", "tensor", None),
            P("dp", "tensor", None),
            P("dp", "tensor", None),
            P(None, None, "tensor"),
            P(None, "tensor"),
            P("tensor", None),
            P(None, None, "tensor"),
            P(None, "tensor"),
            P("tensor", None),
            P(None, "tensor"),
            P("tensor"),
            P("tensor", None),
            P(),
            P(),
            P(),
            P(),
        ),
        check_vma=False,
    )
```

```python
import jax
import jax.numpy as jnp
from jax import lax
from jax.experimental import pallas as pl
from jax.experimental.pallas import tpu as pltpu
from jax.sharding import PartitionSpec as P

D = 512
HEAD = 64
EPSILON = 1e-05
PAIR = 2 * HEAD
FAR = 2.0**100
SCALE = HEAD ** (-0.5)
bf16, f32 = jnp.bfloat16, jnp.float32


def partner(array_in, bit):
    count = lax.axis_size("tensor")
    return lax.ppermute(array_in, "tensor", [(i, i ^ bit) for i in range(count)])


def partner_dp(array_in, bit):
    count = lax.axis_size("dp")
    return lax.ppermute(array_in, "dp", [(i, i ^ bit) for i in range(count)])


def tie(value, *others):
    return lax.optimization_barrier((value, others))[0]


def dp_bits():
    bits = []
    bit = 1
    while bit < lax.axis_size("dp"):
        bits.append(bit)
        bit *= 2
    return bits


def halves(total, bit):
    upper = (lax.axis_index("dp") & bit) != 0
    half = total.shape[-2] // 2
    first, second = total[..., :half, :], total[..., half:, :]
    return jnp.where(upper, second, first), jnp.where(upper, first, second).astype(bf16)


def in_order(mine, other, bit):
    upper = (lax.axis_index("dp") & bit) != 0
    return jnp.concatenate([jnp.where(upper, other, mine), jnp.where(upper, mine, other)], axis=-2)


def half_here(rows, bit):
    half = rows.shape[0] // 2
    upper = (lax.axis_index("dp") & bit) != 0
    return jnp.where(upper, rows[half:], rows[:half])


class DpSum:
    def __init__(self, total, bits):
        self.todo = [("half", bit) for bit in bits[:-1]] + [("swap", bits[-1])]
        self.todo += [("double", bit) for bit in reversed(dp_bits()[:-1])]
        self.value = total
        self.start()

    def start(self):
        kind, bit = self.todo[0]
        if kind == "half":
            self.kept, self.value = halves(self.value, bit)
        else:
            self.kept = self.value = self.value.astype(bf16)
        self.got = partner_dp(self.value, bit)

    def step(self, *after):
        if self.todo:
            if after:
                self.kept, self.got = tie((self.kept, self.got), *after)
            kind, bit = self.todo.pop(0)
            if kind == "double":
                self.value = in_order(self.kept, self.got, bit)
            else:
                self.value = self.kept.astype(f32) + self.got.astype(f32)
            if self.todo:
                self.start()
        return self.value

    def finish(self, *after):
        while self.todo:
            self.step(*after)
        return self.value


def dot_nn(a, b):
    return lax.dot_general(a, b, (((1,), (0,)), ((), ())), preferred_element_type=f32)


def dot_nt(a, b):
    return lax.dot_general(a, b, (((1,), (1,)), ((), ())), preferred_element_type=f32)


def dot_tn(a, b):
    return lax.dot_general(a, b, (((0,), (0,)), ((), ())), preferred_element_type=f32)


def lane_in_head(count):
    return lax.broadcasted_iota(jnp.int32, (count, PAIR), 1) & (HEAD - 1)


def lane_low(count):
    return lax.broadcasted_iota(jnp.int32, (count, PAIR), 1) < HEAD


def as_columns(row):
    return jnp.broadcast_to(row.astype(f32), (PAIR, row.shape[1])).T


def minus_pieces(column, lane):
    high = column.astype(bf16).astype(f32)
    rest = column - high
    middle = rest.astype(bf16).astype(f32)
    low = rest - middle
    return jnp.where(lane == 4, -high, jnp.where(lane == 5, -middle, jnp.where(lane == 6, -low, 0.0)))


def query_extra(ids):
    lane = lane_in_head(ids.shape[0])
    return jnp.where((lane < 4) & (lane.astype(f32) != ids), -FAR, 0.0)


def key_extra(ids):
    lane = lane_in_head(ids.shape[0])
    ones = (lane >= 4) & (lane < 7)
    return jnp.where((lane.astype(f32) == ids) | ones, 1.0, 0.0).astype(bf16)


def attend(pairs, q_ref, k_ref, v_ref, q_extra, k_extra, o_ref, lse_ref):
    n_q, n_k = q_ref.shape[0], k_ref.shape[0]
    low_q, low_k = lane_low(n_q), lane_low(n_k)
    lane = lax.broadcasted_iota(jnp.int32, (n_q, PAIR), 1)
    extra = q_extra.astype(bf16)
    lse_all = jnp.zeros((n_q, PAIR), f32)
    for i in range(pairs):
        c = slice(i * PAIR, (i + 1) * PAIR)
        q2, k2, v2 = q_ref[:, c] * bf16(SCALE), k_ref[:, c], v_ref[:, c]
        scores = [
            dot_nt(jnp.where(low_q, q2, extra), jnp.where(low_k, k2, k_extra)),
            dot_nt(jnp.where(low_q, extra, q2), jnp.where(low_k, k_extra, k2)),
        ]
        outs = []
        for h in range(2):
            top = jnp.max(scores[h], axis=1, keepdims=True)
            terms = jnp.exp(scores[h] - top)
            total = jnp.sum(terms, axis=1, keepdims=True)
            outs.append(dot_nn(terms.astype(bf16), v2) * (1.0 / total))
            lse_all = jnp.where(lane == 2 * i + h, top + jnp.log(total), lse_all)
        o_ref[:, c] = jnp.where(low_q, outs[0], outs[1]).astype(bf16)
    lse_ref[...] = lse_all


def attend_back(pairs, base, q_ref, k_ref, v_ref, o_ref, g_ref, lse_ref, q_extra, k_extra, gq_ref, store):
    n_q, n_k = q_ref.shape[0], k_ref.shape[0]
    low_q, low_k = lane_low(n_q), lane_low(n_k)
    lane = lax.broadcasted_iota(jnp.int32, (n_q, PAIR), 1)
    head_lane = lane_in_head(n_q)
    key_lane = lane_in_head(n_k)
    v_extra = jnp.where((key_lane >= 4) & (key_lane < 7), 1.0, 0.0).astype(bf16)
    nothing = jnp.zeros((n_q, PAIR), bf16)
    lse_all = lse_ref[...]
    for i in range(pairs):
        c = slice(i * PAIR, (i + 1) * PAIR)
        q2, k2, v2, g2 = q_ref[:, c] * bf16(SCALE), k_ref[:, c], v_ref[:, c], g_ref[:, c]
        product = g2.astype(f32) * o_ref[:, c].astype(f32)
        gk, gv, gq = [], [], []
        for h in range(2):
            own_q = low_q if h == 0 else ~low_q
            own_k = low_k if h == 0 else ~low_k
            dots = jnp.sum(jnp.where(own_q, product, 0.0), axis=1, keepdims=True)
            lse = jnp.sum(jnp.where(lane == base + 2 * i + h, lse_all, 0.0), axis=1, keepdims=True)
            q_more = jnp.where(own_q, q2, (q_extra + minus_pieces(lse, head_lane)).astype(bf16))
            g_more = jnp.where(own_q, g2, minus_pieces(dots, head_lane).astype(bf16))
            probs = jnp.exp(dot_nt(jnp.where(own_k, k2, k_extra), q_more))
            g_scores = (probs * dot_nt(jnp.where(own_k, v2, v_extra), g_more)).astype(bf16)
            gv.append(dot_nn(probs.astype(bf16), jnp.where(own_q, g2, nothing)))
            gk.append(dot_nn(g_scores, jnp.where(own_q, q2, nothing)))
            gq.append(dot_tn(g_scores, k2))
        store(i, gk[0] + gk[1], gv[0] + gv[1])
        gq_ref[:, c] = jnp.where(low_q, gq[0], gq[1]) * SCALE


def normed(z):
    centred = z - jnp.mean(z, axis=-1, keepdims=True)
    r = lax.rsqrt(jnp.mean(centred * centred, axis=-1, keepdims=True) + EPSILON)
    return centred * r, r


def norm_back(z, gain, upstream):
    xhat, r = normed(z)
    inner = gain * upstream
    grad = r * (
        inner
        - jnp.mean(inner, axis=-1, keepdims=True)
        - xhat * jnp.mean(inner * xhat, axis=-1, keepdims=True)
    )
    return grad, column_sum(upstream * xhat), column_sum(upstream)


def column_sum(array_in):
    return jnp.sum(array_in, axis=0, keepdims=True)


def lanes(refs):
    return jnp.concatenate([r[...] for r in refs], axis=1)


def bias_row(packs, index):
    rows = [
        sum(p[8 * n + index : 8 * n + index + 1, :].astype(f32) for n in (0, 1, 2)) for p in packs
    ]
    return jnp.concatenate(rows, axis=1)


def mask_column(own_pack, across_pack):
    first = 24
    row = jnp.concatenate([p[first + i : first + i + 1, :] for p, i in ((own_pack, 2), (own_pack, 3), (across_pack, 0), (across_pack, 1))], axis=1)
    return as_columns(row)[:, 0:1], row.astype(f32)


def stacked(refs):
    return jnp.concatenate([r[...] for r in refs], axis=0)


def sequence_rows(spots, ref, blocks):
    size = ref.shape[1] // 4
    return jnp.concatenate(
        [ref[0, pl.ds(pl.multiple_of(spots[1 + j] * size, size), size), :] for j in range(blocks)], axis=0
    )


def kernel_call(body, name, out_shape, operands, smem=1, scratch=(), blocks=(), us=5, limit=60):
    blocks = dict(blocks)

    def spec(dims, place):
        return pl.BlockSpec(dims, lambda step, *scalars: place(*scalars))

    def whole(dims):
        return spec(dims, lambda *scalars: (0,) * len(dims))

    return pl.pallas_call(
        lambda *refs: body(*refs),
        name=name,
        out_shape=out_shape,
        grid_spec=pltpu.PrefetchScalarGridSpec(
            num_scalar_prefetch=smem,
            grid=(1,),
            in_specs=[spec(*blocks[i]) if i in blocks else whole(operands[i].shape) for i in range(smem, len(operands))],
            out_specs=[whole(o.shape) for o in out_shape],
            scratch_shapes=scratch,
        ),
        compiler_params=pltpu.CompilerParams(vmem_limit_bytes=limit * 2**20),
        cost_estimate=pl.CostEstimate(flops=int(us * 1e9), bytes_accessed=1000, transcendentals=0),
    )(*operands)


def pack_part(index):
    return ((D, PAIR), lambda *scalars: (index, 0))


PACK_TAIL = ((32, PAIR), lambda *scalars: (4 * D // 32, 0))


def of_sequence(array):
    return ((1, *array.shape[1:]), lambda spots: (spots[0],) + (0,) * (array.ndim - 1))


def shape(dims, dtype):
    return jax.ShapeDtypeStruct(dims, dtype)


def self_forward(spots, x, q_w, q_x, k_w, k_x, v_w, v_x, t_w, t_x, ids, q_ref, k_ref, v_ref, o_ref, lse_ref):
    rows = sequence_rows(spots, x, 4)
    own = q_ref.shape[0]
    q_ref[...] = (dot_nn(rows[:own], lanes([q_w, q_x])) + bias_row([t_w, t_x], 0)).astype(bf16)
    k_ref[...] = dot_nn(rows, lanes([k_w, k_x])).astype(bf16)
    v_ref[...] = (dot_nn(rows, lanes([v_w, v_x])) + bias_row([t_w, t_x], 1)).astype(bf16)
    columns = as_columns(ids[0:1, :])
    attend(2, q_ref, k_ref, v_ref, query_extra(columns[:own]), key_extra(columns), o_ref, lse_ref)


def out_rows(shards):
    blocks = D // PAIR
    return jnp.concatenate(
        [
            jnp.concatenate([s[j * PAIR : (j + 1) * PAIR, :] for j in range(blocks)], axis=1)
            for s in shards
        ],
        axis=0,
    )


def cross_heads(stream, rows, weights, tails, ids, q_ref, k_ref, v_ref, o_ref, lse_ref):
    own = q_ref.shape[0]
    q_ref[...] = (dot_nn(stream, lanes(weights[0:2])) + bias_row(tails, 2)).astype(bf16)
    k_ref[...] = dot_nn(rows, lanes(weights[2:4])).astype(bf16)
    v_ref[...] = (dot_nn(rows, lanes(weights[4:6])) + bias_row(tails, 3)).astype(bf16)
    queries = query_extra(as_columns(ids[0:1, :own]))
    attend(2, q_ref, k_ref, v_ref, queries, key_extra(as_columns(ids[1:2, :])), o_ref, lse_ref)


def cross_first(
    spots, o_a, o_b, so0, so1, so2, so3, x, e, q_w, q_x, k_w, k_x, v_w, v_x, t0, t1, t2, ids, out_bias, gain, shift,
    s1_ref, z1_ref, q_ref, k_ref, v_ref, o_ref, lse_ref, sums_ref, xo_ref, eo_ref,
):
    own = q_ref.shape[0]
    valid, valid_row = mask_column(t0, t2)
    branch = dot_nn(lanes([o_a, o_b]), out_rows([so0, so1, so2, so3])) + out_bias[0:1, :]
    sums_ref[...] = jnp.zeros_like(sums_ref)
    sums_ref[0:1, :] = column_sum(valid * branch * branch)
    sums_ref[13:14, :] = valid_row
    x_own = sequence_rows(spots, x, 2)
    xo_ref[...] = x_own
    z = x_own.astype(f32) + branch
    z1_ref[...] = z
    stream = (normed(z)[0] * gain[0:1, :] + shift[0:1, :]).astype(bf16)
    s1_ref[...] = stream
    rows = sequence_rows(spots, e, 4)
    eo_ref[...] = rows[:own]
    cross_heads(stream, rows, [q_w, q_x, k_w, k_x, v_w, v_x], [t0, t1], ids, q_ref, k_ref, v_ref, o_ref, lse_ref)


def cross_second(
    spots, s1, o_a, e, q_w, q_x, k_w, k_x, v_w, v_x, co0, co1, co2, co3, t0, t2, t3, ids, out_bias, gain, shift, sums,
    q_ref, k_ref, v_ref, o_ref, lse_ref, s2_ref, z2_ref, sums_ref,
):
    stream = s1[...]
    valid = mask_column(t0, t2)[0]
    rows = sequence_rows(spots, e, 4)
    cross_heads(stream, rows, [q_w, q_x, k_w, k_x, v_w, v_x], [t2, t3], ids, q_ref, k_ref, v_ref, o_ref, lse_ref)
    branch = dot_nn(lanes([o_a, o_ref]), out_rows([co0, co1, co2, co3])) + out_bias[1:2, :]
    sums_ref[...] = sums[...]
    sums_ref[1:2, :] = column_sum(valid * branch * branch)
    z = stream.astype(f32) + branch
    z2_ref[...] = z
    s2_ref[...] = (normed(z)[0] * gain[1:2, :] + shift[1:2, :]).astype(bf16)


def feed(
    spots, s2, z2, fi0, fi1, fi2, fi3, fo0, fo1, fo2, fo3, b0, b1, b2, b3, out_bias, gain, shift, cot, cot_other,
    co0, co1, co2, co3, o_a, o_b, sums,
    kept_out, sent_out, sent_parts, kept_parts, g2_ref, gc_a, gc_b, out_t, sums_ref,
    slope, hidden,
):
    curve = (2.0 / 3.141592653589793) ** 0.5
    stream = s2[...]
    rows, width = stream.shape[0], fi0.shape[1]
    valid = mask_column(b0, b2)[0]
    sums_ref[...] = sums[...]
    branch = jnp.zeros((rows, D), f32) + out_bias[2:3, :]
    ins, outs, offsets = [fi0, fi1, fi2, fi3], [fo0, fo1, fo2, fo3], [b0, b1, b2, b3]
    for j in range(4):
        offset = jnp.concatenate([bias_row([offsets[j]], 4 + n) for n in range(width // PAIR)], axis=1)
        pre = dot_nn(stream, ins[j][...]) + offset
        square = pre * pre
        bend = jnp.tanh(curve * pre * (1.0 + 0.044715 * square))
        half = 0.5 * (1.0 + bend)
        slope[j] = half + 0.5 * pre * (1.0 - bend * bend) * (curve * (1.0 + 3.0 * 0.044715 * square))
        units = (pre * half).astype(bf16)
        hidden[j] = units
        branch = branch + dot_nn(units, outs[j][...])
    z = stream.astype(f32) + branch
    final = normed(z)[0] * gain[2:3, :] + shift[2:3, :]
    low = final.astype(bf16)
    kept_out[...] = low[: rows // 2]
    sent_out[...] = low[rows // 2 :]
    sums_ref[2:3, :] = column_sum(valid * branch * branch)
    sums_ref[3:4, :] = column_sum(valid * final * final)
    upstream = jnp.concatenate([cot[0], cot_other[...].astype(f32)], axis=0) * valid
    g3, row_gain, row_shift = norm_back(z, gain[2:3, :], upstream)
    sums_ref[4:5, :] = row_gain
    sums_ref[5:6, :] = row_shift
    sums_ref[6:7, :] = column_sum(g3)
    g_low = g3.astype(bf16)
    up = g3
    for j in range(4):
        g_pre = dot_nt(g_low, outs[j][...]) * slope[j]
        store_shard_row(sums_ref, j, 1, column_sum(g_pre))
        pre_low = g_pre.astype(bf16)
        up = up + dot_nt(pre_low, ins[j][...])
        to = sent_parts if j % 2 else kept_parts
        to[j // 2, 0:D, :] = dot_tn(stream, pre_low).astype(bf16)
        to[j // 2, D : D + width, :] = dot_tn(hidden[j], g_low).astype(bf16)
    g2, row_gain, row_shift = norm_back(z2[...], gain[1:2, :], up)
    sums_ref[7:8, :] = row_gain
    sums_ref[8:9, :] = row_shift
    sums_ref[9:10, :] = column_sum(g2)
    g2_ref[...] = g2
    g_low = g2.astype(bf16)
    g_cross = dot_nt(g_low, out_rows([co0, co1, co2, co3])).astype(bf16)
    gc_a[...] = g_cross[:, : 2 * PAIR]
    gc_b[...] = g_cross[:, 2 * PAIR :]
    store_blocks(out_t, dot_tn(lanes([o_a, o_b]), g_low))


def store_shard_row(sums_ref, j, row, value):
    sums_ref[16 + 2 * j + row : 17 + 2 * j + row, : value.shape[1]] = value


def store_chunks(to, part):
    for j in range(to.shape[0]):
        to[j] = part[:, j * PAIR : (j + 1) * PAIR].astype(bf16)


def store_blocks(to, part):
    for j in range(4):
        for c in range(D // PAIR):
            block = part[j * PAIR : (j + 1) * PAIR, c * PAIR : (c + 1) * PAIR]
            to[j, c * PAIR : (c + 1) * PAIR, :] = block.astype(bf16)


def kv_store(sent_ref, kept_ref, sums_ref):
    own, width = kept_ref.shape[0], kept_ref.shape[1] // 2

    def store(i, gk, gv):
        here = i * PAIR
        there = (i ^ 1) * PAIR
        kept_ref[:, here : here + PAIR] = gk[:own]
        kept_ref[:, width + here : width + here + PAIR] = gv[:own]
        sent_ref[:, there : there + PAIR] = gk[own:].astype(bf16)
        sent_ref[:, width + there : width + there + PAIR] = gv[own:].astype(bf16)
        sums_ref[1:2, here : here + PAIR] = column_sum(gv)

    return store


def half_back(source, q, k, v, o, lse, g, ids, rows, sent_ref, kept_ref, part_q, sums_ref, gq_ref):
    own = q.shape[0]
    sums_ref[...] = jnp.zeros_like(sums_ref)
    queries = query_extra(as_columns(ids[0:1, :own]))
    keys = key_extra(as_columns(ids[source : source + 1, :]))
    store = kv_store(sent_ref, kept_ref, sums_ref)
    attend_back(2, 0, q, k, v, o, g, lse, queries, keys, gq_ref, store)
    gq = gq_ref[...]
    sums_ref[0:1, : 2 * PAIR] = column_sum(gq)
    low = gq.astype(bf16)
    store_chunks(part_q, dot_tn(rows[...], low))
    return low


def far_back(source, q, k, v, o, lse, g, ids, rows, sent, kept, part_q, low_ref, sums, gq_ref):
    low_ref[...] = half_back(source, q, k, v, o, lse, g, ids, rows, sent, kept, part_q, sums, gq_ref)


def self_back(
    q, k, v, o, lse, g, ids, rows, low_b, acc, w0, w1, w2, w3, sent, kept, part_q, acc_ref, sums, gq_ref
):
    low = half_back(0, q, k, v, o, lse, g, ids, rows, sent, kept, part_q, sums, gq_ref)
    acc_ref[...] = acc[...] + dot_nt(low, lanes([w0, w1])) + dot_nt(low_b[...], lanes([w2, w3]))


def cross_back_norm(
    spots, q, k, v, o, lse, g, ids, rows, low_b, acc, w0, w1, w2, w3, z1, gain, o_a, o_b, so0, so1, so2, so3, sums_b,
    carried,
    sent, kept, part_q, g1_ref, gs_a, gs_b, out_t, sums, all_ref, gq_ref,
):
    low = half_back(1, q, k, v, o, lse, g, ids, rows, sent, kept, part_q, sums, gq_ref)
    up = acc[...] + dot_nt(low, lanes([w0, w1])) + dot_nt(low_b[...], lanes([w2, w3]))
    g1, row_gain, row_shift = norm_back(z1[...], gain[0:1, :], up)
    all_ref[...] = carried[...]
    all_ref[10:11, :] = row_gain
    all_ref[11:12, :] = row_shift
    all_ref[12:13, :] = column_sum(g1)
    for j in range(4):
        c = slice((j % 2) * PAIR, (j % 2 + 1) * PAIR)
        of = sums if j < 2 else sums_b
        store_shard_row(all_ref, j, 0, jnp.concatenate([of[0:1, c], of[1:2, c]], axis=1))
    g1_ref[...] = g1
    g_low = g1.astype(bf16)
    g_self = dot_nt(g_low, out_rows([so0, so1, so2, so3])).astype(bf16)
    gs_a[...] = g_self[:, : 2 * PAIR]
    gs_b[...] = g_self[:, 2 * PAIR :]
    store_blocks(out_t, dot_tn(lanes([o_a, o_b]), g_low))


def finish(first, mode, n_out, *refs):
    kept, other, rows, k_w, k_x, v_w, v_x, part_q, *refs = refs
    along, sums, refs = refs[:n_out], refs[n_out], refs[n_out + 1 :]
    outs = refs if mode == "start" else refs[1:]
    both = (kept[...] + other[...].astype(f32)).astype(bf16)
    gk, gv = both[:, : 2 * PAIR], both[:, 2 * PAIR :]
    res = dot_nt(gk, lanes([k_w, k_x])) + dot_nt(gv, lanes([v_w, v_x]))
    if mode != "start":
        res = res + refs[0][...]
    part = dot_tn(rows[...], both).astype(bf16)
    for j in range(2):
        to = outs[j]
        to[0:D, :] = part_q[j]
        to[D : 2 * D, :] = part[:, j * PAIR : (j + 1) * PAIR]
        to[2 * D : 3 * D, :] = part[:, (2 + j) * PAIR : (3 + j) * PAIR]
        for n in range(n_out):
            to[(3 + n) * D : (4 + n) * D, :] = along[n][j]
        last = (3 + n_out) * D
        to[last:, :] = jnp.zeros((to.shape[0] - last, PAIR), bf16)
        if n_out == 0:
            to[last : last + 2, :] = sums[0:2, j * PAIR : (j + 1) * PAIR].astype(bf16)
        else:
            for c in range(4):
                to[last + 16 * c : last + 16 * (c + 1), :] = sums[0:16, c * PAIR : (c + 1) * PAIR].astype(bf16)
            row = 16 + 2 * (first + j)
            blocks = [(row, 0), (row, 1), (row + 1, 0), (row + 1, 1), (row + 1, 2), (row + 1, 3)]
            shard_rows = jnp.concatenate(
                [sums[r : r + 1, c * PAIR : (c + 1) * PAIR] for r, c in blocks] + [jnp.zeros((2, PAIR), f32)], axis=0
            )
            to[last + 64 : last + 72, :] = shard_rows.astype(bf16)
    if mode == "last":
        half = res.shape[0] // 2
        outs[2][...] = res[:half]
        outs[3][...] = res[half:].astype(bf16)
    else:
        outs[2][...] = res


def own_first(ids, mine, rank):
    row = lax.dynamic_index_in_dim(ids, mine, 0, True)
    size = ids.shape[1] // 4
    parts = [
        lax.dynamic_slice_in_dim(row, (rank ^ step) * size, size, 1) for step in (0, 2, 1, 3)
    ]
    return jnp.concatenate(parts, axis=1)


def per_device(
    decoder_layer_input,
    encoder_state_rows,
    target_segments,
    source_segments,
    valid_mask,
    cotangent,
    self_input_projection,
    self_in_bias,
    self_out_proj,
    cross_input_projection,
    cross_in_bias,
    cross_out_proj,
    feed_in_proj,
    feed_in_bias,
    feed_out_proj,
    out_bias,
    norm_gain,
    norm_bias,
):
    rank = lax.axis_index("tensor")
    mine = rank // 2
    first = mine == 0
    length = decoder_layer_input.shape[1]
    own = length // 2
    width = self_out_proj.shape[0]
    units = feed_in_proj.shape[1]
    spots = jnp.stack([mine, rank, rank ^ 2, rank ^ 1, rank ^ 3]).astype(jnp.int32)

    def attention_weights(in_proj, out_proj, *more):
        blocks = [out_proj[:, j * width : (j + 1) * width] for j in range(D // width)]
        return jnp.concatenate([in_proj.reshape(-1, width), *blocks, *more], axis=0)

    biases = jnp.concatenate([self_in_bias, cross_in_bias, feed_in_bias.reshape(-1, width)], axis=0)
    high = lax.reduce_precision(biases, 8, 7)
    middle = lax.reduce_precision(biases - high, 8, 7)
    low = (biases - high - middle).astype(bf16)
    high, middle = high.astype(bf16), middle.astype(bf16)
    mask_rows = valid_mask.astype(bf16).reshape(2, -1, width)
    mask_kept = jnp.where(first, mask_rows[0], mask_rows[1])
    mask_sent = jnp.where(first, mask_rows[1], mask_rows[0])
    self_shard = attention_weights(
        self_input_projection, self_out_proj, high, middle, low, mask_sent, mask_kept, jnp.zeros((4, width), bf16)
    )
    ids = jnp.concatenate(
        [own_first(target_segments, mine, rank), own_first(source_segments, mine, rank)], axis=0
    )
    self_near = [self_shard, partner(self_shard, 1)]
    self_across = partner(self_shard, 2)

    half_shapes = [
        shape((own, 2 * PAIR), bf16), shape((length, 2 * PAIR), bf16), shape((length, 2 * PAIR), bf16),
        shape((own, 2 * PAIR), bf16), shape((own, PAIR), f32),
    ]
    full = (own, D)
    sums_shape = shape((32, D), f32)

    def parts(index, packs, at):
        return list(packs), {at + i: pack_part(index) for i in range(len(packs))}

    def tails(packs, at):
        return list(packs), {at + i: PACK_TAIL for i in range(len(packs))}

    def laid(operands, *groups):
        blocks = {}
        for group in groups:
            if isinstance(group, tuple):
                more, places = group[0](*group[1:], len(operands))
                operands = operands + more
                blocks.update(places)
            else:
                operands = operands + group
        return operands, blocks

    def sequence(array, at):
        return [array], {at: of_sequence(array)}

    def self_half(shards, x):
        operands, blocks = laid(
            [spots], (sequence, x), (parts, 0, shards), (parts, 1, shards), (parts, 2, shards), (tails, shards), [ids]
        )
        return kernel_call(self_forward, "self_forward", half_shapes, operands, blocks=blocks)

    cross_shard = attention_weights(cross_input_projection, cross_out_proj)
    cross_piece = half_here(cross_shard, 1)
    feed_piece = half_here(feed_in_proj, 1)
    q_a, k_a, v_a, o_a, lse_a = self_half(self_near, tie(decoder_layer_input, cross_piece, feed_piece))
    feed_in_1, feed_out_1, cot_1, cross_piece, feed_piece, cross_shard = tie(
        (feed_in_proj, feed_out_proj, cotangent, cross_piece, feed_piece, cross_shard), q_a
    )
    cot_sent = lax.dynamic_index_in_dim(cot_1, 1 - mine, 0, False).astype(bf16)
    self_far = [self_across, partner(tie(self_across, cot_sent), 1)]
    self_all = self_near + self_far
    cross_got, feed_got = partner(cross_piece, 2), partner(feed_piece, 2)
    q_b, k_b, v_b, o_b, lse_b = self_half(self_far, decoder_layer_input)
    cross_near = [cross_shard, partner(tie(cross_shard, self_across), 1)]
    cross_got, feed_got, cot_sent, feed_in_1, feed_out_1 = tie((cross_got, feed_got, cot_sent, feed_in_1, feed_out_1), q_b)
    cross_got_x, feed_got_x = partner_dp(cross_got, 1), partner_dp(feed_got, 1)
    cut = feed_out_1.shape[0] // 2
    out_top, cot_other = partner(feed_out_1[:cut], 2), partner(cot_sent, 2)
    operands, blocks = laid(
        [spots, o_a, tie(o_b, cross_got, feed_got)], (parts, 3, self_all), (sequence, decoder_layer_input),
        (sequence, encoder_state_rows), (parts, 0, cross_near), (parts, 1, cross_near), (parts, 2, cross_near),
        (tails, self_all[:3]), [ids, out_bias, norm_gain, norm_bias],
    )
    s1, z1, cq_a, ck_a, cv_a, co_a, clse_a, sums, x_own, e_own = kernel_call(
        cross_first,
        "cross_first",
        [shape(full, bf16), shape(full, f32), *half_shapes, sums_shape, shape(full, bf16), shape(full, bf16)],
        operands,
        blocks=blocks,
    )
    cross_got, cross_got_x, feed_got, feed_got_x, out_top, cot_other, feed_in_1, feed_out_1 = tie(
        (cross_got, cross_got_x, feed_got, feed_got_x, out_top, cot_other, feed_in_1, feed_out_1), s1
    )
    cross_across = in_order(cross_got, cross_got_x, 1)
    cross_far = [cross_across, partner(cross_across, 1)]
    cross_all = cross_near + cross_far
    feed_in_across = in_order(feed_got, feed_got_x, 1)
    out_rest = partner(feed_out_1[cut:], 2)
    feed_in_other, feed_out_other = partner(feed_in_1, 1), partner(feed_out_1, 1)
    operands, blocks = laid(
        [spots, tie(s1, feed_in_across, out_top, cot_other), co_a], (sequence, encoder_state_rows),
        (parts, 0, cross_far), (parts, 1, cross_far), (parts, 2, cross_far), (parts, 3, cross_all),
        (tails, [self_all[0], self_all[2], self_all[3]]), [ids, out_bias, norm_gain, norm_bias, sums],
    )
    cq_b, ck_b, cv_b, co_b, clse_b, s2, z2, sums = kernel_call(
        cross_second,
        "cross_second",
        [*half_shapes, shape(full, bf16), shape(full, f32), sums_shape],
        operands,
        blocks=blocks,
    )
    out_top, out_rest = tie((out_top, out_rest), s2)
    feed_out_across = jnp.concatenate([out_top, out_rest], axis=0)
    feed_in_all = [feed_in_1, feed_in_other, feed_in_across, partner(feed_in_across, 1)]
    feed_out_all = [feed_out_1, feed_out_other, feed_out_across, partner(feed_out_across, 1)]

    operands, blocks = laid(
        [spots, s2, z2, *feed_in_all, *feed_out_all], (tails, self_all), [out_bias, norm_gain, norm_bias],
        (sequence, cotangent), [cot_other], (parts, 3, cross_all), [co_a, co_b, sums],
    )
    half = (own, 2 * PAIR)
    out_kept, out_sent, feed_sent, feed_kept, g2, g_cross_a, g_cross_b, cross_out_t, sums = kernel_call(
        feed,
        "feed",
        [
            shape((own // 2, D), bf16), shape((own // 2, D), bf16),
            shape((2, D + units, D), bf16), shape((2, D + units, D), bf16),
            shape(full, f32), shape(half, bf16), shape(half, bf16), shape((4, D, PAIR), bf16), sums_shape,
        ],
        operands,
        scratch=[pltpu.VMEM((4, own, units), f32), pltpu.VMEM((4, own, units), bf16)],
        blocks=blocks,
    )
    feed_got = partner(feed_sent, 1)
    out_got = partner(out_sent, 2)

    kv_shapes = [shape(full, bf16), shape(full, f32), shape((2, D, PAIR), bf16)]

    def back_far(source, heads, g, rows):
        return kernel_call(
            lambda *refs: far_back(source, *refs),
            "attention_back",
            [*kv_shapes, shape(half, bf16), shape((8, D), f32)],
            [*heads, g, ids, rows],
            smem=0,
            scratch=[pltpu.VMEM(half, f32)],
        )

    def finished(first_pair, mode, kept, got, rows, shards, part, along, small, acc=None):
        n_out = len(along)
        last = [shape((own // 2, D), f32), shape((own // 2, D), bf16)] if mode == "last" else [shape(full, f32)]
        count = (3 + n_out) * D + (96 if n_out else 64)
        operands, blocks = laid([kept, got, rows], (parts, 1, shards), (parts, 2, shards), [part])
        if n_out:
            blocks.update(
                {len(operands) + n: ((2, D, PAIR), lambda *scalars: (first_pair // 2, 0, 0)) for n in range(n_out)}
            )
        return kernel_call(
            lambda *refs: finish(first_pair, mode, n_out, *refs),
            "finish",
            [shape((count, width), bf16), shape((count, width), bf16), *last],
            operands + list(along) + [small] + ([] if acc is None else [acc]),
            smem=0,
            blocks=blocks,
            us=2,
        )

    def added(*parts):
        total = parts[0].astype(f32)
        for part in parts[1:]:
            total = total + part.astype(f32)
        return total

    gkv_sent_b, gkv_kept_b, part_b, low_b, sums_b = back_far(1, [cq_b, ck_b, cv_b, co_b, clse_b], g_cross_b, s1)
    gkv_got_b = partner(gkv_sent_b, 1)
    feed_kept, feed_got = tie((feed_kept, feed_got), low_b)

    def half_of(rows, sent):
        cut = rows.shape[-2] // 2
        upper = (lax.axis_index("dp") & 1) != 0
        first, second = rows[..., :cut, :], rows[..., cut:, :]
        return jnp.where(upper, first, second) if sent else jnp.where(upper, second, first)

    in_y = added(feed_kept[1, :D], feed_got[1, :D]).astype(bf16)
    out_x = added(half_of(feed_kept[:, D:], True), half_of(feed_got[:, D:], True)).astype(bf16)
    in_y_got, out_x_got = partner(in_y, 2), partner_dp(out_x, 1)
    operands, blocks = laid(
        [spots, cq_a, ck_a, cv_a, co_a, clse_a, g_cross_a, ids, s1, tie(low_b, in_y, out_x, out_got), g2],
        (parts, 0, cross_all), [z1, norm_gain, o_a, o_b], (parts, 3, self_all), [sums_b, sums],
    )
    gkv_sent, gkv_kept, part_a, g1, g_self_a, g_self_b, self_out_t, sums_a, sums = kernel_call(
        cross_back_norm,
        "cross_back_norm",
        [
            *kv_shapes, shape(full, f32), shape(half, bf16), shape(half, bf16), shape((4, D, PAIR), bf16),
            shape((8, D), f32), sums_shape,
        ],
        operands,
        scratch=[pltpu.VMEM(half, f32)],
        blocks=blocks,
    )
    gkv_got = partner(gkv_sent, 1)
    in_y_got, out_x_got, feed_kept, feed_got = tie((in_y_got, out_x_got, feed_kept, feed_got), g1)
    in_x = added(half_of(feed_kept[0, :D], True), half_of(feed_got[0, :D], True), half_of(in_y_got, True)).astype(bf16)
    out_y = added(half_of(feed_kept[1, D:], False), half_of(feed_got[1, D:], False), out_x_got[1]).astype(bf16)
    in_x_got, out_y_got = partner_dp(in_x, 1), partner(out_y, 2)
    cb_kept, cb_sent, enc_acc = finished(
        2, "start", gkv_kept_b, gkv_got_b, tie(e_own, g1, in_x, out_y), cross_far, part_b, [cross_out_t, self_out_t], sums
    )
    cb_got = partner(cb_sent, 1)

    gkv_sent_b, gkv_kept_b, part_b, low_b, sums_b = back_far(
        0, [q_b, k_b, v_b, o_b, lse_b], g_self_b, tie(x_own, enc_acc)
    )
    gkv_got_b = partner(gkv_sent_b, 1)
    cb_kept, cb_got, in_x_got, out_y_got = tie((cb_kept, cb_got, in_x_got, out_y_got), low_b)
    cross_b = added(cb_kept, cb_got).astype(bf16)
    cut = cross_b.shape[0] // 2
    cross_y = [partner(cross_b[:cut], 2), partner(cross_b[cut:], 2)]
    feed_total = jnp.stack(
        [
            added(half_of(feed_kept[0, :D], False), half_of(feed_got[0, :D], False), half_of(in_y_got, False), in_x_got),
            added(half_of(feed_kept[0, D:], False), half_of(feed_got[0, D:], False), out_x_got[0], out_y_got),
        ]
    )
    feed_sum = DpSum(feed_total, dp_bits()[1:])
    ca_kept, ca_sent, enc_kept, enc_sent = finished(
        0, "last", gkv_kept, gkv_got, tie(e_own, cross_b, feed_sum.value), cross_near, part_a,
        [cross_out_t, self_out_t], sums, enc_acc,
    )
    ca_got = partner(ca_sent, 1)
    sb_kept, sb_sent, acc = finished(
        2, "middle", gkv_kept_b, gkv_got_b, tie(x_own, enc_kept, cross_y[0]), self_far, part_b, [], sums_b, g1
    )
    sb_got = partner(sb_sent, 1)
    feed_sum.step(acc)
    self_b = added(sb_kept, sb_got).astype(bf16)
    self_y = partner(self_b, 2)
    cross_y, ca_kept, ca_got = tie((cross_y, ca_kept, ca_got), self_b, feed_sum.value)
    cross_sum = DpSum(added(ca_kept, ca_got, jnp.concatenate(cross_y, axis=0)), dp_bits())
    operands, blocks = laid(
        [q_a, k_a, v_a, o_a, lse_a, g_self_a, ids, x_own, tie(low_b, self_b, feed_sum.value, cross_sum.value), acc],
        (parts, 0, self_all),
    )
    gkv_sent, gkv_kept, part_a, acc, sums_a = kernel_call(
        self_back,
        "self_back",
        [*kv_shapes, shape(full, f32), shape((8, D), f32)],
        operands,
        smem=0,
        scratch=[pltpu.VMEM(half, f32)],
        blocks=blocks,
    )
    gkv_got = partner(gkv_sent, 1)
    feed_sum.step(acc)
    cross_sum.step(acc)
    sa_kept, sa_sent, in_kept, in_sent = finished(
        0, "last", gkv_kept, gkv_got, tie(x_own, feed_sum.value, cross_sum.value), self_near, part_a, [], sums_a, acc
    )
    sa_got = partner(sa_sent, 1)
    feed_sum.step(in_kept)
    cross_sum.step(in_kept)
    self_y = tie(self_y, in_kept)
    self_sum = DpSum(added(sa_kept, sa_got, self_y), dp_bits())
    enc_sent, in_sent = tie((enc_sent, in_sent), self_sum.value)
    enc_got, in_got = partner(enc_sent, 2), partner(in_sent, 2)

    def to_owner(kept, other):
        other = other.astype(kept.dtype)
        return jnp.stack([jnp.where(first, kept, other), jnp.where(first, other, kept)])

    def in_grad(total):
        return total[: 3 * D].reshape(3, D, width).astype(f32)

    def out_grad(total):
        blocks = [total[c * width : (c + 1) * width] for c in range(D // width)]
        return jnp.concatenate(blocks, axis=1).astype(f32)

    cross_sum.step(self_sum.value)
    feed_total = feed_sum.finish(cross_sum.value)
    self_sum.step()
    layer_output = to_owner(out_kept, tie(out_got, self_sum.value))
    feed_total = tie(feed_total, self_sum.value)
    feed_in_grad, feed_out_grad = feed_total[0].astype(f32), feed_total[1].astype(f32)
    cross_sum.step(self_sum.value, feed_in_grad)
    self_sum.step(layer_output, feed_out_grad)
    encoder_grad = to_owner(enc_kept, tie(enc_got, self_sum.value))
    self_sum.step(encoder_grad)
    input_grad = to_owner(in_kept, tie(in_got, self_sum.value))
    cross_total = cross_sum.finish(self_sum.value)
    self_sum.step(cross_total, input_grad)
    cross_total = tie(cross_total, self_sum.value)
    cross_in_grad, cross_out_grad = in_grad(cross_total), out_grad(cross_total[3 * D : 4 * D])
    self_out_grad = out_grad(cross_total[4 * D : 5 * D])
    common = cross_total[5 * D : 5 * D + 64].astype(f32).reshape(4, 16, PAIR).swapaxes(0, 1).reshape(16, 4 * PAIR)
    shard_sums = cross_total[5 * D + 64 : 5 * D + 72].astype(f32)
    rms_values = jnp.sqrt(jnp.sum(common[0:4], axis=1) / (jnp.sum(common[13]) * D))
    self_total = self_sum.finish(cross_in_grad, cross_out_grad, self_out_grad, common, shard_sums, rms_values)

    return (
        layer_output,
        input_grad,
        encoder_grad,
        in_grad(self_total),
        self_total[3 * D : 3 * D + 2].astype(f32),
        self_out_grad,
        cross_in_grad,
        shard_sums[0:2],
        cross_out_grad,
        feed_in_grad,
        shard_sums[2:6].reshape(units),
        feed_out_grad,
        jnp.stack([common[12], common[9], common[6]]),
        jnp.stack([common[10], common[7], common[4]]),
        jnp.stack([common[11], common[8], common[5]]),
        rms_values,
    )


def solution(mesh):
    return jax.shard_map(
        per_device,
        mesh=mesh,
        in_specs=(
            P("dp", None, None),
            P("dp", None, None),
            P("dp", None),
            P("dp", None),
            P("dp", "tensor"),
            P("dp", "tensor", None),
            P(None, None, "tensor"),
            P(None, "tensor"),
            P("tensor", None),
            P(None, None, "tensor"),
            P(None, "tensor"),
            P("tensor", None),
            P(None, "tensor"),
            P("tensor"),
            P("tensor", None),
            P(),
            P(),
            P(),
        ),
        out_specs=(
            P("dp", "tensor", None),
            P("dp", "tensor", None),
            P("dp", "tensor", None),
            P(None, None, "tensor"),
            P(None, "tensor"),
            P("tensor", None),
            P(None, None, "tensor"),
            P(None, "tensor"),
            P("tensor", None),
            P(None, "tensor"),
            P("tensor"),
            P("tensor", None),
            P(),
            P(),
            P(),
            P(),
        ),
        check_vma=False,
    )
```

```python
import jax
import jax.numpy as jnp
from jax import lax
from jax.experimental import pallas as pl
from jax.experimental.pallas import tpu as pltpu
from jax.sharding import PartitionSpec as P

D = 512
HEAD = 64
EPSILON = 1e-05
PAIR = 2 * HEAD
FAR = 2.0**100
SCALE = HEAD ** (-0.5)
bf16, f32 = jnp.bfloat16, jnp.float32


def partner(array_in, bit):
    count = lax.axis_size("tensor")
    return lax.ppermute(array_in, "tensor", [(i, i ^ bit) for i in range(count)])


def partner_dp(array_in, bit):
    count = lax.axis_size("dp")
    return lax.ppermute(array_in, "dp", [(i, i ^ bit) for i in range(count)])


def tie(value, *others):
    return lax.optimization_barrier((value, others))[0]


def dp_bits():
    bits = []
    bit = 1
    while bit < lax.axis_size("dp"):
        bits.append(bit)
        bit *= 2
    return bits


def halves(total, bit):
    upper = (lax.axis_index("dp") & bit) != 0
    half = total.shape[-2] // 2
    first, second = total[..., :half, :], total[..., half:, :]
    return jnp.where(upper, second, first), jnp.where(upper, first, second).astype(bf16)


def in_order(mine, other, bit):
    upper = (lax.axis_index("dp") & bit) != 0
    return jnp.concatenate([jnp.where(upper, other, mine), jnp.where(upper, mine, other)], axis=-2)


def half_here(rows, bit):
    half = rows.shape[0] // 2
    upper = (lax.axis_index("dp") & bit) != 0
    return jnp.where(upper, rows[half:], rows[:half])


class DpSum:
    def __init__(self, total, bits):
        self.todo = [("half", bit) for bit in bits[:-1]] + [("swap", bits[-1])]
        self.todo += [("double", bit) for bit in reversed(dp_bits()[:-1])]
        self.value = total
        self.start()

    def start(self):
        kind, bit = self.todo[0]
        if kind == "half":
            self.kept, self.value = halves(self.value, bit)
        else:
            self.kept = self.value = self.value.astype(bf16)
        self.got = partner_dp(self.value, bit)

    def step(self, *after):
        if self.todo:
            if after:
                self.kept, self.got = tie((self.kept, self.got), *after)
            kind, bit = self.todo.pop(0)
            if kind == "double":
                self.value = in_order(self.kept, self.got, bit)
            else:
                self.value = self.kept.astype(f32) + self.got.astype(f32)
            if self.todo:
                self.start()
        return self.value

    def finish(self, *after):
        while self.todo:
            self.step(*after)
        return self.value


def dot_nn(a, b):
    return lax.dot_general(a, b, (((1,), (0,)), ((), ())), preferred_element_type=f32)


def dot_nt(a, b):
    return lax.dot_general(a, b, (((1,), (1,)), ((), ())), preferred_element_type=f32)


def dot_tn(a, b):
    return lax.dot_general(a, b, (((0,), (0,)), ((), ())), preferred_element_type=f32)


def lane_in_head(count):
    return lax.broadcasted_iota(jnp.int32, (count, PAIR), 1) & (HEAD - 1)


def lane_low(count):
    return lax.broadcasted_iota(jnp.int32, (count, PAIR), 1) < HEAD


def as_columns(row):
    return jnp.broadcast_to(row.astype(f32), (PAIR, row.shape[1])).T


def minus_pieces(column, lane):
    high = column.astype(bf16).astype(f32)
    rest = column - high
    middle = rest.astype(bf16).astype(f32)
    low = rest - middle
    return jnp.where(lane == 4, -high, jnp.where(lane == 5, -middle, jnp.where(lane == 6, -low, 0.0)))


def query_extra(ids):
    lane = lane_in_head(ids.shape[0])
    return jnp.where((lane < 4) & (lane.astype(f32) != ids), -FAR, 0.0)


def key_extra(ids):
    lane = lane_in_head(ids.shape[0])
    ones = (lane >= 4) & (lane < 7)
    return jnp.where((lane.astype(f32) == ids) | ones, 1.0, 0.0).astype(bf16)


def attend(pairs, q_ref, k_ref, v_ref, q_extra, k_extra, o_ref, lse_ref):
    n_q, n_k = q_ref.shape[0], k_ref.shape[0]
    low_q, low_k = lane_low(n_q), lane_low(n_k)
    lane = lax.broadcasted_iota(jnp.int32, (n_q, PAIR), 1)
    extra = q_extra.astype(bf16)
    lse_all = jnp.zeros((n_q, PAIR), f32)
    for i in range(pairs):
        c = slice(i * PAIR, (i + 1) * PAIR)
        q2, k2, v2 = q_ref[:, c] * bf16(SCALE), k_ref[:, c], v_ref[:, c]
        scores = [
            dot_nt(jnp.where(low_q, q2, extra), jnp.where(low_k, k2, k_extra)),
            dot_nt(jnp.where(low_q, extra, q2), jnp.where(low_k, k_extra, k2)),
        ]
        outs = []
        for h in range(2):
            top = jnp.max(scores[h], axis=1, keepdims=True)
            terms = jnp.exp(scores[h] - top)
            total = jnp.sum(terms, axis=1, keepdims=True)
            outs.append(dot_nn(terms.astype(bf16), v2) * (1.0 / total))
            lse_all = jnp.where(lane == 2 * i + h, top + jnp.log(total), lse_all)
        o_ref[:, c] = jnp.where(low_q, outs[0], outs[1]).astype(bf16)
    lse_ref[...] = lse_all


def attend_back(pairs, base, q_ref, k_ref, v_ref, o_ref, g_ref, lse_ref, q_extra, k_extra, gq_ref, store):
    n_q, n_k = q_ref.shape[0], k_ref.shape[0]
    low_q, low_k = lane_low(n_q), lane_low(n_k)
    lane = lax.broadcasted_iota(jnp.int32, (n_q, PAIR), 1)
    head_lane = lane_in_head(n_q)
    key_lane = lane_in_head(n_k)
    v_extra = jnp.where((key_lane >= 4) & (key_lane < 7), 1.0, 0.0).astype(bf16)
    nothing = jnp.zeros((n_q, PAIR), bf16)
    lse_all = lse_ref[...]
    for i in range(pairs):
        c = slice(i * PAIR, (i + 1) * PAIR)
        q2, k2, v2, g2 = q_ref[:, c] * bf16(SCALE), k_ref[:, c], v_ref[:, c], g_ref[:, c]
        product = g2.astype(f32) * o_ref[:, c].astype(f32)
        gk, gv, gq = [], [], []
        for h in range(2):
            own_q = low_q if h == 0 else ~low_q
            own_k = low_k if h == 0 else ~low_k
            dots = jnp.sum(jnp.where(own_q, product, 0.0), axis=1, keepdims=True)
            lse = jnp.sum(jnp.where(lane == base + 2 * i + h, lse_all, 0.0), axis=1, keepdims=True)
            q_more = jnp.where(own_q, q2, (q_extra + minus_pieces(lse, head_lane)).astype(bf16))
            g_more = jnp.where(own_q, g2, minus_pieces(dots, head_lane).astype(bf16))
            probs = jnp.exp(dot_nt(jnp.where(own_k, k2, k_extra), q_more))
            g_scores = (probs * dot_nt(jnp.where(own_k, v2, v_extra), g_more)).astype(bf16)
            gv.append(dot_nn(probs.astype(bf16), jnp.where(own_q, g2, nothing)))
            gk.append(dot_nn(g_scores, jnp.where(own_q, q2, nothing)))
            gq.append(dot_tn(g_scores, k2))
        store(i, gk[0] + gk[1], gv[0] + gv[1])
        gq_ref[:, c] = jnp.where(low_q, gq[0], gq[1]) * SCALE


def normed(z):
    centred = z - jnp.mean(z, axis=-1, keepdims=True)
    r = lax.rsqrt(jnp.mean(centred * centred, axis=-1, keepdims=True) + EPSILON)
    return centred * r, r


def norm_back(z, gain, upstream):
    xhat, r = normed(z)
    inner = gain * upstream
    grad = r * (
        inner
        - jnp.mean(inner, axis=-1, keepdims=True)
        - xhat * jnp.mean(inner * xhat, axis=-1, keepdims=True)
    )
    return grad, column_sum(upstream * xhat), column_sum(upstream)


def column_sum(array_in):
    return jnp.sum(array_in, axis=0, keepdims=True)


def lanes(refs):
    return jnp.concatenate([r[...] for r in refs], axis=1)


def bias_row(packs, index):
    rows = [
        sum(p[8 * n + index : 8 * n + index + 1, :].astype(f32) for n in (0, 1, 2)) for p in packs
    ]
    return jnp.concatenate(rows, axis=1)


def mask_column(own_pack, across_pack):
    first = 24
    row = jnp.concatenate([p[first + i : first + i + 1, :] for p, i in ((own_pack, 2), (own_pack, 3), (across_pack, 0), (across_pack, 1))], axis=1)
    return as_columns(row)[:, 0:1], row.astype(f32)


def stacked(refs):
    return jnp.concatenate([r[...] for r in refs], axis=0)


def sequence_rows(spots, ref, blocks):
    size = ref.shape[1] // 4
    return jnp.concatenate(
        [ref[0, pl.ds(pl.multiple_of(spots[1 + j] * size, size), size), :] for j in range(blocks)], axis=0
    )


def kernel_call(body, name, out_shape, operands, smem=1, scratch=(), blocks=(), us=5, limit=36):
    blocks = dict(blocks)

    def spec(dims, place):
        return pl.BlockSpec(dims, lambda step, *scalars: place(*scalars))

    def whole(dims):
        return spec(dims, lambda *scalars: (0,) * len(dims))

    return pl.pallas_call(
        lambda *refs: body(*refs),
        name=name,
        out_shape=out_shape,
        grid_spec=pltpu.PrefetchScalarGridSpec(
            num_scalar_prefetch=smem,
            grid=(1,),
            in_specs=[spec(*blocks[i]) if i in blocks else whole(operands[i].shape) for i in range(smem, len(operands))],
            out_specs=[whole(o.shape) for o in out_shape],
            scratch_shapes=scratch,
        ),
        compiler_params=pltpu.CompilerParams(vmem_limit_bytes=limit * 2**20),
        cost_estimate=pl.CostEstimate(flops=int(us * 1e9), bytes_accessed=1000, transcendentals=0),
    )(*operands)


def pack_part(index):
    return ((D, PAIR), lambda *scalars: (index, 0))


PACK_TAIL = ((32, PAIR), lambda *scalars: (4 * D // 32, 0))


def of_sequence(array):
    return ((1, *array.shape[1:]), lambda spots: (spots[0],) + (0,) * (array.ndim - 1))


def shape(dims, dtype):
    return jax.ShapeDtypeStruct(dims, dtype)


def self_forward(spots, x, q_w, q_x, k_w, k_x, v_w, v_x, t_w, t_x, ids, q_ref, k_ref, v_ref, o_ref, lse_ref):
    rows = sequence_rows(spots, x, 4)
    own = q_ref.shape[0]
    q_ref[...] = (dot_nn(rows[:own], lanes([q_w, q_x])) + bias_row([t_w, t_x], 0)).astype(bf16)
    k_ref[...] = dot_nn(rows, lanes([k_w, k_x])).astype(bf16)
    v_ref[...] = (dot_nn(rows, lanes([v_w, v_x])) + bias_row([t_w, t_x], 1)).astype(bf16)
    columns = as_columns(ids[0:1, :])
    attend(2, q_ref, k_ref, v_ref, query_extra(columns[:own]), key_extra(columns), o_ref, lse_ref)


def out_rows(shards):
    blocks = D // PAIR
    return jnp.concatenate(
        [
            jnp.concatenate([s[j * PAIR : (j + 1) * PAIR, :] for j in range(blocks)], axis=1)
            for s in shards
        ],
        axis=0,
    )


def cross_heads(stream, rows, weights, tails, ids, q_ref, k_ref, v_ref, o_ref, lse_ref):
    own = q_ref.shape[0]
    q_ref[...] = (dot_nn(stream, lanes(weights[0:2])) + bias_row(tails, 2)).astype(bf16)
    k_ref[...] = dot_nn(rows, lanes(weights[2:4])).astype(bf16)
    v_ref[...] = (dot_nn(rows, lanes(weights[4:6])) + bias_row(tails, 3)).astype(bf16)
    queries = query_extra(as_columns(ids[0:1, :own]))
    attend(2, q_ref, k_ref, v_ref, queries, key_extra(as_columns(ids[1:2, :])), o_ref, lse_ref)


def cross_first(
    spots, o_a, o_b, so0, so1, so2, so3, x, e, q_w, q_x, k_w, k_x, v_w, v_x, t0, t1, t2, ids, out_bias, gain, shift,
    s1_ref, z1_ref, q_ref, k_ref, v_ref, o_ref, lse_ref, sums_ref, xo_ref, eo_ref,
):
    own = q_ref.shape[0]
    valid, valid_row = mask_column(t0, t2)
    branch = dot_nn(lanes([o_a, o_b]), out_rows([so0, so1, so2, so3])) + out_bias[0:1, :]
    sums_ref[...] = jnp.zeros_like(sums_ref)
    sums_ref[0:1, :] = column_sum(valid * branch * branch)
    sums_ref[13:14, :] = valid_row
    x_own = sequence_rows(spots, x, 2)
    xo_ref[...] = x_own
    z = x_own.astype(f32) + branch
    z1_ref[...] = z
    stream = (normed(z)[0] * gain[0:1, :] + shift[0:1, :]).astype(bf16)
    s1_ref[...] = stream
    rows = sequence_rows(spots, e, 4)
    eo_ref[...] = rows[:own]
    cross_heads(stream, rows, [q_w, q_x, k_w, k_x, v_w, v_x], [t0, t1], ids, q_ref, k_ref, v_ref, o_ref, lse_ref)


def cross_second(
    spots, s1, o_a, e, q_w, q_x, k_w, k_x, v_w, v_x, co0, co1, co2, co3, t0, t2, t3, ids, out_bias, gain, shift, sums,
    q_ref, k_ref, v_ref, o_ref, lse_ref, s2_ref, z2_ref, sums_ref,
):
    stream = s1[...]
    valid = mask_column(t0, t2)[0]
    rows = sequence_rows(spots, e, 4)
    cross_heads(stream, rows, [q_w, q_x, k_w, k_x, v_w, v_x], [t2, t3], ids, q_ref, k_ref, v_ref, o_ref, lse_ref)
    branch = dot_nn(lanes([o_a, o_ref]), out_rows([co0, co1, co2, co3])) + out_bias[1:2, :]
    sums_ref[...] = sums[...]
    sums_ref[1:2, :] = column_sum(valid * branch * branch)
    z = stream.astype(f32) + branch
    z2_ref[...] = z
    s2_ref[...] = (normed(z)[0] * gain[1:2, :] + shift[1:2, :]).astype(bf16)


def feed(
    spots, s2, z2, fi0, fi1, fi2, fi3, fo0, fo1, fo2, fo3, b0, b1, b2, b3, out_bias, gain, shift, cot, cot_other,
    co0, co1, co2, co3, o_a, o_b, sums,
    kept_out, sent_out, sent_parts, kept_parts, g2_ref, gc_a, gc_b, out_t, sums_ref,
    slope, hidden,
):
    curve = (2.0 / 3.141592653589793) ** 0.5
    stream = s2[...]
    rows, width = stream.shape[0], fi0.shape[1]
    valid = mask_column(b0, b2)[0]
    sums_ref[...] = sums[...]
    branch = jnp.zeros((rows, D), f32) + out_bias[2:3, :]
    ins, outs, offsets = [fi0, fi1, fi2, fi3], [fo0, fo1, fo2, fo3], [b0, b1, b2, b3]
    for j in range(4):
        offset = jnp.concatenate([bias_row([offsets[j]], 4 + n) for n in range(width // PAIR)], axis=1)
        pre = dot_nn(stream, ins[j][...]) + offset
        square = pre * pre
        bend = jnp.tanh(curve * pre * (1.0 + 0.044715 * square))
        half = 0.5 * (1.0 + bend)
        slope[j] = half + 0.5 * pre * (1.0 - bend * bend) * (curve * (1.0 + 3.0 * 0.044715 * square))
        units = (pre * half).astype(bf16)
        hidden[j] = units
        branch = branch + dot_nn(units, outs[j][...])
    z = stream.astype(f32) + branch
    final = normed(z)[0] * gain[2:3, :] + shift[2:3, :]
    low = final.astype(bf16)
    kept_out[...] = low[: rows // 2]
    sent_out[...] = low[rows // 2 :]
    sums_ref[2:3, :] = column_sum(valid * branch * branch)
    sums_ref[3:4, :] = column_sum(valid * final * final)
    upstream = jnp.concatenate([cot[0], cot_other[...].astype(f32)], axis=0) * valid
    g3, row_gain, row_shift = norm_back(z, gain[2:3, :], upstream)
    sums_ref[4:5, :] = row_gain
    sums_ref[5:6, :] = row_shift
    sums_ref[6:7, :] = column_sum(g3)
    g_low = g3.astype(bf16)
    up = g3
    for j in range(4):
        g_pre = dot_nt(g_low, outs[j][...]) * slope[j]
        store_shard_row(sums_ref, j, 1, column_sum(g_pre))
        pre_low = g_pre.astype(bf16)
        up = up + dot_nt(pre_low, ins[j][...])
        to = sent_parts if j % 2 else kept_parts
        to[j // 2, 0:D, :] = dot_tn(stream, pre_low).astype(bf16)
        to[j // 2, D : D + width, :] = dot_tn(hidden[j], g_low).astype(bf16)
    g2, row_gain, row_shift = norm_back(z2[...], gain[1:2, :], up)
    sums_ref[7:8, :] = row_gain
    sums_ref[8:9, :] = row_shift
    sums_ref[9:10, :] = column_sum(g2)
    g2_ref[...] = g2
    g_low = g2.astype(bf16)
    g_cross = dot_nt(g_low, out_rows([co0, co1, co2, co3])).astype(bf16)
    gc_a[...] = g_cross[:, : 2 * PAIR]
    gc_b[...] = g_cross[:, 2 * PAIR :]
    store_blocks(out_t, dot_tn(lanes([o_a, o_b]), g_low))


def store_shard_row(sums_ref, j, row, value):
    sums_ref[16 + 2 * j + row : 17 + 2 * j + row, : value.shape[1]] = value


def store_chunks(to, part):
    for j in range(to.shape[0]):
        to[j] = part[:, j * PAIR : (j + 1) * PAIR].astype(bf16)


def store_blocks(to, part):
    for j in range(4):
        for c in range(D // PAIR):
            block = part[j * PAIR : (j + 1) * PAIR, c * PAIR : (c + 1) * PAIR]
            to[j, c * PAIR : (c + 1) * PAIR, :] = block.astype(bf16)


def kv_store(sent_ref, kept_ref, sums_ref):
    own, width = kept_ref.shape[0], kept_ref.shape[1] // 2

    def store(i, gk, gv):
        here = i * PAIR
        there = (i ^ 1) * PAIR
        kept_ref[:, here : here + PAIR] = gk[:own]
        kept_ref[:, width + here : width + here + PAIR] = gv[:own]
        sent_ref[:, there : there + PAIR] = gk[own:].astype(bf16)
        sent_ref[:, width + there : width + there + PAIR] = gv[own:].astype(bf16)
        sums_ref[1:2, here : here + PAIR] = column_sum(gv)

    return store


def half_back(source, q, k, v, o, lse, g, ids, rows, sent_ref, kept_ref, part_q, sums_ref, gq_ref):
    own = q.shape[0]
    sums_ref[...] = jnp.zeros_like(sums_ref)
    queries = query_extra(as_columns(ids[0:1, :own]))
    keys = key_extra(as_columns(ids[source : source + 1, :]))
    store = kv_store(sent_ref, kept_ref, sums_ref)
    attend_back(2, 0, q, k, v, o, g, lse, queries, keys, gq_ref, store)
    gq = gq_ref[...]
    sums_ref[0:1, : 2 * PAIR] = column_sum(gq)
    low = gq.astype(bf16)
    store_chunks(part_q, dot_tn(rows[...], low))
    return low


def far_back(source, q, k, v, o, lse, g, ids, rows, sent, kept, part_q, low_ref, sums, gq_ref):
    low_ref[...] = half_back(source, q, k, v, o, lse, g, ids, rows, sent, kept, part_q, sums, gq_ref)


def self_back(
    q, k, v, o, lse, g, ids, rows, low_b, acc, w0, w1, w2, w3, sent, kept, part_q, acc_ref, sums, gq_ref
):
    low = half_back(0, q, k, v, o, lse, g, ids, rows, sent, kept, part_q, sums, gq_ref)
    acc_ref[...] = acc[...] + dot_nt(low, lanes([w0, w1])) + dot_nt(low_b[...], lanes([w2, w3]))


def cross_back_norm(
    spots, q, k, v, o, lse, g, ids, rows, low_b, acc, w0, w1, w2, w3, z1, gain, o_a, o_b, so0, so1, so2, so3, sums_b,
    carried,
    sent, kept, part_q, g1_ref, gs_a, gs_b, out_t, sums, all_ref, gq_ref,
):
    low = half_back(1, q, k, v, o, lse, g, ids, rows, sent, kept, part_q, sums, gq_ref)
    up = acc[...] + dot_nt(low, lanes([w0, w1])) + dot_nt(low_b[...], lanes([w2, w3]))
    g1, row_gain, row_shift = norm_back(z1[...], gain[0:1, :], up)
    all_ref[...] = carried[...]
    all_ref[10:11, :] = row_gain
    all_ref[11:12, :] = row_shift
    all_ref[12:13, :] = column_sum(g1)
    for j in range(4):
        c = slice((j % 2) * PAIR, (j % 2 + 1) * PAIR)
        of = sums if j < 2 else sums_b
        store_shard_row(all_ref, j, 0, jnp.concatenate([of[0:1, c], of[1:2, c]], axis=1))
    g1_ref[...] = g1
    g_low = g1.astype(bf16)
    g_self = dot_nt(g_low, out_rows([so0, so1, so2, so3])).astype(bf16)
    gs_a[...] = g_self[:, : 2 * PAIR]
    gs_b[...] = g_self[:, 2 * PAIR :]
    store_blocks(out_t, dot_tn(lanes([o_a, o_b]), g_low))


def finish(first, mode, n_out, *refs):
    kept, other, rows, k_w, k_x, v_w, v_x, part_q, *refs = refs
    along, sums, refs = refs[:n_out], refs[n_out], refs[n_out + 1 :]
    outs = refs if mode == "start" else refs[1:]
    both = (kept[...] + other[...].astype(f32)).astype(bf16)
    gk, gv = both[:, : 2 * PAIR], both[:, 2 * PAIR :]
    res = dot_nt(gk, lanes([k_w, k_x])) + dot_nt(gv, lanes([v_w, v_x]))
    if mode != "start":
        res = res + refs[0][...]
    part = dot_tn(rows[...], both).astype(bf16)
    for j in range(2):
        to = outs[j]
        to[0:D, :] = part_q[j]
        to[D : 2 * D, :] = part[:, j * PAIR : (j + 1) * PAIR]
        to[2 * D : 3 * D, :] = part[:, (2 + j) * PAIR : (3 + j) * PAIR]
        for n in range(n_out):
            to[(3 + n) * D : (4 + n) * D, :] = along[n][j]
        last = (3 + n_out) * D
        to[last:, :] = jnp.zeros((to.shape[0] - last, PAIR), bf16)
        if n_out == 0:
            to[last : last + 2, :] = sums[0:2, j * PAIR : (j + 1) * PAIR].astype(bf16)
        else:
            for c in range(4):
                to[last + 16 * c : last + 16 * (c + 1), :] = sums[0:16, c * PAIR : (c + 1) * PAIR].astype(bf16)
            row = 16 + 2 * (first + j)
            blocks = [(row, 0), (row, 1), (row + 1, 0), (row + 1, 1), (row + 1, 2), (row + 1, 3)]
            shard_rows = jnp.concatenate(
                [sums[r : r + 1, c * PAIR : (c + 1) * PAIR] for r, c in blocks] + [jnp.zeros((2, PAIR), f32)], axis=0
            )
            to[last + 64 : last + 72, :] = shard_rows.astype(bf16)
    if mode == "last":
        half = res.shape[0] // 2
        outs[2][...] = res[:half]
        outs[3][...] = res[half:].astype(bf16)
    else:
        outs[2][...] = res


def own_first(ids, mine, rank):
    row = lax.dynamic_index_in_dim(ids, mine, 0, True)
    size = ids.shape[1] // 4
    parts = [
        lax.dynamic_slice_in_dim(row, (rank ^ step) * size, size, 1) for step in (0, 2, 1, 3)
    ]
    return jnp.concatenate(parts, axis=1)


def per_device(
    decoder_layer_input,
    encoder_state_rows,
    target_segments,
    source_segments,
    valid_mask,
    cotangent,
    self_input_projection,
    self_in_bias,
    self_out_proj,
    cross_input_projection,
    cross_in_bias,
    cross_out_proj,
    feed_in_proj,
    feed_in_bias,
    feed_out_proj,
    out_bias,
    norm_gain,
    norm_bias,
):
    rank = lax.axis_index("tensor")
    mine = rank // 2
    first = mine == 0
    length = decoder_layer_input.shape[1]
    own = length // 2
    width = self_out_proj.shape[0]
    units = feed_in_proj.shape[1]
    spots = jnp.stack([mine, rank, rank ^ 2, rank ^ 1, rank ^ 3]).astype(jnp.int32)

    def attention_weights(in_proj, out_proj, *more):
        blocks = [out_proj[:, j * width : (j + 1) * width] for j in range(D // width)]
        return jnp.concatenate([in_proj.reshape(-1, width), *blocks, *more], axis=0)

    biases = jnp.concatenate([self_in_bias, cross_in_bias, feed_in_bias.reshape(-1, width)], axis=0)
    high = lax.reduce_precision(biases, 8, 7)
    middle = lax.reduce_precision(biases - high, 8, 7)
    low = (biases - high - middle).astype(bf16)
    high, middle = high.astype(bf16), middle.astype(bf16)
    mask_rows = valid_mask.astype(bf16).reshape(2, -1, width)
    mask_kept = jnp.where(first, mask_rows[0], mask_rows[1])
    mask_sent = jnp.where(first, mask_rows[1], mask_rows[0])
    self_shard = attention_weights(
        self_input_projection, self_out_proj, high, middle, low, mask_sent, mask_kept, jnp.zeros((4, width), bf16)
    )
    ids = jnp.concatenate(
        [own_first(target_segments, mine, rank), own_first(source_segments, mine, rank)], axis=0
    )
    self_near = [self_shard, partner(self_shard, 1)]
    self_across = partner(self_shard, 2)

    half_shapes = [
        shape((own, 2 * PAIR), bf16), shape((length, 2 * PAIR), bf16), shape((length, 2 * PAIR), bf16),
        shape((own, 2 * PAIR), bf16), shape((own, PAIR), f32),
    ]
    full = (own, D)
    sums_shape = shape((32, D), f32)

    def parts(index, packs, at):
        return list(packs), {at + i: pack_part(index) for i in range(len(packs))}

    def tails(packs, at):
        return list(packs), {at + i: PACK_TAIL for i in range(len(packs))}

    def laid(operands, *groups):
        blocks = {}
        for group in groups:
            if isinstance(group, tuple):
                more, places = group[0](*group[1:], len(operands))
                operands = operands + more
                blocks.update(places)
            else:
                operands = operands + group
        return operands, blocks

    def sequence(array, at):
        return [array], {at: of_sequence(array)}

    def self_half(shards, x):
        operands, blocks = laid(
            [spots], (sequence, x), (parts, 0, shards), (parts, 1, shards), (parts, 2, shards), (tails, shards), [ids]
        )
        return kernel_call(self_forward, "self_forward", half_shapes, operands, blocks=blocks)

    cross_shard = attention_weights(cross_input_projection, cross_out_proj)
    cross_piece = half_here(cross_shard, 1)
    feed_piece = half_here(feed_in_proj, 1)
    q_a, k_a, v_a, o_a, lse_a = self_half(self_near, tie(decoder_layer_input, cross_piece, feed_piece))
    feed_in_1, feed_out_1, cot_1, cross_piece, feed_piece, cross_shard = tie(
        (feed_in_proj, feed_out_proj, cotangent, cross_piece, feed_piece, cross_shard), q_a
    )
    cot_sent = lax.dynamic_index_in_dim(cot_1, 1 - mine, 0, False).astype(bf16)
    self_far = [self_across, partner(tie(self_across, cot_sent), 1)]
    self_all = self_near + self_far
    cross_got, feed_got = partner(cross_piece, 2), partner(feed_piece, 2)
    q_b, k_b, v_b, o_b, lse_b = self_half(self_far, decoder_layer_input)
    cross_near = [cross_shard, partner(tie(cross_shard, self_across), 1)]
    cross_got, feed_got, cot_sent, feed_in_1, feed_out_1 = tie((cross_got, feed_got, cot_sent, feed_in_1, feed_out_1), q_b)
    cross_got_x, feed_got_x = partner_dp(cross_got, 1), partner_dp(feed_got, 1)
    cut = feed_out_1.shape[0] // 2
    out_top, cot_other = partner(feed_out_1[:cut], 2), partner(cot_sent, 2)
    operands, blocks = laid(
        [spots, o_a, tie(o_b, cross_got, feed_got)], (parts, 3, self_all), (sequence, decoder_layer_input),
        (sequence, encoder_state_rows), (parts, 0, cross_near), (parts, 1, cross_near), (parts, 2, cross_near),
        (tails, self_all[:3]), [ids, out_bias, norm_gain, norm_bias],
    )
    s1, z1, cq_a, ck_a, cv_a, co_a, clse_a, sums, x_own, e_own = kernel_call(
        cross_first,
        "cross_first",
        [shape(full, bf16), shape(full, f32), *half_shapes, sums_shape, shape(full, bf16), shape(full, bf16)],
        operands,
        blocks=blocks,
    )
    cross_got, cross_got_x, feed_got, feed_got_x, out_top, cot_other, feed_in_1, feed_out_1 = tie(
        (cross_got, cross_got_x, feed_got, feed_got_x, out_top, cot_other, feed_in_1, feed_out_1), s1
    )
    cross_across = in_order(cross_got, cross_got_x, 1)
    cross_far = [cross_across, partner(cross_across, 1)]
    cross_all = cross_near + cross_far
    feed_in_across = in_order(feed_got, feed_got_x, 1)
    out_rest = partner(feed_out_1[cut:], 2)
    feed_in_other, feed_out_other = partner(feed_in_1, 1), partner(feed_out_1, 1)
    operands, blocks = laid(
        [spots, tie(s1, feed_in_across, out_top, cot_other), co_a], (sequence, encoder_state_rows),
        (parts, 0, cross_far), (parts, 1, cross_far), (parts, 2, cross_far), (parts, 3, cross_all),
        (tails, [self_all[0], self_all[2], self_all[3]]), [ids, out_bias, norm_gain, norm_bias, sums],
    )
    cq_b, ck_b, cv_b, co_b, clse_b, s2, z2, sums = kernel_call(
        cross_second,
        "cross_second",
        [*half_shapes, shape(full, bf16), shape(full, f32), sums_shape],
        operands,
        blocks=blocks,
    )
    out_top, out_rest = tie((out_top, out_rest), s2)
    feed_out_across = jnp.concatenate([out_top, out_rest], axis=0)
    feed_in_all = [feed_in_1, feed_in_other, feed_in_across, partner(feed_in_across, 1)]
    feed_out_all = [feed_out_1, feed_out_other, feed_out_across, partner(feed_out_across, 1)]

    operands, blocks = laid(
        [spots, s2, z2, *feed_in_all, *feed_out_all], (tails, self_all), [out_bias, norm_gain, norm_bias],
        (sequence, cotangent), [cot_other], (parts, 3, cross_all), [co_a, co_b, sums],
    )
    half = (own, 2 * PAIR)
    out_kept, out_sent, feed_sent, feed_kept, g2, g_cross_a, g_cross_b, cross_out_t, sums = kernel_call(
        feed,
        "feed",
        [
            shape((own // 2, D), bf16), shape((own // 2, D), bf16),
            shape((2, D + units, D), bf16), shape((2, D + units, D), bf16),
            shape(full, f32), shape(half, bf16), shape(half, bf16), shape((4, D, PAIR), bf16), sums_shape,
        ],
        operands,
        scratch=[pltpu.VMEM((4, own, units), f32), pltpu.VMEM((4, own, units), bf16)],
        blocks=blocks,
    )
    feed_got = partner(feed_sent, 1)
    out_got = partner(out_sent, 2)

    kv_shapes = [shape(full, bf16), shape(full, f32), shape((2, D, PAIR), bf16)]

    def back_far(source, heads, g, rows):
        return kernel_call(
            lambda *refs: far_back(source, *refs),
            "attention_back",
            [*kv_shapes, shape(half, bf16), shape((8, D), f32)],
            [*heads, g, ids, rows],
            smem=0,
            scratch=[pltpu.VMEM(half, f32)],
        )

    def finished(first_pair, mode, kept, got, rows, shards, part, along, small, acc=None):
        n_out = len(along)
        last = [shape((own // 2, D), f32), shape((own // 2, D), bf16)] if mode == "last" else [shape(full, f32)]
        count = (3 + n_out) * D + (96 if n_out else 64)
        operands, blocks = laid([kept, got, rows], (parts, 1, shards), (parts, 2, shards), [part])
        if n_out:
            blocks.update(
                {len(operands) + n: ((2, D, PAIR), lambda *scalars: (first_pair // 2, 0, 0)) for n in range(n_out)}
            )
        return kernel_call(
            lambda *refs: finish(first_pair, mode, n_out, *refs),
            "finish",
            [shape((count, width), bf16), shape((count, width), bf16), *last],
            operands + list(along) + [small] + ([] if acc is None else [acc]),
            smem=0,
            blocks=blocks,
            us=2,
        )

    def added(*parts):
        total = parts[0].astype(f32)
        for part in parts[1:]:
            total = total + part.astype(f32)
        return total

    gkv_sent_b, gkv_kept_b, part_b, low_b, sums_b = back_far(1, [cq_b, ck_b, cv_b, co_b, clse_b], g_cross_b, s1)
    gkv_got_b = partner(gkv_sent_b, 1)
    feed_kept, feed_got = tie((feed_kept, feed_got), low_b)

    def half_of(rows, sent):
        cut = rows.shape[-2] // 2
        upper = (lax.axis_index("dp") & 1) != 0
        first, second = rows[..., :cut, :], rows[..., cut:, :]
        return jnp.where(upper, first, second) if sent else jnp.where(upper, second, first)

    in_y = added(feed_kept[1, :D], feed_got[1, :D]).astype(bf16)
    out_x = added(half_of(feed_kept[:, D:], True), half_of(feed_got[:, D:], True)).astype(bf16)
    in_y_got, out_x_got = partner(in_y, 2), partner_dp(out_x, 1)
    operands, blocks = laid(
        [spots, cq_a, ck_a, cv_a, co_a, clse_a, g_cross_a, ids, s1, tie(low_b, in_y, out_x, out_got), g2],
        (parts, 0, cross_all), [z1, norm_gain, o_a, o_b], (parts, 3, self_all), [sums_b, sums],
    )
    gkv_sent, gkv_kept, part_a, g1, g_self_a, g_self_b, self_out_t, sums_a, sums = kernel_call(
        cross_back_norm,
        "cross_back_norm",
        [
            *kv_shapes, shape(full, f32), shape(half, bf16), shape(half, bf16), shape((4, D, PAIR), bf16),
            shape((8, D), f32), sums_shape,
        ],
        operands,
        scratch=[pltpu.VMEM(half, f32)],
        blocks=blocks,
    )
    gkv_got = partner(gkv_sent, 1)
    in_y_got, out_x_got, feed_kept, feed_got = tie((in_y_got, out_x_got, feed_kept, feed_got), g1)
    in_x = added(half_of(feed_kept[0, :D], True), half_of(feed_got[0, :D], True), half_of(in_y_got, True)).astype(bf16)
    out_y = added(half_of(feed_kept[1, D:], False), half_of(feed_got[1, D:], False), out_x_got[1]).astype(bf16)
    in_x_got, out_y_got = partner_dp(in_x, 1), partner(out_y, 2)
    cb_kept, cb_sent, enc_acc = finished(
        2, "start", gkv_kept_b, gkv_got_b, tie(e_own, g1, in_x, out_y), cross_far, part_b, [cross_out_t, self_out_t], sums
    )
    cb_got = partner(cb_sent, 1)

    gkv_sent_b, gkv_kept_b, part_b, low_b, sums_b = back_far(
        0, [q_b, k_b, v_b, o_b, lse_b], g_self_b, tie(x_own, enc_acc)
    )
    gkv_got_b = partner(gkv_sent_b, 1)
    cb_kept, cb_got, in_x_got, out_y_got = tie((cb_kept, cb_got, in_x_got, out_y_got), low_b)
    cross_b = added(cb_kept, cb_got).astype(bf16)
    cut = cross_b.shape[0] // 2
    cross_y = [partner(cross_b[:cut], 2), partner(cross_b[cut:], 2)]
    feed_total = jnp.stack(
        [
            added(half_of(feed_kept[0, :D], False), half_of(feed_got[0, :D], False), half_of(in_y_got, False), in_x_got),
            added(half_of(feed_kept[0, D:], False), half_of(feed_got[0, D:], False), out_x_got[0], out_y_got),
        ]
    )
    feed_sum = DpSum(feed_total, dp_bits()[1:])
    ca_kept, ca_sent, enc_kept, enc_sent = finished(
        0, "last", gkv_kept, gkv_got, tie(e_own, cross_b, feed_sum.value), cross_near, part_a,
        [cross_out_t, self_out_t], sums, enc_acc,
    )
    ca_got = partner(ca_sent, 1)
    sb_kept, sb_sent, acc = finished(
        2, "middle", gkv_kept_b, gkv_got_b, tie(x_own, enc_kept, cross_y[0]), self_far, part_b, [], sums_b, g1
    )
    sb_got = partner(sb_sent, 1)
    feed_sum.step(acc)
    self_b = added(sb_kept, sb_got).astype(bf16)
    self_y = partner(self_b, 2)
    cross_y, ca_kept, ca_got = tie((cross_y, ca_kept, ca_got), self_b, feed_sum.value)
    cross_sum = DpSum(added(ca_kept, ca_got, jnp.concatenate(cross_y, axis=0)), dp_bits())
    operands, blocks = laid(
        [q_a, k_a, v_a, o_a, lse_a, g_self_a, ids, x_own, tie(low_b, self_b, feed_sum.value, cross_sum.value), acc],
        (parts, 0, self_all),
    )
    gkv_sent, gkv_kept, part_a, acc, sums_a = kernel_call(
        self_back,
        "self_back",
        [*kv_shapes, shape(full, f32), shape((8, D), f32)],
        operands,
        smem=0,
        scratch=[pltpu.VMEM(half, f32)],
        blocks=blocks,
    )
    gkv_got = partner(gkv_sent, 1)
    feed_sum.step(acc)
    cross_sum.step(acc)
    sa_kept, sa_sent, in_kept, in_sent = finished(
        0, "last", gkv_kept, gkv_got, tie(x_own, feed_sum.value, cross_sum.value), self_near, part_a, [], sums_a, acc
    )
    sa_got = partner(sa_sent, 1)
    feed_sum.step(in_kept)
    cross_sum.step(in_kept)
    self_y = tie(self_y, in_kept)
    self_sum = DpSum(added(sa_kept, sa_got, self_y), dp_bits())
    enc_sent, in_sent = tie((enc_sent, in_sent), self_sum.value)
    enc_got, in_got = partner(enc_sent, 2), partner(in_sent, 2)

    def to_owner(kept, other):
        other = other.astype(kept.dtype)
        return jnp.stack([jnp.where(first, kept, other), jnp.where(first, other, kept)])

    def in_grad(total):
        return total[: 3 * D].reshape(3, D, width).astype(f32)

    def out_grad(total):
        blocks = [total[c * width : (c + 1) * width] for c in range(D // width)]
        return jnp.concatenate(blocks, axis=1).astype(f32)

    cross_sum.step(self_sum.value)
    feed_total = feed_sum.finish(cross_sum.value)
    self_sum.step()
    layer_output = to_owner(out_kept, tie(out_got, self_sum.value))
    feed_total = tie(feed_total, self_sum.value)
    feed_in_grad, feed_out_grad = feed_total[0].astype(f32), feed_total[1].astype(f32)
    cross_sum.step(self_sum.value, feed_in_grad)
    self_sum.step(layer_output, feed_out_grad)
    encoder_grad = to_owner(enc_kept, tie(enc_got, self_sum.value))
    self_sum.step(encoder_grad)
    input_grad = to_owner(in_kept, tie(in_got, self_sum.value))
    cross_total = cross_sum.finish(self_sum.value)
    self_sum.step(cross_total, input_grad)
    cross_total = tie(cross_total, self_sum.value)
    cross_in_grad, cross_out_grad = in_grad(cross_total), out_grad(cross_total[3 * D : 4 * D])
    self_out_grad = out_grad(cross_total[4 * D : 5 * D])
    common = cross_total[5 * D : 5 * D + 64].astype(f32).reshape(4, 16, PAIR).swapaxes(0, 1).reshape(16, 4 * PAIR)
    shard_sums = cross_total[5 * D + 64 : 5 * D + 72].astype(f32)
    rms_values = jnp.sqrt(jnp.sum(common[0:4], axis=1) / (jnp.sum(common[13]) * D))
    self_total = self_sum.finish(cross_in_grad, cross_out_grad, self_out_grad, common, shard_sums, rms_values)

    return (
        layer_output,
        input_grad,
        encoder_grad,
        in_grad(self_total),
        self_total[3 * D : 3 * D + 2].astype(f32),
        self_out_grad,
        cross_in_grad,
        shard_sums[0:2],
        cross_out_grad,
        feed_in_grad,
        shard_sums[2:6].reshape(units),
        feed_out_grad,
        jnp.stack([common[12], common[9], common[6]]),
        jnp.stack([common[10], common[7], common[4]]),
        jnp.stack([common[11], common[8], common[5]]),
        rms_values,
    )


def solution(mesh):
    return jax.shard_map(
        per_device,
        mesh=mesh,
        in_specs=(
            P("dp", None, None),
            P("dp", None, None),
            P("dp", None),
            P("dp", None),
            P("dp", "tensor"),
            P("dp", "tensor", None),
            P(None, None, "tensor"),
            P(None, "tensor"),
            P("tensor", None),
            P(None, None, "tensor"),
            P(None, "tensor"),
            P("tensor", None),
            P(None, "tensor"),
            P("tensor"),
            P("tensor", None),
            P(),
            P(),
            P(),
        ),
        out_specs=(
            P("dp", "tensor", None),
            P("dp", "tensor", None),
            P("dp", "tensor", None),
            P(None, None, "tensor"),
            P(None, "tensor"),
            P("tensor", None),
            P(None, None, "tensor"),
            P(None, "tensor"),
            P("tensor", None),
            P(None, "tensor"),
            P("tensor"),
            P("tensor", None),
            P(),
            P(),
            P(),
            P(),
        ),
        check_vma=False,
    )
```

```python
import jax
import jax.numpy as jnp
from jax import lax
from jax.experimental import pallas as pl
from jax.experimental.pallas import tpu as pltpu
from jax.sharding import PartitionSpec as P

D = 512
HEAD = 64
EPSILON = 1e-05
PAIR = 2 * HEAD
FAR = 2.0**100
SCALE = HEAD ** (-0.5)
bf16, f32 = jnp.bfloat16, jnp.float32


def partner(array_in, bit):
    count = lax.axis_size("tensor")
    return lax.ppermute(array_in, "tensor", [(i, i ^ bit) for i in range(count)])


def partner_dp(array_in, bit):
    count = lax.axis_size("dp")
    return lax.ppermute(array_in, "dp", [(i, i ^ bit) for i in range(count)])


def tie(value, *others):
    return lax.optimization_barrier((value, others))[0]


def dp_bits():
    bits = []
    bit = 1
    while bit < lax.axis_size("dp"):
        bits.append(bit)
        bit *= 2
    return bits


def halves(total, bit):
    upper = (lax.axis_index("dp") & bit) != 0
    half = total.shape[-2] // 2
    first, second = total[..., :half, :], total[..., half:, :]
    return jnp.where(upper, second, first), jnp.where(upper, first, second).astype(bf16)


def in_order(mine, other, bit):
    upper = (lax.axis_index("dp") & bit) != 0
    return jnp.concatenate([jnp.where(upper, other, mine), jnp.where(upper, mine, other)], axis=-2)


def half_here(rows, bit):
    half = rows.shape[0] // 2
    upper = (lax.axis_index("dp") & bit) != 0
    return jnp.where(upper, rows[half:], rows[:half])


class DpSum:
    def __init__(self, total, bits):
        self.todo = [("half", bit) for bit in bits[:-1]] + [("swap", bits[-1])]
        self.todo += [("double", bit) for bit in reversed(dp_bits()[:-1])]
        self.value = total
        self.start()

    def start(self):
        kind, bit = self.todo[0]
        if kind == "half":
            self.kept, self.value = halves(self.value, bit)
        else:
            self.kept = self.value = self.value.astype(bf16)
        self.got = partner_dp(self.value, bit)

    def step(self, *after):
        if self.todo:
            if after:
                self.kept, self.got = tie((self.kept, self.got), *after)
            kind, bit = self.todo.pop(0)
            if kind == "double":
                self.value = in_order(self.kept, self.got, bit)
            else:
                self.value = self.kept.astype(f32) + self.got.astype(f32)
            if self.todo:
                self.start()
        return self.value

    def finish(self, *after):
        while self.todo:
            self.step(*after)
        return self.value


def dot_nn(a, b):
    return lax.dot_general(a, b, (((1,), (0,)), ((), ())), preferred_element_type=f32)


def dot_nt(a, b):
    return lax.dot_general(a, b, (((1,), (1,)), ((), ())), preferred_element_type=f32)


def dot_tn(a, b):
    return lax.dot_general(a, b, (((0,), (0,)), ((), ())), preferred_element_type=f32)


def lane_in_head(count):
    return lax.broadcasted_iota(jnp.int32, (count, PAIR), 1) & (HEAD - 1)


def lane_low(count):
    return lax.broadcasted_iota(jnp.int32, (count, PAIR), 1) < HEAD


def as_columns(row):
    return jnp.broadcast_to(row.astype(f32), (PAIR, row.shape[1])).T


def minus_pieces(column, lane):
    high = column.astype(bf16).astype(f32)
    rest = column - high
    middle = rest.astype(bf16).astype(f32)
    low = rest - middle
    return jnp.where(lane == 4, -high, jnp.where(lane == 5, -middle, jnp.where(lane == 6, -low, 0.0)))


def query_extra(ids):
    lane = lane_in_head(ids.shape[0])
    return jnp.where((lane < 4) & (lane.astype(f32) != ids), -FAR, 0.0)


def key_extra(ids):
    lane = lane_in_head(ids.shape[0])
    ones = (lane >= 4) & (lane < 7)
    return jnp.where((lane.astype(f32) == ids) | ones, 1.0, 0.0).astype(bf16)


def attend(pairs, q_ref, k_ref, v_ref, q_extra, k_extra, o_ref, lse_ref):
    n_q, n_k = q_ref.shape[0], k_ref.shape[0]
    low_q, low_k = lane_low(n_q), lane_low(n_k)
    lane = lax.broadcasted_iota(jnp.int32, (n_q, PAIR), 1)
    extra = q_extra.astype(bf16)
    lse_all = jnp.zeros((n_q, PAIR), f32)
    for i in range(pairs):
        c = slice(i * PAIR, (i + 1) * PAIR)
        q2, k2, v2 = q_ref[:, c] * bf16(SCALE), k_ref[:, c], v_ref[:, c]
        scores = [
            dot_nt(jnp.where(low_q, q2, extra), jnp.where(low_k, k2, k_extra)),
            dot_nt(jnp.where(low_q, extra, q2), jnp.where(low_k, k_extra, k2)),
        ]
        outs = []
        for h in range(2):
            top = jnp.max(scores[h], axis=1, keepdims=True)
            terms = jnp.exp(scores[h] - top)
            total = jnp.sum(terms, axis=1, keepdims=True)
            outs.append(dot_nn(terms.astype(bf16), v2) * (1.0 / total))
            lse_all = jnp.where(lane == 2 * i + h, top + jnp.log(total), lse_all)
        o_ref[:, c] = jnp.where(low_q, outs[0], outs[1]).astype(bf16)
    lse_ref[...] = lse_all


def attend_back(pairs, base, q_ref, k_ref, v_ref, o_ref, g_ref, lse_ref, q_extra, k_extra, gq_ref, store):
    n_q, n_k = q_ref.shape[0], k_ref.shape[0]
    low_q, low_k = lane_low(n_q), lane_low(n_k)
    lane = lax.broadcasted_iota(jnp.int32, (n_q, PAIR), 1)
    head_lane = lane_in_head(n_q)
    key_lane = lane_in_head(n_k)
    v_extra = jnp.where((key_lane >= 4) & (key_lane < 7), 1.0, 0.0).astype(bf16)
    nothing = jnp.zeros((n_q, PAIR), bf16)
    lse_all = lse_ref[...]
    for i in range(pairs):
        c = slice(i * PAIR, (i + 1) * PAIR)
        q2, k2, v2, g2 = q_ref[:, c] * bf16(SCALE), k_ref[:, c], v_ref[:, c], g_ref[:, c]
        product = g2.astype(f32) * o_ref[:, c].astype(f32)
        gk, gv, gq = [], [], []
        for h in range(2):
            own_q = low_q if h == 0 else ~low_q
            own_k = low_k if h == 0 else ~low_k
            dots = jnp.sum(jnp.where(own_q, product, 0.0), axis=1, keepdims=True)
            lse = jnp.sum(jnp.where(lane == base + 2 * i + h, lse_all, 0.0), axis=1, keepdims=True)
            q_more = jnp.where(own_q, q2, (q_extra + minus_pieces(lse, head_lane)).astype(bf16))
            g_more = jnp.where(own_q, g2, minus_pieces(dots, head_lane).astype(bf16))
            probs = jnp.exp(dot_nt(jnp.where(own_k, k2, k_extra), q_more))
            g_scores = (probs * dot_nt(jnp.where(own_k, v2, v_extra), g_more)).astype(bf16)
            gv.append(dot_nn(probs.astype(bf16), jnp.where(own_q, g2, nothing)))
            gk.append(dot_nn(g_scores, jnp.where(own_q, q2, nothing)))
            gq.append(dot_tn(g_scores, k2))
        store(i, gk[0] + gk[1], gv[0] + gv[1])
        gq_ref[:, c] = jnp.where(low_q, gq[0], gq[1]) * SCALE


def normed(z):
    centred = z - jnp.mean(z, axis=-1, keepdims=True)
    r = lax.rsqrt(jnp.mean(centred * centred, axis=-1, keepdims=True) + EPSILON)
    return centred * r, r


def norm_back(z, gain, upstream):
    xhat, r = normed(z)
    inner = gain * upstream
    grad = r * (
        inner
        - jnp.mean(inner, axis=-1, keepdims=True)
        - xhat * jnp.mean(inner * xhat, axis=-1, keepdims=True)
    )
    return grad, column_sum(upstream * xhat), column_sum(upstream)


def column_sum(array_in):
    return jnp.sum(array_in, axis=0, keepdims=True)


def lanes(refs):
    return jnp.concatenate([r[...] for r in refs], axis=1)


def bias_row(packs, index):
    rows = [
        sum(p[8 * n + index : 8 * n + index + 1, :].astype(f32) for n in (0, 1, 2)) for p in packs
    ]
    return jnp.concatenate(rows, axis=1)


def mask_column(own_pack, across_pack):
    first = 24
    row = jnp.concatenate([p[first + i : first + i + 1, :] for p, i in ((own_pack, 2), (own_pack, 3), (across_pack, 0), (across_pack, 1))], axis=1)
    return as_columns(row)[:, 0:1], row.astype(f32)


def stacked(refs):
    return jnp.concatenate([r[...] for r in refs], axis=0)


def sequence_rows(spots, ref, blocks):
    size = ref.shape[1] // 4
    return jnp.concatenate(
        [ref[0, pl.ds(pl.multiple_of(spots[1 + j] * size, size), size), :] for j in range(blocks)], axis=0
    )


def kernel_call(body, name, out_shape, operands, smem=1, scratch=(), blocks=(), us=5, limit=36):
    blocks = dict(blocks)

    def spec(dims, place):
        return pl.BlockSpec(dims, lambda step, *scalars: place(*scalars))

    def whole(dims):
        return spec(dims, lambda *scalars: (0,) * len(dims))

    return pl.pallas_call(
        lambda *refs: body(*refs),
        name=name,
        out_shape=out_shape,
        grid_spec=pltpu.PrefetchScalarGridSpec(
            num_scalar_prefetch=smem,
            grid=(1,),
            in_specs=[spec(*blocks[i]) if i in blocks else whole(operands[i].shape) for i in range(smem, len(operands))],
            out_specs=[whole(o.shape) for o in out_shape],
            scratch_shapes=scratch,
        ),
        compiler_params=pltpu.CompilerParams(vmem_limit_bytes=limit * 2**20),
        cost_estimate=pl.CostEstimate(flops=int(us * 1e9), bytes_accessed=1000, transcendentals=0),
    )(*operands)


def pack_part(index):
    return ((D, PAIR), lambda *scalars: (index, 0))


PACK_TAIL = ((32, PAIR), lambda *scalars: (4 * D // 32, 0))


def of_sequence(array):
    return ((1, *array.shape[1:]), lambda spots: (spots[0],) + (0,) * (array.ndim - 1))


def shape(dims, dtype):
    return jax.ShapeDtypeStruct(dims, dtype)


def self_forward(spots, x, q_w, q_x, k_w, k_x, v_w, v_x, t_w, t_x, ids, q_ref, k_ref, v_ref, o_ref, lse_ref):
    rows = sequence_rows(spots, x, 4)
    own = q_ref.shape[0]
    q_ref[...] = (dot_nn(rows[:own], lanes([q_w, q_x])) + bias_row([t_w, t_x], 0)).astype(bf16)
    k_ref[...] = dot_nn(rows, lanes([k_w, k_x])).astype(bf16)
    v_ref[...] = (dot_nn(rows, lanes([v_w, v_x])) + bias_row([t_w, t_x], 1)).astype(bf16)
    columns = as_columns(ids[0:1, :])
    attend(2, q_ref, k_ref, v_ref, query_extra(columns[:own]), key_extra(columns), o_ref, lse_ref)


def out_rows(shards):
    blocks = D // PAIR
    return jnp.concatenate(
        [
            jnp.concatenate([s[j * PAIR : (j + 1) * PAIR, :] for j in range(blocks)], axis=1)
            for s in shards
        ],
        axis=0,
    )


def cross_heads(stream, rows, weights, tails, ids, q_ref, k_ref, v_ref, o_ref, lse_ref):
    own = q_ref.shape[0]
    q_ref[...] = (dot_nn(stream, lanes(weights[0:2])) + bias_row(tails, 2)).astype(bf16)
    k_ref[...] = dot_nn(rows, lanes(weights[2:4])).astype(bf16)
    v_ref[...] = (dot_nn(rows, lanes(weights[4:6])) + bias_row(tails, 3)).astype(bf16)
    queries = query_extra(as_columns(ids[0:1, :own]))
    attend(2, q_ref, k_ref, v_ref, queries, key_extra(as_columns(ids[1:2, :])), o_ref, lse_ref)


def cross_first(
    spots, o_a, o_b, so0, so1, so2, so3, x, e, q_w, q_x, k_w, k_x, v_w, v_x, t0, t1, t2, ids, out_bias, gain, shift,
    s1_ref, z1_ref, q_ref, k_ref, v_ref, o_ref, lse_ref, sums_ref, xo_ref, eo_ref,
):
    own = q_ref.shape[0]
    valid, valid_row = mask_column(t0, t2)
    branch = dot_nn(lanes([o_a, o_b]), out_rows([so0, so1, so2, so3])) + out_bias[0:1, :]
    sums_ref[...] = jnp.zeros_like(sums_ref)
    sums_ref[0:1, :] = column_sum(valid * branch * branch)
    sums_ref[13:14, :] = valid_row
    x_own = sequence_rows(spots, x, 2)
    xo_ref[...] = x_own
    z = x_own.astype(f32) + branch
    z1_ref[...] = z
    stream = (normed(z)[0] * gain[0:1, :] + shift[0:1, :]).astype(bf16)
    s1_ref[...] = stream
    rows = sequence_rows(spots, e, 4)
    eo_ref[...] = rows[:own]
    cross_heads(stream, rows, [q_w, q_x, k_w, k_x, v_w, v_x], [t0, t1], ids, q_ref, k_ref, v_ref, o_ref, lse_ref)


def cross_second(
    spots, s1, o_a, e, q_w, q_x, k_w, k_x, v_w, v_x, co0, co1, co2, co3, t0, t2, t3, ids, out_bias, gain, shift, sums,
    q_ref, k_ref, v_ref, o_ref, lse_ref, s2_ref, z2_ref, sums_ref,
):
    stream = s1[...]
    valid = mask_column(t0, t2)[0]
    rows = sequence_rows(spots, e, 4)
    cross_heads(stream, rows, [q_w, q_x, k_w, k_x, v_w, v_x], [t2, t3], ids, q_ref, k_ref, v_ref, o_ref, lse_ref)
    branch = dot_nn(lanes([o_a, o_ref]), out_rows([co0, co1, co2, co3])) + out_bias[1:2, :]
    sums_ref[...] = sums[...]
    sums_ref[1:2, :] = column_sum(valid * branch * branch)
    z = stream.astype(f32) + branch
    z2_ref[...] = z
    s2_ref[...] = (normed(z)[0] * gain[1:2, :] + shift[1:2, :]).astype(bf16)


def feed(
    spots, s2, z2, fi0, fi1, fi2, fi3, fo0, fo1, fo2, fo3, b0, b1, b2, b3, out_bias, gain, shift, cot, cot_other,
    co0, co1, co2, co3, o_a, o_b, sums,
    kept_out, sent_out, sent_parts, kept_parts, g2_ref, gc_a, gc_b, out_t, sums_ref,
    slope, hidden,
):
    curve = (2.0 / 3.141592653589793) ** 0.5
    stream = s2[...]
    rows, width = stream.shape[0], fi0.shape[1]
    valid = mask_column(b0, b2)[0]
    sums_ref[...] = sums[...]
    branch = jnp.zeros((rows, D), f32) + out_bias[2:3, :]
    ins, outs, offsets = [fi0, fi1, fi2, fi3], [fo0, fo1, fo2, fo3], [b0, b1, b2, b3]
    for j in range(4):
        offset = jnp.concatenate([bias_row([offsets[j]], 4 + n) for n in range(width // PAIR)], axis=1)
        pre = dot_nn(stream, ins[j][...]) + offset
        square = pre * pre
        bend = jnp.tanh(curve * pre * (1.0 + 0.044715 * square))
        half = 0.5 * (1.0 + bend)
        slope[j] = half + 0.5 * pre * (1.0 - bend * bend) * (curve * (1.0 + 3.0 * 0.044715 * square))
        units = (pre * half).astype(bf16)
        hidden[j] = units
        branch = branch + dot_nn(units, outs[j][...])
    z = stream.astype(f32) + branch
    final = normed(z)[0] * gain[2:3, :] + shift[2:3, :]
    low = final.astype(bf16)
    kept_out[...] = low[: rows // 2]
    sent_out[...] = low[rows // 2 :]
    sums_ref[2:3, :] = column_sum(valid * branch * branch)
    sums_ref[3:4, :] = column_sum(valid * final * final)
    upstream = jnp.concatenate([cot[0], cot_other[...].astype(f32)], axis=0) * valid
    g3, row_gain, row_shift = norm_back(z, gain[2:3, :], upstream)
    sums_ref[4:5, :] = row_gain
    sums_ref[5:6, :] = row_shift
    sums_ref[6:7, :] = column_sum(g3)
    g_low = g3.astype(bf16)
    up = g3
    for j in range(4):
        g_pre = dot_nt(g_low, outs[j][...]) * slope[j]
        store_shard_row(sums_ref, j, 1, column_sum(g_pre))
        pre_low = g_pre.astype(bf16)
        up = up + dot_nt(pre_low, ins[j][...])
        to = sent_parts if j % 2 else kept_parts
        to[j // 2, 0:D, :] = dot_tn(stream, pre_low).astype(bf16)
        to[j // 2, D : D + width, :] = dot_tn(hidden[j], g_low).astype(bf16)
    g2, row_gain, row_shift = norm_back(z2[...], gain[1:2, :], up)
    sums_ref[7:8, :] = row_gain
    sums_ref[8:9, :] = row_shift
    sums_ref[9:10, :] = column_sum(g2)
    g2_ref[...] = g2
    g_low = g2.astype(bf16)
    g_cross = dot_nt(g_low, out_rows([co0, co1, co2, co3])).astype(bf16)
    gc_a[...] = g_cross[:, : 2 * PAIR]
    gc_b[...] = g_cross[:, 2 * PAIR :]
    store_blocks(out_t, dot_tn(lanes([o_a, o_b]), g_low))


def store_shard_row(sums_ref, j, row, value):
    sums_ref[16 + 2 * j + row : 17 + 2 * j + row, : value.shape[1]] = value


def store_chunks(to, part):
    for j in range(to.shape[0]):
        to[j] = part[:, j * PAIR : (j + 1) * PAIR].astype(bf16)


def store_blocks(to, part):
    for j in range(4):
        for c in range(D // PAIR):
            block = part[j * PAIR : (j + 1) * PAIR, c * PAIR : (c + 1) * PAIR]
            to[j, c * PAIR : (c + 1) * PAIR, :] = block.astype(bf16)


def kv_store(sent_ref, kept_ref, sums_ref):
    own, width = kept_ref.shape[0], kept_ref.shape[1] // 2

    def store(i, gk, gv):
        here = i * PAIR
        there = (i ^ 1) * PAIR
        kept_ref[:, here : here + PAIR] = gk[:own]
        kept_ref[:, width + here : width + here + PAIR] = gv[:own]
        sent_ref[:, there : there + PAIR] = gk[own:].astype(bf16)
        sent_ref[:, width + there : width + there + PAIR] = gv[own:].astype(bf16)
        sums_ref[1:2, here : here + PAIR] = column_sum(gv)

    return store


def half_back(source, q, k, v, o, lse, g, ids, rows, sent_ref, kept_ref, part_q, sums_ref, gq_ref):
    own = q.shape[0]
    sums_ref[...] = jnp.zeros_like(sums_ref)
    queries = query_extra(as_columns(ids[0:1, :own]))
    keys = key_extra(as_columns(ids[source : source + 1, :]))
    store = kv_store(sent_ref, kept_ref, sums_ref)
    attend_back(2, 0, q, k, v, o, g, lse, queries, keys, gq_ref, store)
    gq = gq_ref[...]
    sums_ref[0:1, : 2 * PAIR] = column_sum(gq)
    low = gq.astype(bf16)
    store_chunks(part_q, dot_tn(rows[...], low))
    return low


def far_back(source, q, k, v, o, lse, g, ids, rows, sent, kept, part_q, low_ref, sums, gq_ref):
    low_ref[...] = half_back(source, q, k, v, o, lse, g, ids, rows, sent, kept, part_q, sums, gq_ref)


def self_back(
    q, k, v, o, lse, g, ids, rows, low_b, acc, w0, w1, w2, w3, sent, kept, part_q, acc_ref, sums, gq_ref
):
    low = half_back(0, q, k, v, o, lse, g, ids, rows, sent, kept, part_q, sums, gq_ref)
    acc_ref[...] = acc[...] + dot_nt(low, lanes([w0, w1])) + dot_nt(low_b[...], lanes([w2, w3]))


def cross_back_norm(
    spots, q, k, v, o, lse, g, ids, rows, low_b, acc, w0, w1, w2, w3, z1, gain, o_a, o_b, so0, so1, so2, so3, sums_b,
    carried,
    sent, kept, part_q, g1_ref, gs_a, gs_b, out_t, sums, all_ref, gq_ref,
):
    low = half_back(1, q, k, v, o, lse, g, ids, rows, sent, kept, part_q, sums, gq_ref)
    up = acc[...] + dot_nt(low, lanes([w0, w1])) + dot_nt(low_b[...], lanes([w2, w3]))
    g1, row_gain, row_shift = norm_back(z1[...], gain[0:1, :], up)
    all_ref[...] = carried[...]
    all_ref[10:11, :] = row_gain
    all_ref[11:12, :] = row_shift
    all_ref[12:13, :] = column_sum(g1)
    for j in range(4):
        c = slice((j % 2) * PAIR, (j % 2 + 1) * PAIR)
        of = sums if j < 2 else sums_b
        store_shard_row(all_ref, j, 0, jnp.concatenate([of[0:1, c], of[1:2, c]], axis=1))
    g1_ref[...] = g1
    g_low = g1.astype(bf16)
    g_self = dot_nt(g_low, out_rows([so0, so1, so2, so3])).astype(bf16)
    gs_a[...] = g_self[:, : 2 * PAIR]
    gs_b[...] = g_self[:, 2 * PAIR :]
    store_blocks(out_t, dot_tn(lanes([o_a, o_b]), g_low))


def finish(first, mode, n_out, *refs):
    kept, other, rows, k_w, k_x, v_w, v_x, part_q, *refs = refs
    along, sums, refs = refs[:n_out], refs[n_out], refs[n_out + 1 :]
    outs = refs if mode == "start" else refs[1:]
    both = (kept[...] + other[...].astype(f32)).astype(bf16)
    gk, gv = both[:, : 2 * PAIR], both[:, 2 * PAIR :]
    res = dot_nt(gk, lanes([k_w, k_x])) + dot_nt(gv, lanes([v_w, v_x]))
    if mode != "start":
        res = res + refs[0][...]
    part = dot_tn(rows[...], both).astype(bf16)
    for j in range(2):
        to = outs[j]
        to[0:D, :] = part_q[j]
        to[D : 2 * D, :] = part[:, j * PAIR : (j + 1) * PAIR]
        to[2 * D : 3 * D, :] = part[:, (2 + j) * PAIR : (3 + j) * PAIR]
        for n in range(n_out):
            to[(3 + n) * D : (4 + n) * D, :] = along[n][j]
        last = (3 + n_out) * D
        to[last:, :] = jnp.zeros((to.shape[0] - last, PAIR), bf16)
        if n_out == 0:
            to[last : last + 2, :] = sums[0:2, j * PAIR : (j + 1) * PAIR].astype(bf16)
        else:
            for c in range(4):
                to[last + 16 * c : last + 16 * (c + 1), :] = sums[0:16, c * PAIR : (c + 1) * PAIR].astype(bf16)
            row = 16 + 2 * (first + j)
            blocks = [(row, 0), (row, 1), (row + 1, 0), (row + 1, 1), (row + 1, 2), (row + 1, 3)]
            shard_rows = jnp.concatenate(
                [sums[r : r + 1, c * PAIR : (c + 1) * PAIR] for r, c in blocks] + [jnp.zeros((2, PAIR), f32)], axis=0
            )
            to[last + 64 : last + 72, :] = shard_rows.astype(bf16)
    if mode == "last":
        half = res.shape[0] // 2
        outs[2][...] = res[:half]
        outs[3][...] = res[half:].astype(bf16)
    else:
        outs[2][...] = res


def own_first(ids, mine, rank):
    row = lax.dynamic_index_in_dim(ids, mine, 0, True)
    size = ids.shape[1] // 4
    parts = [
        lax.dynamic_slice_in_dim(row, (rank ^ step) * size, size, 1) for step in (0, 2, 1, 3)
    ]
    return jnp.concatenate(parts, axis=1)


def per_device(
    decoder_layer_input,
    encoder_state_rows,
    target_segments,
    source_segments,
    valid_mask,
    cotangent,
    self_input_projection,
    self_in_bias,
    self_out_proj,
    cross_input_projection,
    cross_in_bias,
    cross_out_proj,
    feed_in_proj,
    feed_in_bias,
    feed_out_proj,
    out_bias,
    norm_gain,
    norm_bias,
):
    rank = lax.axis_index("tensor")
    mine = rank // 2
    first = mine == 0
    length = decoder_layer_input.shape[1]
    own = length // 2
    width = self_out_proj.shape[0]
    units = feed_in_proj.shape[1]
    spots = jnp.stack([mine, rank, rank ^ 2, rank ^ 1, rank ^ 3]).astype(jnp.int32)

    def attention_weights(in_proj, out_proj, *more):
        blocks = [out_proj[:, j * width : (j + 1) * width] for j in range(D // width)]
        return jnp.concatenate([in_proj.reshape(-1, width), *blocks, *more], axis=0)

    biases = jnp.concatenate([self_in_bias, cross_in_bias, feed_in_bias.reshape(-1, width)], axis=0)
    high = lax.reduce_precision(biases, 8, 7)
    middle = lax.reduce_precision(biases - high, 8, 7)
    low = (biases - high - middle).astype(bf16)
    high, middle = high.astype(bf16), middle.astype(bf16)
    mask_rows = valid_mask.astype(bf16).reshape(2, -1, width)
    mask_kept = jnp.where(first, mask_rows[0], mask_rows[1])
    mask_sent = jnp.where(first, mask_rows[1], mask_rows[0])
    self_shard = attention_weights(
        self_input_projection, self_out_proj, high, middle, low, mask_sent, mask_kept, jnp.zeros((4, width), bf16)
    )
    ids = jnp.concatenate(
        [own_first(target_segments, mine, rank), own_first(source_segments, mine, rank)], axis=0
    )
    self_near = [self_shard, partner(self_shard, 1)]
    self_across = partner(self_shard, 2)

    half_shapes = [
        shape((own, 2 * PAIR), bf16), shape((length, 2 * PAIR), bf16), shape((length, 2 * PAIR), bf16),
        shape((own, 2 * PAIR), bf16), shape((own, PAIR), f32),
    ]
    full = (own, D)
    sums_shape = shape((32, D), f32)

    def parts(index, packs, at):
        return list(packs), {at + i: pack_part(index) for i in range(len(packs))}

    def tails(packs, at):
        return list(packs), {at + i: PACK_TAIL for i in range(len(packs))}

    def laid(operands, *groups):
        blocks = {}
        for group in groups:
            if isinstance(group, tuple):
                more, places = group[0](*group[1:], len(operands))
                operands = operands + more
                blocks.update(places)
            else:
                operands = operands + group
        return operands, blocks

    def sequence(array, at):
        return [array], {at: of_sequence(array)}

    def self_half(shards, x):
        operands, blocks = laid(
            [spots], (sequence, x), (parts, 0, shards), (parts, 1, shards), (parts, 2, shards), (tails, shards), [ids]
        )
        return kernel_call(self_forward, "self_forward", half_shapes, operands, blocks=blocks)

    cross_shard = attention_weights(cross_input_projection, cross_out_proj)
    cross_piece = half_here(cross_shard, 1)
    feed_piece = half_here(feed_in_proj, 1)
    q_a, k_a, v_a, o_a, lse_a = self_half(self_near, tie(decoder_layer_input, cross_piece, feed_piece))
    feed_in_1, feed_out_1, cot_1, cross_piece, feed_piece, cross_shard = tie(
        (feed_in_proj, feed_out_proj, cotangent, cross_piece, feed_piece, cross_shard), q_a
    )
    cot_sent = lax.dynamic_index_in_dim(cot_1, 1 - mine, 0, False).astype(bf16)
    self_far = [self_across, partner(tie(self_across, cot_sent), 1)]
    self_all = self_near + self_far
    cross_got, feed_got = partner(cross_piece, 2), partner(feed_piece, 2)
    q_b, k_b, v_b, o_b, lse_b = self_half(self_far, decoder_layer_input)
    cross_near = [cross_shard, partner(tie(cross_shard, self_across), 1)]
    cross_got, feed_got, cot_sent, feed_in_1, feed_out_1 = tie((cross_got, feed_got, cot_sent, feed_in_1, feed_out_1), q_b)
    cross_got_x, feed_got_x = partner_dp(cross_got, 1), partner_dp(feed_got, 1)
    cut = feed_out_1.shape[0] // 2
    out_top, cot_other = partner(feed_out_1[:cut], 2), partner(cot_sent, 2)
    operands, blocks = laid(
        [spots, o_a, tie(o_b, cross_got, feed_got)], (parts, 3, self_all), (sequence, decoder_layer_input),
        (sequence, encoder_state_rows), (parts, 0, cross_near), (parts, 1, cross_near), (parts, 2, cross_near),
        (tails, self_all[:3]), [ids, out_bias, norm_gain, norm_bias],
    )
    s1, z1, cq_a, ck_a, cv_a, co_a, clse_a, sums, x_own, e_own = kernel_call(
        cross_first,
        "cross_first",
        [shape(full, bf16), shape(full, f32), *half_shapes, sums_shape, shape(full, bf16), shape(full, bf16)],
        operands,
        blocks=blocks,
    )
    cross_got, cross_got_x, feed_got, feed_got_x, out_top, cot_other, feed_in_1, feed_out_1 = tie(
        (cross_got, cross_got_x, feed_got, feed_got_x, out_top, cot_other, feed_in_1, feed_out_1), s1
    )
    cross_across = in_order(cross_got, cross_got_x, 1)
    cross_far = [cross_across, partner(cross_across, 1)]
    cross_all = cross_near + cross_far
    feed_in_across = in_order(feed_got, feed_got_x, 1)
    out_rest = partner(feed_out_1[cut:], 2)
    feed_in_other, feed_out_other = partner(feed_in_1, 1), partner(feed_out_1, 1)
    operands, blocks = laid(
        [spots, tie(s1, feed_in_across, out_top, cot_other), co_a], (sequence, encoder_state_rows),
        (parts, 0, cross_far), (parts, 1, cross_far), (parts, 2, cross_far), (parts, 3, cross_all),
        (tails, [self_all[0], self_all[2], self_all[3]]), [ids, out_bias, norm_gain, norm_bias, sums],
    )
    cq_b, ck_b, cv_b, co_b, clse_b, s2, z2, sums = kernel_call(
        cross_second,
        "cross_second",
        [*half_shapes, shape(full, bf16), shape(full, f32), sums_shape],
        operands,
        blocks=blocks,
    )
    out_top, out_rest = tie((out_top, out_rest), s2)
    feed_out_across = jnp.concatenate([out_top, out_rest], axis=0)
    feed_in_all = [feed_in_1, feed_in_other, feed_in_across, partner(feed_in_across, 1)]
    feed_out_all = [feed_out_1, feed_out_other, feed_out_across, partner(feed_out_across, 1)]

    operands, blocks = laid(
        [spots, s2, z2, *feed_in_all, *feed_out_all], (tails, self_all), [out_bias, norm_gain, norm_bias],
        (sequence, cotangent), [cot_other], (parts, 3, cross_all), [co_a, co_b, sums],
    )
    half = (own, 2 * PAIR)
    out_kept, out_sent, feed_sent, feed_kept, g2, g_cross_a, g_cross_b, cross_out_t, sums = kernel_call(
        feed,
        "feed",
        [
            shape((own // 2, D), bf16), shape((own // 2, D), bf16),
            shape((2, D + units, D), bf16), shape((2, D + units, D), bf16),
            shape(full, f32), shape(half, bf16), shape(half, bf16), shape((4, D, PAIR), bf16), sums_shape,
        ],
        operands,
        scratch=[pltpu.VMEM((4, own, units), f32), pltpu.VMEM((4, own, units), bf16)],
        blocks=blocks,
    )
    feed_got = partner(feed_sent, 1)
    out_got = partner(out_sent, 2)

    kv_shapes = [shape(full, bf16), shape(full, f32), shape((2, D, PAIR), bf16)]

    def back_far(source, heads, g, rows):
        return kernel_call(
            lambda *refs: far_back(source, *refs),
            "attention_back",
            [*kv_shapes, shape(half, bf16), shape((8, D), f32)],
            [*heads, g, ids, rows],
            smem=0,
            scratch=[pltpu.VMEM(half, f32)],
        )

    def finished(first_pair, mode, kept, got, rows, shards, part, along, small, acc=None):
        n_out = len(along)
        last = [shape((own // 2, D), f32), shape((own // 2, D), bf16)] if mode == "last" else [shape(full, f32)]
        count = (3 + n_out) * D + (96 if n_out else 64)
        operands, blocks = laid([kept, got, rows], (parts, 1, shards), (parts, 2, shards), [part])
        if n_out:
            blocks.update(
                {len(operands) + n: ((2, D, PAIR), lambda *scalars: (first_pair // 2, 0, 0)) for n in range(n_out)}
            )
        return kernel_call(
            lambda *refs: finish(first_pair, mode, n_out, *refs),
            "finish",
            [shape((count, width), bf16), shape((count, width), bf16), *last],
            operands + list(along) + [small] + ([] if acc is None else [acc]),
            smem=0,
            blocks=blocks,
            us=2,
        )

    def added(*parts):
        total = parts[0].astype(f32)
        for part in parts[1:]:
            total = total + part.astype(f32)
        return total

    gkv_sent_b, gkv_kept_b, part_b, low_b, sums_b = back_far(1, [cq_b, ck_b, cv_b, co_b, clse_b], g_cross_b, s1)
    gkv_got_b = partner(gkv_sent_b, 1)
    feed_kept, feed_got = tie((feed_kept, feed_got), low_b)

    def half_of(rows, sent):
        cut = rows.shape[-2] // 2
        upper = (lax.axis_index("dp") & 1) != 0
        first, second = rows[..., :cut, :], rows[..., cut:, :]
        return jnp.where(upper, first, second) if sent else jnp.where(upper, second, first)

    in_y = added(feed_kept[1, :D], feed_got[1, :D]).astype(bf16)
    out_x = added(half_of(feed_kept[:, D:], True), half_of(feed_got[:, D:], True)).astype(bf16)
    in_y_got, out_x_got = partner(in_y, 2), partner_dp(out_x, 1)
    operands, blocks = laid(
        [spots, cq_a, ck_a, cv_a, co_a, clse_a, g_cross_a, ids, s1, tie(low_b, in_y, out_x, out_got), g2],
        (parts, 0, cross_all), [z1, norm_gain, o_a, o_b], (parts, 3, self_all), [sums_b, sums],
    )
    gkv_sent, gkv_kept, part_a, g1, g_self_a, g_self_b, self_out_t, sums_a, sums = kernel_call(
        cross_back_norm,
        "cross_back_norm",
        [
            *kv_shapes, shape(full, f32), shape(half, bf16), shape(half, bf16), shape((4, D, PAIR), bf16),
            shape((8, D), f32), sums_shape,
        ],
        operands,
        scratch=[pltpu.VMEM(half, f32)],
        blocks=blocks,
    )
    gkv_got = partner(gkv_sent, 1)
    cb_kept, cb_sent, enc_acc = finished(
        2, "start", gkv_kept_b, gkv_got_b, tie(e_own, g1), cross_far, part_b, [cross_out_t, self_out_t], sums
    )
    cb_got = partner(cb_sent, 1)
    in_y_got, out_x_got, feed_kept, feed_got = tie((in_y_got, out_x_got, feed_kept, feed_got), enc_acc)
    in_x = added(half_of(feed_kept[0, :D], True), half_of(feed_got[0, :D], True), half_of(in_y_got, True)).astype(bf16)
    out_y = added(half_of(feed_kept[1, D:], False), half_of(feed_got[1, D:], False), out_x_got[1]).astype(bf16)
    in_x_got, out_y_got = partner_dp(in_x, 1), partner(out_y, 2)
    cb_kept, cb_got = tie((cb_kept, cb_got), in_x, out_y)
    cross_b = added(cb_kept, cb_got).astype(bf16)
    cut = cross_b.shape[0] // 2
    cross_y = [partner(cross_b[:cut], 2), None]

    gkv_sent_b, gkv_kept_b, part_b, low_b, sums_b = back_far(
        0, [q_b, k_b, v_b, o_b, lse_b], g_self_b, tie(x_own, enc_acc, in_x, out_y, cross_b)
    )
    gkv_got_b = partner(gkv_sent_b, 1)
    in_x_got, out_y_got, cross_y[0] = tie((in_x_got, out_y_got, cross_y[0]), low_b)
    cross_y[1] = partner(tie(cross_b[cut:], cross_y[0]), 2)
    feed_total = jnp.stack(
        [
            added(half_of(feed_kept[0, :D], False), half_of(feed_got[0, :D], False), half_of(in_y_got, False), in_x_got),
            added(half_of(feed_kept[0, D:], False), half_of(feed_got[0, D:], False), out_x_got[0], out_y_got),
        ]
    )
    feed_sum = DpSum(feed_total, dp_bits()[1:])
    ca_kept, ca_sent, enc_kept, enc_sent = finished(
        0, "last", gkv_kept, gkv_got, tie(e_own, cross_y[0], feed_sum.value), cross_near, part_a,
        [cross_out_t, self_out_t], sums, enc_acc,
    )
    ca_got = partner(ca_sent, 1)
    sb_kept, sb_sent, acc = finished(
        2, "middle", gkv_kept_b, gkv_got_b, tie(x_own, enc_kept), self_far, part_b, [], sums_b, g1
    )
    sb_got = partner(sb_sent, 1)
    feed_sum.step(acc)
    self_b = added(sb_kept, sb_got).astype(bf16)
    self_y = partner(self_b, 2)
    cross_y, ca_kept, ca_got = tie((cross_y, ca_kept, ca_got), self_b, feed_sum.value)
    cross_sum = DpSum(added(ca_kept, ca_got, jnp.concatenate(cross_y, axis=0)), dp_bits())
    operands, blocks = laid(
        [q_a, k_a, v_a, o_a, lse_a, g_self_a, ids, x_own, tie(low_b, self_b, feed_sum.value, cross_sum.value), acc],
        (parts, 0, self_all),
    )
    gkv_sent, gkv_kept, part_a, acc, sums_a = kernel_call(
        self_back,
        "self_back",
        [*kv_shapes, shape(full, f32), shape((8, D), f32)],
        operands,
        smem=0,
        scratch=[pltpu.VMEM(half, f32)],
        blocks=blocks,
    )
    gkv_got = partner(gkv_sent, 1)
    feed_sum.step(acc)
    cross_sum.step(acc)
    sa_kept, sa_sent, in_kept, in_sent = finished(
        0, "last", gkv_kept, gkv_got, tie(x_own, feed_sum.value, cross_sum.value), self_near, part_a, [], sums_a, acc
    )
    sa_got = partner(sa_sent, 1)
    self_y = tie(self_y, in_kept)
    self_sum = DpSum(added(sa_kept, sa_got, self_y), dp_bits())
    enc_sent, in_sent = tie((enc_sent, in_sent), self_sum.value)
    enc_got, in_got = partner(enc_sent, 2), partner(in_sent, 2)

    def to_owner(kept, other):
        other = other.astype(kept.dtype)
        return jnp.stack([jnp.where(first, kept, other), jnp.where(first, other, kept)])

    def in_grad(total):
        return total[: 3 * D].reshape(3, D, width).astype(f32)

    def out_grad(total):
        blocks = [total[c * width : (c + 1) * width] for c in range(D // width)]
        return jnp.concatenate(blocks, axis=1).astype(f32)

    self_sum.step()
    feed_sum.step(self_sum.value)
    cross_sum.step(feed_sum.value)
    self_sum.step()
    cross_sum.step(self_sum.value)
    feed_total = feed_sum.finish(cross_sum.value)
    layer_output = to_owner(out_kept, tie(out_got, self_sum.value))
    feed_total = tie(feed_total, self_sum.value)
    feed_in_grad, feed_out_grad = feed_total[0].astype(f32), feed_total[1].astype(f32)
    encoder_grad = to_owner(enc_kept, tie(enc_got, self_sum.value))
    self_sum.step(layer_output, feed_in_grad)
    cross_sum.step(self_sum.value, encoder_grad, feed_out_grad)
    input_grad = to_owner(in_kept, tie(in_got, self_sum.value))
    cross_total = cross_sum.finish(self_sum.value)
    self_sum.step(cross_total, input_grad)
    cross_total = tie(cross_total, self_sum.value)
    cross_in_grad, cross_out_grad = in_grad(cross_total), out_grad(cross_total[3 * D : 4 * D])
    self_out_grad = out_grad(cross_total[4 * D : 5 * D])
    common = cross_total[5 * D : 5 * D + 64].astype(f32).reshape(4, 16, PAIR).swapaxes(0, 1).reshape(16, 4 * PAIR)
    shard_sums = cross_total[5 * D + 64 : 5 * D + 72].astype(f32)
    rms_values = jnp.sqrt(jnp.sum(common[0:4], axis=1) / (jnp.sum(common[13]) * D))
    self_total = self_sum.finish(cross_in_grad, cross_out_grad, self_out_grad, common, shard_sums, rms_values)

    return (
        layer_output,
        input_grad,
        encoder_grad,
        in_grad(self_total),
        self_total[3 * D : 3 * D + 2].astype(f32),
        self_out_grad,
        cross_in_grad,
        shard_sums[0:2],
        cross_out_grad,
        feed_in_grad,
        shard_sums[2:6].reshape(units),
        feed_out_grad,
        jnp.stack([common[12], common[9], common[6]]),
        jnp.stack([common[10], common[7], common[4]]),
        jnp.stack([common[11], common[8], common[5]]),
        rms_values,
    )


def solution(mesh):
    return jax.shard_map(
        per_device,
        mesh=mesh,
        in_specs=(
            P("dp", None, None),
            P("dp", None, None),
            P("dp", None),
            P("dp", None),
            P("dp", "tensor"),
            P("dp", "tensor", None),
            P(None, None, "tensor"),
            P(None, "tensor"),
            P("tensor", None),
            P(None, None, "tensor"),
            P(None, "tensor"),
            P("tensor", None),
            P(None, "tensor"),
            P("tensor"),
            P("tensor", None),
            P(),
            P(),
            P(),
        ),
        out_specs=(
            P("dp", "tensor", None),
            P("dp", "tensor", None),
            P("dp", "tensor", None),
            P(None, None, "tensor"),
            P(None, "tensor"),
            P("tensor", None),
            P(None, None, "tensor"),
            P(None, "tensor"),
            P("tensor", None),
            P(None, "tensor"),
            P("tensor"),
            P("tensor", None),
            P(),
            P(),
            P(),
            P(),
        ),
        check_vma=False,
    )
```

```python
import jax
import jax.numpy as jnp
from jax import lax
from jax.experimental import pallas as pl
from jax.experimental.pallas import tpu as pltpu
from jax.sharding import PartitionSpec as P

D = 512
HEAD = 64
EPSILON = 1e-05
PAIR = 2 * HEAD
FAR = 2.0**100
SCALE = HEAD ** (-0.5)
bf16, f32 = jnp.bfloat16, jnp.float32


def partner(array_in, bit):
    count = lax.axis_size("tensor")
    return lax.ppermute(array_in, "tensor", [(i, i ^ bit) for i in range(count)])


def partner_dp(array_in, bit):
    count = lax.axis_size("dp")
    return lax.ppermute(array_in, "dp", [(i, i ^ bit) for i in range(count)])


def tie(value, *others):
    return lax.optimization_barrier((value, others))[0]


def dp_bits():
    bits = []
    bit = 1
    while bit < lax.axis_size("dp"):
        bits.append(bit)
        bit *= 2
    return bits


def halves(total, bit):
    upper = (lax.axis_index("dp") & bit) != 0
    half = total.shape[-2] // 2
    first, second = total[..., :half, :], total[..., half:, :]
    return jnp.where(upper, second, first), jnp.where(upper, first, second).astype(bf16)


def in_order(mine, other, bit):
    upper = (lax.axis_index("dp") & bit) != 0
    return jnp.concatenate([jnp.where(upper, other, mine), jnp.where(upper, mine, other)], axis=-2)


def half_here(rows, bit):
    half = rows.shape[0] // 2
    upper = (lax.axis_index("dp") & bit) != 0
    return jnp.where(upper, rows[half:], rows[:half])


class DpSum:
    def __init__(self, total, bits):
        self.todo = [("half", bit) for bit in bits[:-1]] + [("swap", bits[-1])]
        self.todo += [("double", bit) for bit in reversed(dp_bits()[:-1])]
        self.value = total
        self.start()

    def start(self):
        kind, bit = self.todo[0]
        if kind == "half":
            self.kept, self.value = halves(self.value, bit)
        else:
            self.kept = self.value = self.value.astype(bf16)
        self.got = partner_dp(self.value, bit)

    def step(self, *after):
        if self.todo:
            if after:
                self.kept, self.got = tie((self.kept, self.got), *after)
            kind, bit = self.todo.pop(0)
            if kind == "double":
                self.value = in_order(self.kept, self.got, bit)
            else:
                self.value = self.kept.astype(f32) + self.got.astype(f32)
            if self.todo:
                self.start()
        return self.value

    def finish(self, *after):
        while self.todo:
            self.step(*after)
        return self.value


def dot_nn(a, b):
    return lax.dot_general(a, b, (((1,), (0,)), ((), ())), preferred_element_type=f32)


def dot_nt(a, b):
    return lax.dot_general(a, b, (((1,), (1,)), ((), ())), preferred_element_type=f32)


def dot_tn(a, b):
    return lax.dot_general(a, b, (((0,), (0,)), ((), ())), preferred_element_type=f32)


def lane_in_head(count):
    return lax.broadcasted_iota(jnp.int32, (count, PAIR), 1) & (HEAD - 1)


def lane_low(count):
    return lax.broadcasted_iota(jnp.int32, (count, PAIR), 1) < HEAD


def as_columns(row):
    return jnp.broadcast_to(row.astype(f32), (PAIR, row.shape[1])).T


def minus_pieces(column, lane):
    high = column.astype(bf16).astype(f32)
    rest = column - high
    middle = rest.astype(bf16).astype(f32)
    low = rest - middle
    return jnp.where(lane == 4, -high, jnp.where(lane == 5, -middle, jnp.where(lane == 6, -low, 0.0)))


def query_extra(ids):
    lane = lane_in_head(ids.shape[0])
    return jnp.where((lane < 4) & (lane.astype(f32) != ids), -FAR, 0.0)


def key_extra(ids):
    lane = lane_in_head(ids.shape[0])
    ones = (lane >= 4) & (lane < 7)
    return jnp.where((lane.astype(f32) == ids) | ones, 1.0, 0.0).astype(bf16)


def attend(pairs, q_ref, k_ref, v_ref, q_extra, k_extra, o_ref, lse_ref):
    n_q, n_k = q_ref.shape[0], k_ref.shape[0]
    low_q, low_k = lane_low(n_q), lane_low(n_k)
    lane = lax.broadcasted_iota(jnp.int32, (n_q, PAIR), 1)
    extra = q_extra.astype(bf16)
    lse_all = jnp.zeros((n_q, PAIR), f32)
    for i in range(pairs):
        c = slice(i * PAIR, (i + 1) * PAIR)
        q2, k2, v2 = q_ref[:, c] * bf16(SCALE), k_ref[:, c], v_ref[:, c]
        scores = [
            dot_nt(jnp.where(low_q, q2, extra), jnp.where(low_k, k2, k_extra)),
            dot_nt(jnp.where(low_q, extra, q2), jnp.where(low_k, k_extra, k2)),
        ]
        outs = []
        for h in range(2):
            top = jnp.max(scores[h], axis=1, keepdims=True)
            terms = jnp.exp(scores[h] - top)
            total = jnp.sum(terms, axis=1, keepdims=True)
            outs.append(dot_nn(terms.astype(bf16), v2) * (1.0 / total))
            lse_all = jnp.where(lane == 2 * i + h, top + jnp.log(total), lse_all)
        o_ref[:, c] = jnp.where(low_q, outs[0], outs[1]).astype(bf16)
    lse_ref[...] = lse_all


def attend_back(pairs, base, q_ref, k_ref, v_ref, o_ref, g_ref, lse_ref, q_extra, k_extra, gq_ref, store):
    n_q, n_k = q_ref.shape[0], k_ref.shape[0]
    low_q, low_k = lane_low(n_q), lane_low(n_k)
    lane = lax.broadcasted_iota(jnp.int32, (n_q, PAIR), 1)
    head_lane = lane_in_head(n_q)
    key_lane = lane_in_head(n_k)
    v_extra = jnp.where((key_lane >= 4) & (key_lane < 7), 1.0, 0.0).astype(bf16)
    nothing = jnp.zeros((n_q, PAIR), bf16)
    lse_all = lse_ref[...]
    for i in range(pairs):
        c = slice(i * PAIR, (i + 1) * PAIR)
        q2, k2, v2, g2 = q_ref[:, c] * bf16(SCALE), k_ref[:, c], v_ref[:, c], g_ref[:, c]
        product = g2.astype(f32) * o_ref[:, c].astype(f32)
        gk, gv, gq = [], [], []
        for h in range(2):
            own_q = low_q if h == 0 else ~low_q
            own_k = low_k if h == 0 else ~low_k
            dots = jnp.sum(jnp.where(own_q, product, 0.0), axis=1, keepdims=True)
            lse = jnp.sum(jnp.where(lane == base + 2 * i + h, lse_all, 0.0), axis=1, keepdims=True)
            q_more = jnp.where(own_q, q2, (q_extra + minus_pieces(lse, head_lane)).astype(bf16))
            g_more = jnp.where(own_q, g2, minus_pieces(dots, head_lane).astype(bf16))
            probs = jnp.exp(dot_nt(jnp.where(own_k, k2, k_extra), q_more))
            g_scores = (probs * dot_nt(jnp.where(own_k, v2, v_extra), g_more)).astype(bf16)
            gv.append(dot_nn(probs.astype(bf16), jnp.where(own_q, g2, nothing)))
            gk.append(dot_nn(g_scores, jnp.where(own_q, q2, nothing)))
            gq.append(dot_tn(g_scores, k2))
        store(i, gk[0] + gk[1], gv[0] + gv[1])
        gq_ref[:, c] = jnp.where(low_q, gq[0], gq[1]) * SCALE


def normed(z):
    centred = z - jnp.mean(z, axis=-1, keepdims=True)
    r = lax.rsqrt(jnp.mean(centred * centred, axis=-1, keepdims=True) + EPSILON)
    return centred * r, r


def norm_back(z, gain, upstream):
    xhat, r = normed(z)
    inner = gain * upstream
    grad = r * (
        inner
        - jnp.mean(inner, axis=-1, keepdims=True)
        - xhat * jnp.mean(inner * xhat, axis=-1, keepdims=True)
    )
    return grad, column_sum(upstream * xhat), column_sum(upstream)


def column_sum(array_in):
    return jnp.sum(array_in, axis=0, keepdims=True)


def lanes(refs):
    return jnp.concatenate([r[...] for r in refs], axis=1)


def bias_row(packs, index):
    rows = [
        sum(p[8 * n + index : 8 * n + index + 1, :].astype(f32) for n in (0, 1, 2)) for p in packs
    ]
    return jnp.concatenate(rows, axis=1)


def mask_column(own_pack, across_pack):
    first = 24
    row = jnp.concatenate([p[first + i : first + i + 1, :] for p, i in ((own_pack, 2), (own_pack, 3), (across_pack, 0), (across_pack, 1))], axis=1)
    return as_columns(row)[:, 0:1], row.astype(f32)


def stacked(refs):
    return jnp.concatenate([r[...] for r in refs], axis=0)


def sequence_rows(spots, ref, blocks):
    size = ref.shape[1] // 4
    return jnp.concatenate(
        [ref[0, pl.ds(pl.multiple_of(spots[1 + j] * size, size), size), :] for j in range(blocks)], axis=0
    )


def kernel_call(body, name, out_shape, operands, smem=1, scratch=(), blocks=(), us=5, limit=36):
    blocks = dict(blocks)

    def spec(dims, place):
        return pl.BlockSpec(dims, lambda step, *scalars: place(*scalars))

    def whole(dims):
        return spec(dims, lambda *scalars: (0,) * len(dims))

    return pl.pallas_call(
        lambda *refs: body(*refs),
        name=name,
        out_shape=out_shape,
        grid_spec=pltpu.PrefetchScalarGridSpec(
            num_scalar_prefetch=smem,
            grid=(1,),
            in_specs=[spec(*blocks[i]) if i in blocks else whole(operands[i].shape) for i in range(smem, len(operands))],
            out_specs=[whole(o.shape) for o in out_shape],
            scratch_shapes=scratch,
        ),
        compiler_params=pltpu.CompilerParams(vmem_limit_bytes=limit * 2**20),
        cost_estimate=pl.CostEstimate(flops=int(us * 1e9), bytes_accessed=1000, transcendentals=0),
    )(*operands)


def pack_part(index):
    return ((D, PAIR), lambda *scalars: (index, 0))


PACK_TAIL = ((32, PAIR), lambda *scalars: (4 * D // 32, 0))


def of_sequence(array):
    return ((1, *array.shape[1:]), lambda spots: (spots[0],) + (0,) * (array.ndim - 1))


def shape(dims, dtype):
    return jax.ShapeDtypeStruct(dims, dtype)


def self_forward(spots, x, q_w, q_x, k_w, k_x, v_w, v_x, t_w, t_x, ids, q_ref, k_ref, v_ref, o_ref, lse_ref):
    rows = sequence_rows(spots, x, 4)
    own = q_ref.shape[0]
    q_ref[...] = (dot_nn(rows[:own], lanes([q_w, q_x])) + bias_row([t_w, t_x], 0)).astype(bf16)
    k_ref[...] = dot_nn(rows, lanes([k_w, k_x])).astype(bf16)
    v_ref[...] = (dot_nn(rows, lanes([v_w, v_x])) + bias_row([t_w, t_x], 1)).astype(bf16)
    columns = as_columns(ids[0:1, :])
    attend(2, q_ref, k_ref, v_ref, query_extra(columns[:own]), key_extra(columns), o_ref, lse_ref)


def out_rows(shards):
    blocks = D // PAIR
    return jnp.concatenate(
        [
            jnp.concatenate([s[j * PAIR : (j + 1) * PAIR, :] for j in range(blocks)], axis=1)
            for s in shards
        ],
        axis=0,
    )


def cross_heads(stream, rows, weights, tails, ids, q_ref, k_ref, v_ref, o_ref, lse_ref):
    own = q_ref.shape[0]
    q_ref[...] = (dot_nn(stream, lanes(weights[0:2])) + bias_row(tails, 2)).astype(bf16)
    k_ref[...] = dot_nn(rows, lanes(weights[2:4])).astype(bf16)
    v_ref[...] = (dot_nn(rows, lanes(weights[4:6])) + bias_row(tails, 3)).astype(bf16)
    queries = query_extra(as_columns(ids[0:1, :own]))
    attend(2, q_ref, k_ref, v_ref, queries, key_extra(as_columns(ids[1:2, :])), o_ref, lse_ref)


def cross_first(
    spots, o_a, o_b, so0, so1, so2, so3, x, e, q_w, q_x, k_w, k_x, v_w, v_x, t0, t1, t2, ids, out_bias, gain, shift,
    s1_ref, z1_ref, q_ref, k_ref, v_ref, o_ref, lse_ref, sums_ref, xo_ref, eo_ref,
):
    own = q_ref.shape[0]
    valid, valid_row = mask_column(t0, t2)
    branch = dot_nn(lanes([o_a, o_b]), out_rows([so0, so1, so2, so3])) + out_bias[0:1, :]
    sums_ref[...] = jnp.zeros_like(sums_ref)
    sums_ref[0:1, :] = column_sum(valid * branch * branch)
    sums_ref[13:14, :] = valid_row
    x_own = sequence_rows(spots, x, 2)
    xo_ref[...] = x_own
    z = x_own.astype(f32) + branch
    z1_ref[...] = z
    stream = (normed(z)[0] * gain[0:1, :] + shift[0:1, :]).astype(bf16)
    s1_ref[...] = stream
    rows = sequence_rows(spots, e, 4)
    eo_ref[...] = rows[:own]
    cross_heads(stream, rows, [q_w, q_x, k_w, k_x, v_w, v_x], [t0, t1], ids, q_ref, k_ref, v_ref, o_ref, lse_ref)


def cross_second(
    spots, s1, o_a, e, q_w, q_x, k_w, k_x, v_w, v_x, co0, co1, co2, co3, t0, t2, t3, ids, out_bias, gain, shift, sums,
    q_ref, k_ref, v_ref, o_ref, lse_ref, s2_ref, z2_ref, sums_ref,
):
    stream = s1[...]
    valid = mask_column(t0, t2)[0]
    rows = sequence_rows(spots, e, 4)
    cross_heads(stream, rows, [q_w, q_x, k_w, k_x, v_w, v_x], [t2, t3], ids, q_ref, k_ref, v_ref, o_ref, lse_ref)
    branch = dot_nn(lanes([o_a, o_ref]), out_rows([co0, co1, co2, co3])) + out_bias[1:2, :]
    sums_ref[...] = sums[...]
    sums_ref[1:2, :] = column_sum(valid * branch * branch)
    z = stream.astype(f32) + branch
    z2_ref[...] = z
    s2_ref[...] = (normed(z)[0] * gain[1:2, :] + shift[1:2, :]).astype(bf16)


def feed(
    spots, s2, z2, fi0, fi1, fi2, fi3, fo0, fo1, fo2, fo3, b0, b1, b2, b3, out_bias, gain, shift, cot, cot_other,
    co0, co1, co2, co3, o_a, o_b, sums,
    kept_out, sent_out, sent_parts, kept_parts, g2_ref, gc_a, gc_b, out_t, sums_ref,
    slope, hidden,
):
    curve = (2.0 / 3.141592653589793) ** 0.5
    stream = s2[...]
    rows, width = stream.shape[0], fi0.shape[1]
    valid = mask_column(b0, b2)[0]
    sums_ref[...] = sums[...]
    branch = jnp.zeros((rows, D), f32) + out_bias[2:3, :]
    ins, outs, offsets = [fi0, fi1, fi2, fi3], [fo0, fo1, fo2, fo3], [b0, b1, b2, b3]
    for j in range(4):
        offset = jnp.concatenate([bias_row([offsets[j]], 4 + n) for n in range(width // PAIR)], axis=1)
        pre = dot_nn(stream, ins[j][...]) + offset
        square = pre * pre
        bend = jnp.tanh(curve * pre * (1.0 + 0.044715 * square))
        half = 0.5 * (1.0 + bend)
        slope[j] = half + 0.5 * pre * (1.0 - bend * bend) * (curve * (1.0 + 3.0 * 0.044715 * square))
        units = (pre * half).astype(bf16)
        hidden[j] = units
        branch = branch + dot_nn(units, outs[j][...])
    z = stream.astype(f32) + branch
    final = normed(z)[0] * gain[2:3, :] + shift[2:3, :]
    low = final.astype(bf16)
    kept_out[...] = low[: rows // 2]
    sent_out[...] = low[rows // 2 :]
    sums_ref[2:3, :] = column_sum(valid * branch * branch)
    sums_ref[3:4, :] = column_sum(valid * final * final)
    upstream = jnp.concatenate([cot[0], cot_other[...].astype(f32)], axis=0) * valid
    g3, row_gain, row_shift = norm_back(z, gain[2:3, :], upstream)
    sums_ref[4:5, :] = row_gain
    sums_ref[5:6, :] = row_shift
    sums_ref[6:7, :] = column_sum(g3)
    g_low = g3.astype(bf16)
    up = g3
    for j in range(4):
        g_pre = dot_nt(g_low, outs[j][...]) * slope[j]
        store_shard_row(sums_ref, j, 1, column_sum(g_pre))
        pre_low = g_pre.astype(bf16)
        up = up + dot_nt(pre_low, ins[j][...])
        to = sent_parts if j % 2 else kept_parts
        to[j // 2, 0:D, :] = dot_tn(stream, pre_low).astype(bf16)
        to[j // 2, D : D + width, :] = dot_tn(hidden[j], g_low).astype(bf16)
    g2, row_gain, row_shift = norm_back(z2[...], gain[1:2, :], up)
    sums_ref[7:8, :] = row_gain
    sums_ref[8:9, :] = row_shift
    sums_ref[9:10, :] = column_sum(g2)
    g2_ref[...] = g2
    g_low = g2.astype(bf16)
    g_cross = dot_nt(g_low, out_rows([co0, co1, co2, co3])).astype(bf16)
    gc_a[...] = g_cross[:, : 2 * PAIR]
    gc_b[...] = g_cross[:, 2 * PAIR :]
    store_blocks(out_t, dot_tn(lanes([o_a, o_b]), g_low))


def store_shard_row(sums_ref, j, row, value):
    sums_ref[16 + 2 * j + row : 17 + 2 * j + row, : value.shape[1]] = value


def store_chunks(to, part):
    for j in range(to.shape[0]):
        to[j] = part[:, j * PAIR : (j + 1) * PAIR].astype(bf16)


def store_blocks(to, part):
    for j in range(4):
        for c in range(D // PAIR):
            block = part[j * PAIR : (j + 1) * PAIR, c * PAIR : (c + 1) * PAIR]
            to[j, c * PAIR : (c + 1) * PAIR, :] = block.astype(bf16)


def kv_store(sent_ref, kept_ref, sums_ref):
    own, width = kept_ref.shape[0], kept_ref.shape[1] // 2

    def store(i, gk, gv):
        here = i * PAIR
        there = (i ^ 1) * PAIR
        kept_ref[:, here : here + PAIR] = gk[:own]
        kept_ref[:, width + here : width + here + PAIR] = gv[:own]
        sent_ref[:, there : there + PAIR] = gk[own:].astype(bf16)
        sent_ref[:, width + there : width + there + PAIR] = gv[own:].astype(bf16)
        sums_ref[1:2, here : here + PAIR] = column_sum(gv)

    return store


def half_back(source, q, k, v, o, lse, g, ids, rows, sent_ref, kept_ref, part_q, sums_ref, gq_ref):
    own = q.shape[0]
    sums_ref[...] = jnp.zeros_like(sums_ref)
    queries = query_extra(as_columns(ids[0:1, :own]))
    keys = key_extra(as_columns(ids[source : source + 1, :]))
    store = kv_store(sent_ref, kept_ref, sums_ref)
    attend_back(2, 0, q, k, v, o, g, lse, queries, keys, gq_ref, store)
    gq = gq_ref[...]
    sums_ref[0:1, : 2 * PAIR] = column_sum(gq)
    low = gq.astype(bf16)
    store_chunks(part_q, dot_tn(rows[...], low))
    return low


def far_back(source, q, k, v, o, lse, g, ids, rows, sent, kept, part_q, low_ref, sums, gq_ref):
    low_ref[...] = half_back(source, q, k, v, o, lse, g, ids, rows, sent, kept, part_q, sums, gq_ref)


def self_back(
    q, k, v, o, lse, g, ids, rows, low_b, acc, w0, w1, w2, w3, sent, kept, part_q, acc_ref, sums, gq_ref
):
    low = half_back(0, q, k, v, o, lse, g, ids, rows, sent, kept, part_q, sums, gq_ref)
    acc_ref[...] = acc[...] + dot_nt(low, lanes([w0, w1])) + dot_nt(low_b[...], lanes([w2, w3]))


def cross_back_norm(
    spots, q, k, v, o, lse, g, ids, rows, low_b, acc, w0, w1, w2, w3, z1, gain, o_a, o_b, so0, so1, so2, so3, sums_b,
    carried,
    sent, kept, part_q, g1_ref, gs_a, gs_b, out_t, sums, all_ref, gq_ref,
):
    low = half_back(1, q, k, v, o, lse, g, ids, rows, sent, kept, part_q, sums, gq_ref)
    up = acc[...] + dot_nt(low, lanes([w0, w1])) + dot_nt(low_b[...], lanes([w2, w3]))
    g1, row_gain, row_shift = norm_back(z1[...], gain[0:1, :], up)
    all_ref[...] = carried[...]
    all_ref[10:11, :] = row_gain
    all_ref[11:12, :] = row_shift
    all_ref[12:13, :] = column_sum(g1)
    for j in range(4):
        c = slice((j % 2) * PAIR, (j % 2 + 1) * PAIR)
        of = sums if j < 2 else sums_b
        store_shard_row(all_ref, j, 0, jnp.concatenate([of[0:1, c], of[1:2, c]], axis=1))
    g1_ref[...] = g1
    g_low = g1.astype(bf16)
    g_self = dot_nt(g_low, out_rows([so0, so1, so2, so3])).astype(bf16)
    gs_a[...] = g_self[:, : 2 * PAIR]
    gs_b[...] = g_self[:, 2 * PAIR :]
    store_blocks(out_t, dot_tn(lanes([o_a, o_b]), g_low))


def finish(first, mode, n_out, *refs):
    kept, other, rows, k_w, k_x, v_w, v_x, part_q, *refs = refs
    along, sums, refs = refs[:n_out], refs[n_out], refs[n_out + 1 :]
    outs = refs if mode == "start" else refs[1:]
    both = (kept[...] + other[...].astype(f32)).astype(bf16)
    gk, gv = both[:, : 2 * PAIR], both[:, 2 * PAIR :]
    res = dot_nt(gk, lanes([k_w, k_x])) + dot_nt(gv, lanes([v_w, v_x]))
    if mode != "start":
        res = res + refs[0][...]
    part = dot_tn(rows[...], both).astype(bf16)
    for j in range(2):
        to = outs[j]
        to[0:D, :] = part_q[j]
        to[D : 2 * D, :] = part[:, j * PAIR : (j + 1) * PAIR]
        to[2 * D : 3 * D, :] = part[:, (2 + j) * PAIR : (3 + j) * PAIR]
        for n in range(n_out):
            to[(3 + n) * D : (4 + n) * D, :] = along[n][j]
        last = (3 + n_out) * D
        to[last:, :] = jnp.zeros((to.shape[0] - last, PAIR), bf16)
        if n_out == 0:
            to[last : last + 2, :] = sums[0:2, j * PAIR : (j + 1) * PAIR].astype(bf16)
        else:
            for c in range(4):
                to[last + 16 * c : last + 16 * (c + 1), :] = sums[0:16, c * PAIR : (c + 1) * PAIR].astype(bf16)
            row = 16 + 2 * (first + j)
            blocks = [(row, 0), (row, 1), (row + 1, 0), (row + 1, 1), (row + 1, 2), (row + 1, 3)]
            shard_rows = jnp.concatenate(
                [sums[r : r + 1, c * PAIR : (c + 1) * PAIR] for r, c in blocks] + [jnp.zeros((2, PAIR), f32)], axis=0
            )
            to[last + 64 : last + 72, :] = shard_rows.astype(bf16)
    if mode == "last":
        half = res.shape[0] // 2
        outs[2][...] = res[:half]
        outs[3][...] = res[half:].astype(bf16)
    else:
        outs[2][...] = res


def own_first(ids, mine, rank):
    row = lax.dynamic_index_in_dim(ids, mine, 0, True)
    size = ids.shape[1] // 4
    parts = [
        lax.dynamic_slice_in_dim(row, (rank ^ step) * size, size, 1) for step in (0, 2, 1, 3)
    ]
    return jnp.concatenate(parts, axis=1)


def per_device(
    decoder_layer_input,
    encoder_state_rows,
    target_segments,
    source_segments,
    valid_mask,
    cotangent,
    self_input_projection,
    self_in_bias,
    self_out_proj,
    cross_input_projection,
    cross_in_bias,
    cross_out_proj,
    feed_in_proj,
    feed_in_bias,
    feed_out_proj,
    out_bias,
    norm_gain,
    norm_bias,
):
    rank = lax.axis_index("tensor")
    mine = rank // 2
    first = mine == 0
    length = decoder_layer_input.shape[1]
    own = length // 2
    width = self_out_proj.shape[0]
    units = feed_in_proj.shape[1]
    spots = jnp.stack([mine, rank, rank ^ 2, rank ^ 1, rank ^ 3]).astype(jnp.int32)

    def attention_weights(in_proj, out_proj, *more):
        blocks = [out_proj[:, j * width : (j + 1) * width] for j in range(D // width)]
        return jnp.concatenate([in_proj.reshape(-1, width), *blocks, *more], axis=0)

    biases = jnp.concatenate([self_in_bias, cross_in_bias, feed_in_bias.reshape(-1, width)], axis=0)
    high = lax.reduce_precision(biases, 8, 7)
    middle = lax.reduce_precision(biases - high, 8, 7)
    low = (biases - high - middle).astype(bf16)
    high, middle = high.astype(bf16), middle.astype(bf16)
    mask_rows = valid_mask.astype(bf16).reshape(2, -1, width)
    mask_kept = jnp.where(first, mask_rows[0], mask_rows[1])
    mask_sent = jnp.where(first, mask_rows[1], mask_rows[0])
    self_shard = attention_weights(
        self_input_projection, self_out_proj, high, middle, low, mask_sent, mask_kept, jnp.zeros((4, width), bf16)
    )
    ids = jnp.concatenate(
        [own_first(target_segments, mine, rank), own_first(source_segments, mine, rank)], axis=0
    )
    self_near = [self_shard, partner(self_shard, 1)]
    self_across = partner(self_shard, 2)

    half_shapes = [
        shape((own, 2 * PAIR), bf16), shape((length, 2 * PAIR), bf16), shape((length, 2 * PAIR), bf16),
        shape((own, 2 * PAIR), bf16), shape((own, PAIR), f32),
    ]
    full = (own, D)
    sums_shape = shape((32, D), f32)

    def parts(index, packs, at):
        return list(packs), {at + i: pack_part(index) for i in range(len(packs))}

    def tails(packs, at):
        return list(packs), {at + i: PACK_TAIL for i in range(len(packs))}

    def laid(operands, *groups):
        blocks = {}
        for group in groups:
            if isinstance(group, tuple):
                more, places = group[0](*group[1:], len(operands))
                operands = operands + more
                blocks.update(places)
            else:
                operands = operands + group
        return operands, blocks

    def sequence(array, at):
        return [array], {at: of_sequence(array)}

    def self_half(shards, x):
        operands, blocks = laid(
            [spots], (sequence, x), (parts, 0, shards), (parts, 1, shards), (parts, 2, shards), (tails, shards), [ids]
        )
        return kernel_call(self_forward, "self_forward", half_shapes, operands, blocks=blocks)

    cross_shard = attention_weights(cross_input_projection, cross_out_proj)
    cross_piece = half_here(cross_shard, 1)
    feed_piece = half_here(feed_in_proj, 1)
    q_a, k_a, v_a, o_a, lse_a = self_half(self_near, tie(decoder_layer_input, cross_piece, feed_piece))
    feed_in_1, feed_out_1, cot_1, cross_piece, feed_piece, cross_shard = tie(
        (feed_in_proj, feed_out_proj, cotangent, cross_piece, feed_piece, cross_shard), q_a
    )
    cot_sent = lax.dynamic_index_in_dim(cot_1, 1 - mine, 0, False).astype(bf16)
    self_far = [self_across, partner(tie(self_across, cot_sent), 1)]
    self_all = self_near + self_far
    cross_got, feed_got = partner(cross_piece, 2), partner(feed_piece, 2)
    q_b, k_b, v_b, o_b, lse_b = self_half(self_far, decoder_layer_input)
    cross_near = [cross_shard, partner(tie(cross_shard, self_across), 1)]
    cross_got, feed_got, cot_sent, feed_in_1, feed_out_1 = tie((cross_got, feed_got, cot_sent, feed_in_1, feed_out_1), q_b)
    cross_got_x, feed_got_x = partner_dp(cross_got, 1), partner_dp(feed_got, 1)
    cut = feed_out_1.shape[0] // 2
    out_top, cot_other = partner(feed_out_1[:cut], 2), partner(cot_sent, 2)
    operands, blocks = laid(
        [spots, o_a, tie(o_b, cross_got, feed_got)], (parts, 3, self_all), (sequence, decoder_layer_input),
        (sequence, encoder_state_rows), (parts, 0, cross_near), (parts, 1, cross_near), (parts, 2, cross_near),
        (tails, self_all[:3]), [ids, out_bias, norm_gain, norm_bias],
    )
    s1, z1, cq_a, ck_a, cv_a, co_a, clse_a, sums, x_own, e_own = kernel_call(
        cross_first,
        "cross_first",
        [shape(full, bf16), shape(full, f32), *half_shapes, sums_shape, shape(full, bf16), shape(full, bf16)],
        operands,
        blocks=blocks,
    )
    cross_got, cross_got_x, feed_got, feed_got_x, out_top, cot_other, feed_in_1, feed_out_1 = tie(
        (cross_got, cross_got_x, feed_got, feed_got_x, out_top, cot_other, feed_in_1, feed_out_1), s1
    )
    cross_across = in_order(cross_got, cross_got_x, 1)
    cross_far = [cross_across, partner(cross_across, 1)]
    cross_all = cross_near + cross_far
    feed_in_across = in_order(feed_got, feed_got_x, 1)
    out_rest = partner(feed_out_1[cut:], 2)
    feed_in_other, feed_out_other = partner(feed_in_1, 1), partner(feed_out_1, 1)
    operands, blocks = laid(
        [spots, tie(s1, feed_in_across, out_top, cot_other), co_a], (sequence, encoder_state_rows),
        (parts, 0, cross_far), (parts, 1, cross_far), (parts, 2, cross_far), (parts, 3, cross_all),
        (tails, [self_all[0], self_all[2], self_all[3]]), [ids, out_bias, norm_gain, norm_bias, sums],
    )
    cq_b, ck_b, cv_b, co_b, clse_b, s2, z2, sums = kernel_call(
        cross_second,
        "cross_second",
        [*half_shapes, shape(full, bf16), shape(full, f32), sums_shape],
        operands,
        blocks=blocks,
    )
    out_top, out_rest = tie((out_top, out_rest), s2)
    feed_out_across = jnp.concatenate([out_top, out_rest], axis=0)
    feed_in_all = [feed_in_1, feed_in_other, feed_in_across, partner(feed_in_across, 1)]
    feed_out_all = [feed_out_1, feed_out_other, feed_out_across, partner(feed_out_across, 1)]

    operands, blocks = laid(
        [spots, s2, z2, *feed_in_all, *feed_out_all], (tails, self_all), [out_bias, norm_gain, norm_bias],
        (sequence, cotangent), [cot_other], (parts, 3, cross_all), [co_a, co_b, sums],
    )
    half = (own, 2 * PAIR)
    out_kept, out_sent, feed_sent, feed_kept, g2, g_cross_a, g_cross_b, cross_out_t, sums = kernel_call(
        feed,
        "feed",
        [
            shape((own // 2, D), bf16), shape((own // 2, D), bf16),
            shape((2, D + units, D), bf16), shape((2, D + units, D), bf16),
            shape(full, f32), shape(half, bf16), shape(half, bf16), shape((4, D, PAIR), bf16), sums_shape,
        ],
        operands,
        scratch=[pltpu.VMEM((4, own, units), f32), pltpu.VMEM((4, own, units), bf16)],
        blocks=blocks,
    )
    feed_got = partner(feed_sent, 1)
    out_got = partner(out_sent, 2)

    kv_shapes = [shape(full, bf16), shape(full, f32), shape((2, D, PAIR), bf16)]

    def back_far(source, heads, g, rows):
        return kernel_call(
            lambda *refs: far_back(source, *refs),
            "attention_back",
            [*kv_shapes, shape(half, bf16), shape((8, D), f32)],
            [*heads, g, ids, rows],
            smem=0,
            scratch=[pltpu.VMEM(half, f32)],
        )

    def finished(first_pair, mode, kept, got, rows, shards, part, along, small, acc=None):
        n_out = len(along)
        last = [shape((own // 2, D), f32), shape((own // 2, D), bf16)] if mode == "last" else [shape(full, f32)]
        count = (3 + n_out) * D + (96 if n_out else 64)
        operands, blocks = laid([kept, got, rows], (parts, 1, shards), (parts, 2, shards), [part])
        if n_out:
            blocks.update(
                {len(operands) + n: ((2, D, PAIR), lambda *scalars: (first_pair // 2, 0, 0)) for n in range(n_out)}
            )
        return kernel_call(
            lambda *refs: finish(first_pair, mode, n_out, *refs),
            "finish",
            [shape((count, width), bf16), shape((count, width), bf16), *last],
            operands + list(along) + [small] + ([] if acc is None else [acc]),
            smem=0,
            blocks=blocks,
            us=2,
        )

    def added(*parts):
        total = parts[0].astype(f32)
        for part in parts[1:]:
            total = total + part.astype(f32)
        return total

    gkv_sent_b, gkv_kept_b, part_b, low_b, sums_b = back_far(1, [cq_b, ck_b, cv_b, co_b, clse_b], g_cross_b, s1)
    gkv_got_b = partner(gkv_sent_b, 1)
    feed_kept, feed_got = tie((feed_kept, feed_got), low_b)

    def half_of(rows, sent):
        cut = rows.shape[-2] // 2
        upper = (lax.axis_index("dp") & 1) != 0
        first, second = rows[..., :cut, :], rows[..., cut:, :]
        return jnp.where(upper, first, second) if sent else jnp.where(upper, second, first)

    in_y = added(feed_kept[1, :D], feed_got[1, :D]).astype(bf16)
    out_x = added(half_of(feed_kept[:, D:], True), half_of(feed_got[:, D:], True)).astype(bf16)
    in_y_got, out_x_got = partner(in_y, 2), partner_dp(out_x, 1)
    operands, blocks = laid(
        [spots, cq_a, ck_a, cv_a, co_a, clse_a, g_cross_a, ids, s1, tie(low_b, in_y, out_x, out_got), g2],
        (parts, 0, cross_all), [z1, norm_gain, o_a, o_b], (parts, 3, self_all), [sums_b, sums],
    )
    gkv_sent, gkv_kept, part_a, g1, g_self_a, g_self_b, self_out_t, sums_a, sums = kernel_call(
        cross_back_norm,
        "cross_back_norm",
        [
            *kv_shapes, shape(full, f32), shape(half, bf16), shape(half, bf16), shape((4, D, PAIR), bf16),
            shape((8, D), f32), sums_shape,
        ],
        operands,
        scratch=[pltpu.VMEM(half, f32)],
        blocks=blocks,
    )
    gkv_got = partner(gkv_sent, 1)
    cb_kept, cb_sent, enc_acc = finished(
        2, "start", gkv_kept_b, gkv_got_b, tie(e_own, g1), cross_far, part_b, [cross_out_t, self_out_t], sums
    )
    cb_got = partner(cb_sent, 1)
    in_y_got, out_x_got, feed_kept, feed_got = tie((in_y_got, out_x_got, feed_kept, feed_got), enc_acc)
    in_x = added(half_of(feed_kept[0, :D], True), half_of(feed_got[0, :D], True), half_of(in_y_got, True)).astype(bf16)
    out_y = added(half_of(feed_kept[1, D:], False), half_of(feed_got[1, D:], False), out_x_got[1]).astype(bf16)
    in_x_got, out_y_got = partner_dp(in_x, 1), partner(out_y, 2)
    cb_kept, cb_got = tie((cb_kept, cb_got), in_x, out_y)
    cross_b = added(cb_kept, cb_got).astype(bf16)
    cut = cross_b.shape[0] // 2
    cross_y = [partner(cross_b[:cut], 2), None]

    gkv_sent_b, gkv_kept_b, part_b, low_b, sums_b = back_far(
        0, [q_b, k_b, v_b, o_b, lse_b], g_self_b, tie(x_own, enc_acc, in_x, out_y, cross_b)
    )
    gkv_got_b = partner(gkv_sent_b, 1)
    in_x_got, out_y_got, cross_y[0] = tie((in_x_got, out_y_got, cross_y[0]), low_b)
    cross_y[1] = partner(tie(cross_b[cut:], cross_y[0]), 2)
    feed_total = jnp.stack(
        [
            added(half_of(feed_kept[0, :D], False), half_of(feed_got[0, :D], False), half_of(in_y_got, False), in_x_got),
            added(half_of(feed_kept[0, D:], False), half_of(feed_got[0, D:], False), out_x_got[0], out_y_got),
        ]
    )
    feed_sum = DpSum(feed_total, dp_bits()[1:])
    ca_kept, ca_sent, enc_kept, enc_sent = finished(
        0, "last", gkv_kept, gkv_got, tie(e_own, cross_y[0], feed_sum.value), cross_near, part_a,
        [cross_out_t, self_out_t], sums, enc_acc,
    )
    ca_got = partner(ca_sent, 1)
    sb_kept, sb_sent, acc = finished(
        2, "middle", gkv_kept_b, gkv_got_b, tie(x_own, enc_kept), self_far, part_b, [], sums_b, g1
    )
    sb_got = partner(sb_sent, 1)
    feed_sum.step(acc)
    self_b = added(sb_kept, sb_got).astype(bf16)
    self_y = partner(self_b, 2)
    cross_y, ca_kept, ca_got = tie((cross_y, ca_kept, ca_got), self_b, feed_sum.value)
    cross_sum = DpSum(added(ca_kept, ca_got, jnp.concatenate(cross_y, axis=0)), dp_bits())
    operands, blocks = laid(
        [q_a, k_a, v_a, o_a, lse_a, g_self_a, ids, x_own, tie(low_b, self_b, feed_sum.value, cross_sum.value), acc],
        (parts, 0, self_all),
    )
    gkv_sent, gkv_kept, part_a, acc, sums_a = kernel_call(
        self_back,
        "self_back",
        [*kv_shapes, shape(full, f32), shape((8, D), f32)],
        operands,
        smem=0,
        scratch=[pltpu.VMEM(half, f32)],
        blocks=blocks,
    )
    gkv_got = partner(gkv_sent, 1)
    feed_sum.step(acc)
    cross_sum.step(acc)
    sa_kept, sa_sent, in_kept, in_sent = finished(
        0, "last", gkv_kept, gkv_got, x_own, self_near, part_a, [], sums_a, acc
    )
    sa_got = partner(sa_sent, 1)
    self_y = tie(self_y, in_kept)
    self_sum = DpSum(added(sa_kept, sa_got, self_y), dp_bits())
    enc_sent, in_sent = tie((enc_sent, in_sent), self_sum.value)
    enc_got, in_got = partner(enc_sent, 2), partner(in_sent, 2)

    def to_owner(kept, other):
        other = other.astype(kept.dtype)
        return jnp.stack([jnp.where(first, kept, other), jnp.where(first, other, kept)])

    def in_grad(total):
        return total[: 3 * D].reshape(3, D, width).astype(f32)

    def out_grad(total):
        blocks = [total[c * width : (c + 1) * width] for c in range(D // width)]
        return jnp.concatenate(blocks, axis=1).astype(f32)

    self_sum.step()
    feed_sum.step(self_sum.value)
    cross_sum.step(feed_sum.value)
    self_sum.step()
    cross_sum.step(self_sum.value)
    feed_total = feed_sum.finish(cross_sum.value)
    layer_output = to_owner(out_kept, tie(out_got, self_sum.value))
    feed_total = tie(feed_total, self_sum.value)
    feed_in_grad, feed_out_grad = feed_total[0].astype(f32), feed_total[1].astype(f32)
    encoder_grad = to_owner(enc_kept, tie(enc_got, self_sum.value))
    self_sum.step(layer_output, feed_in_grad)
    cross_sum.step(self_sum.value, encoder_grad, feed_out_grad)
    input_grad = to_owner(in_kept, tie(in_got, self_sum.value))
    cross_total = cross_sum.finish(self_sum.value)
    self_sum.step(cross_total, input_grad)
    cross_total = tie(cross_total, self_sum.value)
    cross_in_grad, cross_out_grad = in_grad(cross_total), out_grad(cross_total[3 * D : 4 * D])
    self_out_grad = out_grad(cross_total[4 * D : 5 * D])
    common = cross_total[5 * D : 5 * D + 64].astype(f32).reshape(4, 16, PAIR).swapaxes(0, 1).reshape(16, 4 * PAIR)
    shard_sums = cross_total[5 * D + 64 : 5 * D + 72].astype(f32)
    rms_values = jnp.sqrt(jnp.sum(common[0:4], axis=1) / (jnp.sum(common[13]) * D))
    self_total = self_sum.finish(cross_in_grad, cross_out_grad, self_out_grad, common, shard_sums, rms_values)

    return (
        layer_output,
        input_grad,
        encoder_grad,
        in_grad(self_total),
        self_total[3 * D : 3 * D + 2].astype(f32),
        self_out_grad,
        cross_in_grad,
        shard_sums[0:2],
        cross_out_grad,
        feed_in_grad,
        shard_sums[2:6].reshape(units),
        feed_out_grad,
        jnp.stack([common[12], common[9], common[6]]),
        jnp.stack([common[10], common[7], common[4]]),
        jnp.stack([common[11], common[8], common[5]]),
        rms_values,
    )


def solution(mesh):
    return jax.shard_map(
        per_device,
        mesh=mesh,
        in_specs=(
            P("dp", None, None),
            P("dp", None, None),
            P("dp", None),
            P("dp", None),
            P("dp", "tensor"),
            P("dp", "tensor", None),
            P(None, None, "tensor"),
            P(None, "tensor"),
            P("tensor", None),
            P(None, None, "tensor"),
            P(None, "tensor"),
            P("tensor", None),
            P(None, "tensor"),
            P("tensor"),
            P("tensor", None),
            P(),
            P(),
            P(),
        ),
        out_specs=(
            P("dp", "tensor", None),
            P("dp", "tensor", None),
            P("dp", "tensor", None),
            P(None, None, "tensor"),
            P(None, "tensor"),
            P("tensor", None),
            P(None, None, "tensor"),
            P(None, "tensor"),
            P("tensor", None),
            P(None, "tensor"),
            P("tensor"),
            P("tensor", None),
            P(),
            P(),
            P(),
            P(),
        ),
        check_vma=False,
    )
```

```python
import jax
import jax.numpy as jnp
from jax import lax
from jax.experimental import pallas as pl
from jax.experimental.pallas import tpu as pltpu
from jax.sharding import PartitionSpec as P

D = 512
HEAD = 64
EPSILON = 1e-05
PAIR = 2 * HEAD
FAR = 2.0**100
SCALE = HEAD ** (-0.5)
bf16, f32 = jnp.bfloat16, jnp.float32


def partner(array_in, bit):
    count = lax.axis_size("tensor")
    return lax.ppermute(array_in, "tensor", [(i, i ^ bit) for i in range(count)])


def partner_dp(array_in, bit):
    count = lax.axis_size("dp")
    return lax.ppermute(array_in, "dp", [(i, i ^ bit) for i in range(count)])


def tie(value, *others):
    return lax.optimization_barrier((value, others))[0]


def dp_bits():
    bits = []
    bit = 1
    while bit < lax.axis_size("dp"):
        bits.append(bit)
        bit *= 2
    return bits


def halves(total, bit):
    upper = (lax.axis_index("dp") & bit) != 0
    half = total.shape[-2] // 2
    first, second = total[..., :half, :], total[..., half:, :]
    return jnp.where(upper, second, first), jnp.where(upper, first, second).astype(bf16)


def in_order(mine, other, bit):
    upper = (lax.axis_index("dp") & bit) != 0
    return jnp.concatenate([jnp.where(upper, other, mine), jnp.where(upper, mine, other)], axis=-2)


def half_here(rows, bit):
    half = rows.shape[0] // 2
    upper = (lax.axis_index("dp") & bit) != 0
    return jnp.where(upper, rows[half:], rows[:half])


class DpSum:
    def __init__(self, total, bits):
        self.todo = [("half", bit) for bit in bits[:-1]] + [("swap", bits[-1])]
        self.todo += [("double", bit) for bit in reversed(dp_bits()[:-1])]
        self.value = total
        self.start()

    def start(self):
        kind, bit = self.todo[0]
        if kind == "half":
            self.kept, self.value = halves(self.value, bit)
        else:
            self.kept = self.value = self.value.astype(bf16)
        self.got = partner_dp(self.value, bit)

    def step(self, *after):
        if self.todo:
            if after:
                self.kept, self.got = tie((self.kept, self.got), *after)
            kind, bit = self.todo.pop(0)
            if kind == "double":
                self.value = in_order(self.kept, self.got, bit)
            else:
                self.value = self.kept.astype(f32) + self.got.astype(f32)
            if self.todo:
                self.start()
        return self.value

    def finish(self, *after):
        while self.todo:
            self.step(*after)
        return self.value


def dot_nn(a, b):
    return lax.dot_general(a, b, (((1,), (0,)), ((), ())), preferred_element_type=f32)


def dot_nt(a, b):
    return lax.dot_general(a, b, (((1,), (1,)), ((), ())), preferred_element_type=f32)


def dot_tn(a, b):
    return lax.dot_general(a, b, (((0,), (0,)), ((), ())), preferred_element_type=f32)


def lane_in_head(count):
    return lax.broadcasted_iota(jnp.int32, (count, PAIR), 1) & (HEAD - 1)


def lane_low(count):
    return lax.broadcasted_iota(jnp.int32, (count, PAIR), 1) < HEAD


def as_columns(row):
    return jnp.broadcast_to(row.astype(f32), (PAIR, row.shape[1])).T


def minus_pieces(column, lane):
    high = column.astype(bf16).astype(f32)
    rest = column - high
    middle = rest.astype(bf16).astype(f32)
    low = rest - middle
    return jnp.where(lane == 4, -high, jnp.where(lane == 5, -middle, jnp.where(lane == 6, -low, 0.0)))


def query_extra(ids):
    lane = lane_in_head(ids.shape[0])
    return jnp.where((lane < 4) & (lane.astype(f32) != ids), -FAR, 0.0)


def key_extra(ids):
    lane = lane_in_head(ids.shape[0])
    ones = (lane >= 4) & (lane < 7)
    return jnp.where((lane.astype(f32) == ids) | ones, 1.0, 0.0).astype(bf16)


def attend(pairs, q_ref, k_ref, v_ref, q_extra, k_extra, o_ref, lse_ref):
    n_q, n_k = q_ref.shape[0], k_ref.shape[0]
    low_q, low_k = lane_low(n_q), lane_low(n_k)
    lane = lax.broadcasted_iota(jnp.int32, (n_q, PAIR), 1)
    extra = q_extra.astype(bf16)
    lse_all = jnp.zeros((n_q, PAIR), f32)
    for i in range(pairs):
        c = slice(i * PAIR, (i + 1) * PAIR)
        q2, k2, v2 = q_ref[:, c] * bf16(SCALE), k_ref[:, c], v_ref[:, c]
        scores = [
            dot_nt(jnp.where(low_q, q2, extra), jnp.where(low_k, k2, k_extra)),
            dot_nt(jnp.where(low_q, extra, q2), jnp.where(low_k, k_extra, k2)),
        ]
        outs = []
        for h in range(2):
            top = jnp.max(scores[h], axis=1, keepdims=True)
            terms = jnp.exp(scores[h] - top)
            total = jnp.sum(terms, axis=1, keepdims=True)
            outs.append(dot_nn(terms.astype(bf16), v2) * (1.0 / total))
            lse_all = jnp.where(lane == 2 * i + h, top + jnp.log(total), lse_all)
        o_ref[:, c] = jnp.where(low_q, outs[0], outs[1]).astype(bf16)
    lse_ref[...] = lse_all


def attend_back(pairs, base, q_ref, k_ref, v_ref, o_ref, g_ref, lse_ref, q_extra, k_extra, gq_ref, store):
    n_q, n_k = q_ref.shape[0], k_ref.shape[0]
    low_q, low_k = lane_low(n_q), lane_low(n_k)
    lane = lax.broadcasted_iota(jnp.int32, (n_q, PAIR), 1)
    head_lane = lane_in_head(n_q)
    key_lane = lane_in_head(n_k)
    v_extra = jnp.where((key_lane >= 4) & (key_lane < 7), 1.0, 0.0).astype(bf16)
    nothing = jnp.zeros((n_q, PAIR), bf16)
    lse_all = lse_ref[...]
    for i in range(pairs):
        c = slice(i * PAIR, (i + 1) * PAIR)
        q2, k2, v2, g2 = q_ref[:, c] * bf16(SCALE), k_ref[:, c], v_ref[:, c], g_ref[:, c]
        product = g2.astype(f32) * o_ref[:, c].astype(f32)
        gk, gv, gq = [], [], []
        for h in range(2):
            own_q = low_q if h == 0 else ~low_q
            own_k = low_k if h == 0 else ~low_k
            dots = jnp.sum(jnp.where(own_q, product, 0.0), axis=1, keepdims=True)
            lse = jnp.sum(jnp.where(lane == base + 2 * i + h, lse_all, 0.0), axis=1, keepdims=True)
            q_more = jnp.where(own_q, q2, (q_extra + minus_pieces(lse, head_lane)).astype(bf16))
            g_more = jnp.where(own_q, g2, minus_pieces(dots, head_lane).astype(bf16))
            probs = jnp.exp(dot_nt(jnp.where(own_k, k2, k_extra), q_more))
            g_scores = (probs * dot_nt(jnp.where(own_k, v2, v_extra), g_more)).astype(bf16)
            gv.append(dot_nn(probs.astype(bf16), jnp.where(own_q, g2, nothing)))
            gk.append(dot_nn(g_scores, jnp.where(own_q, q2, nothing)))
            gq.append(dot_tn(g_scores, k2))
        store(i, gk[0] + gk[1], gv[0] + gv[1])
        gq_ref[:, c] = jnp.where(low_q, gq[0], gq[1]) * SCALE


def normed(z):
    centred = z - jnp.mean(z, axis=-1, keepdims=True)
    r = lax.rsqrt(jnp.mean(centred * centred, axis=-1, keepdims=True) + EPSILON)
    return centred * r, r


def norm_back(z, gain, upstream):
    xhat, r = normed(z)
    inner = gain * upstream
    grad = r * (
        inner
        - jnp.mean(inner, axis=-1, keepdims=True)
        - xhat * jnp.mean(inner * xhat, axis=-1, keepdims=True)
    )
    return grad, column_sum(upstream * xhat), column_sum(upstream)


def column_sum(array_in):
    return jnp.sum(array_in, axis=0, keepdims=True)


def lanes(refs):
    return jnp.concatenate([r[...] for r in refs], axis=1)


def bias_row(packs, index):
    rows = [
        sum(p[8 * n + index : 8 * n + index + 1, :].astype(f32) for n in (0, 1, 2)) for p in packs
    ]
    return jnp.concatenate(rows, axis=1)


def mask_column(own_pack, across_pack):
    first = 24
    row = jnp.concatenate([p[first + i : first + i + 1, :] for p, i in ((own_pack, 2), (own_pack, 3), (across_pack, 0), (across_pack, 1))], axis=1)
    return as_columns(row)[:, 0:1], row.astype(f32)


def stacked(refs):
    return jnp.concatenate([r[...] for r in refs], axis=0)


def sequence_rows(spots, ref, blocks):
    size = ref.shape[1] // 4
    return jnp.concatenate(
        [ref[0, pl.ds(pl.multiple_of(spots[1 + j] * size, size), size), :] for j in range(blocks)], axis=0
    )


def kernel_call(body, name, out_shape, operands, smem=1, scratch=(), blocks=(), us=5, limit=32):
    blocks = dict(blocks)

    def spec(dims, place):
        return pl.BlockSpec(dims, lambda step, *scalars: place(*scalars))

    def whole(dims):
        return spec(dims, lambda *scalars: (0,) * len(dims))

    return pl.pallas_call(
        lambda *refs: body(*refs),
        name=name,
        out_shape=out_shape,
        grid_spec=pltpu.PrefetchScalarGridSpec(
            num_scalar_prefetch=smem,
            grid=(1,),
            in_specs=[spec(*blocks[i]) if i in blocks else whole(operands[i].shape) for i in range(smem, len(operands))],
            out_specs=[whole(o.shape) for o in out_shape],
            scratch_shapes=scratch,
        ),
        compiler_params=pltpu.CompilerParams(vmem_limit_bytes=limit * 2**20),
        cost_estimate=pl.CostEstimate(flops=int(us * 1e9), bytes_accessed=1000, transcendentals=0),
    )(*operands)


def pack_part(index):
    return ((D, PAIR), lambda *scalars: (index, 0))


PACK_TAIL = ((32, PAIR), lambda *scalars: (4 * D // 32, 0))


def of_sequence(array):
    return ((1, *array.shape[1:]), lambda spots: (spots[0],) + (0,) * (array.ndim - 1))


def shape(dims, dtype):
    return jax.ShapeDtypeStruct(dims, dtype)


def self_forward(spots, x, q_w, q_x, k_w, k_x, v_w, v_x, t_w, t_x, ids, q_ref, k_ref, v_ref, o_ref, lse_ref):
    rows = sequence_rows(spots, x, 4)
    own = q_ref.shape[0]
    q_ref[...] = (dot_nn(rows[:own], lanes([q_w, q_x])) + bias_row([t_w, t_x], 0)).astype(bf16)
    k_ref[...] = dot_nn(rows, lanes([k_w, k_x])).astype(bf16)
    v_ref[...] = (dot_nn(rows, lanes([v_w, v_x])) + bias_row([t_w, t_x], 1)).astype(bf16)
    columns = as_columns(ids[0:1, :])
    attend(2, q_ref, k_ref, v_ref, query_extra(columns[:own]), key_extra(columns), o_ref, lse_ref)


def out_rows(shards):
    blocks = D // PAIR
    return jnp.concatenate(
        [
            jnp.concatenate([s[j * PAIR : (j + 1) * PAIR, :] for j in range(blocks)], axis=1)
            for s in shards
        ],
        axis=0,
    )


def cross_heads(stream, rows, weights, tails, ids, q_ref, k_ref, v_ref, o_ref, lse_ref):
    own = q_ref.shape[0]
    q_ref[...] = (dot_nn(stream, lanes(weights[0:2])) + bias_row(tails, 2)).astype(bf16)
    k_ref[...] = dot_nn(rows, lanes(weights[2:4])).astype(bf16)
    v_ref[...] = (dot_nn(rows, lanes(weights[4:6])) + bias_row(tails, 3)).astype(bf16)
    queries = query_extra(as_columns(ids[0:1, :own]))
    attend(2, q_ref, k_ref, v_ref, queries, key_extra(as_columns(ids[1:2, :])), o_ref, lse_ref)


def cross_first(
    spots, o_a, o_b, so0, so1, so2, so3, x, e, q_w, q_x, k_w, k_x, v_w, v_x, t0, t1, t2, ids, out_bias, gain, shift,
    s1_ref, z1_ref, q_ref, k_ref, v_ref, o_ref, lse_ref, sums_ref, xo_ref, eo_ref,
):
    own = q_ref.shape[0]
    valid, valid_row = mask_column(t0, t2)
    branch = dot_nn(lanes([o_a, o_b]), out_rows([so0, so1, so2, so3])) + out_bias[0:1, :]
    sums_ref[...] = jnp.zeros_like(sums_ref)
    sums_ref[0:1, :] = column_sum(valid * branch * branch)
    sums_ref[13:14, :] = valid_row
    x_own = sequence_rows(spots, x, 2)
    xo_ref[...] = x_own
    z = x_own.astype(f32) + branch
    z1_ref[...] = z
    stream = (normed(z)[0] * gain[0:1, :] + shift[0:1, :]).astype(bf16)
    s1_ref[...] = stream
    rows = sequence_rows(spots, e, 4)
    eo_ref[...] = rows[:own]
    cross_heads(stream, rows, [q_w, q_x, k_w, k_x, v_w, v_x], [t0, t1], ids, q_ref, k_ref, v_ref, o_ref, lse_ref)


def cross_second(
    spots, s1, o_a, e, q_w, q_x, k_w, k_x, v_w, v_x, co0, co1, co2, co3, t0, t2, t3, ids, out_bias, gain, shift, sums,
    q_ref, k_ref, v_ref, o_ref, lse_ref, s2_ref, z2_ref, sums_ref,
):
    stream = s1[...]
    valid = mask_column(t0, t2)[0]
    rows = sequence_rows(spots, e, 4)
    cross_heads(stream, rows, [q_w, q_x, k_w, k_x, v_w, v_x], [t2, t3], ids, q_ref, k_ref, v_ref, o_ref, lse_ref)
    branch = dot_nn(lanes([o_a, o_ref]), out_rows([co0, co1, co2, co3])) + out_bias[1:2, :]
    sums_ref[...] = sums[...]
    sums_ref[1:2, :] = column_sum(valid * branch * branch)
    z = stream.astype(f32) + branch
    z2_ref[...] = z
    s2_ref[...] = (normed(z)[0] * gain[1:2, :] + shift[1:2, :]).astype(bf16)


def feed(
    spots, s2, z2, fi0, fi1, fi2, fi3, fo0, fo1, fo2, fo3, b0, b1, b2, b3, out_bias, gain, shift, cot, cot_other,
    co0, co1, co2, co3, o_a, o_b, sums,
    kept_out, sent_out, sent_parts, kept_parts, g2_ref, gc_a, gc_b, out_t, sums_ref,
    slope, hidden,
):
    curve = (2.0 / 3.141592653589793) ** 0.5
    stream = s2[...]
    rows, width = stream.shape[0], fi0.shape[1]
    valid = mask_column(b0, b2)[0]
    sums_ref[...] = sums[...]
    branch = jnp.zeros((rows, D), f32) + out_bias[2:3, :]
    ins, outs, offsets = [fi0, fi1, fi2, fi3], [fo0, fo1, fo2, fo3], [b0, b1, b2, b3]
    for j in range(4):
        offset = jnp.concatenate([bias_row([offsets[j]], 4 + n) for n in range(width // PAIR)], axis=1)
        pre = dot_nn(stream, ins[j][...]) + offset
        square = pre * pre
        bend = jnp.tanh(curve * pre * (1.0 + 0.044715 * square))
        half = 0.5 * (1.0 + bend)
        slope[j] = half + 0.5 * pre * (1.0 - bend * bend) * (curve * (1.0 + 3.0 * 0.044715 * square))
        units = (pre * half).astype(bf16)
        hidden[j] = units
        branch = branch + dot_nn(units, outs[j][...])
    z = stream.astype(f32) + branch
    final = normed(z)[0] * gain[2:3, :] + shift[2:3, :]
    low = final.astype(bf16)
    kept_out[...] = low[: rows // 2]
    sent_out[...] = low[rows // 2 :]
    sums_ref[2:3, :] = column_sum(valid * branch * branch)
    sums_ref[3:4, :] = column_sum(valid * final * final)
    upstream = jnp.concatenate([cot[0], cot_other[...].astype(f32)], axis=0) * valid
    g3, row_gain, row_shift = norm_back(z, gain[2:3, :], upstream)
    sums_ref[4:5, :] = row_gain
    sums_ref[5:6, :] = row_shift
    sums_ref[6:7, :] = column_sum(g3)
    g_low = g3.astype(bf16)
    up = g3
    for j in range(4):
        g_pre = dot_nt(g_low, outs[j][...]) * slope[j]
        store_shard_row(sums_ref, j, 1, column_sum(g_pre))
        pre_low = g_pre.astype(bf16)
        up = up + dot_nt(pre_low, ins[j][...])
        to = sent_parts if j % 2 else kept_parts
        to[j // 2, 0:D, :] = dot_tn(stream, pre_low).astype(bf16)
        to[j // 2, D : D + width, :] = dot_tn(hidden[j], g_low).astype(bf16)
    g2, row_gain, row_shift = norm_back(z2[...], gain[1:2, :], up)
    sums_ref[7:8, :] = row_gain
    sums_ref[8:9, :] = row_shift
    sums_ref[9:10, :] = column_sum(g2)
    g2_ref[...] = g2
    g_low = g2.astype(bf16)
    g_cross = dot_nt(g_low, out_rows([co0, co1, co2, co3])).astype(bf16)
    gc_a[...] = g_cross[:, : 2 * PAIR]
    gc_b[...] = g_cross[:, 2 * PAIR :]
    store_blocks(out_t, dot_tn(lanes([o_a, o_b]), g_low))


def store_shard_row(sums_ref, j, row, value):
    sums_ref[16 + 2 * j + row : 17 + 2 * j + row, : value.shape[1]] = value


def store_chunks(to, part):
    for j in range(to.shape[0]):
        to[j] = part[:, j * PAIR : (j + 1) * PAIR].astype(bf16)


def store_blocks(to, part):
    for j in range(4):
        for c in range(D // PAIR):
            block = part[j * PAIR : (j + 1) * PAIR, c * PAIR : (c + 1) * PAIR]
            to[j, c * PAIR : (c + 1) * PAIR, :] = block.astype(bf16)


def kv_store(sent_ref, kept_ref, sums_ref):
    own, width = kept_ref.shape[0], kept_ref.shape[1] // 2

    def store(i, gk, gv):
        here = i * PAIR
        there = (i ^ 1) * PAIR
        kept_ref[:, here : here + PAIR] = gk[:own]
        kept_ref[:, width + here : width + here + PAIR] = gv[:own]
        sent_ref[:, there : there + PAIR] = gk[own:].astype(bf16)
        sent_ref[:, width + there : width + there + PAIR] = gv[own:].astype(bf16)
        sums_ref[1:2, here : here + PAIR] = column_sum(gv)

    return store


def half_back(source, q, k, v, o, lse, g, ids, rows, sent_ref, kept_ref, part_q, sums_ref, gq_ref):
    own = q.shape[0]
    sums_ref[...] = jnp.zeros_like(sums_ref)
    queries = query_extra(as_columns(ids[0:1, :own]))
    keys = key_extra(as_columns(ids[source : source + 1, :]))
    store = kv_store(sent_ref, kept_ref, sums_ref)
    attend_back(2, 0, q, k, v, o, g, lse, queries, keys, gq_ref, store)
    gq = gq_ref[...]
    sums_ref[0:1, : 2 * PAIR] = column_sum(gq)
    low = gq.astype(bf16)
    store_chunks(part_q, dot_tn(rows[...], low))
    return low


def far_back(source, q, k, v, o, lse, g, ids, rows, sent, kept, part_q, low_ref, sums, gq_ref):
    low_ref[...] = half_back(source, q, k, v, o, lse, g, ids, rows, sent, kept, part_q, sums, gq_ref)


def self_back(
    q, k, v, o, lse, g, ids, rows, low_b, acc, w0, w1, w2, w3, sent, kept, part_q, acc_ref, sums, gq_ref
):
    low = half_back(0, q, k, v, o, lse, g, ids, rows, sent, kept, part_q, sums, gq_ref)
    acc_ref[...] = acc[...] + dot_nt(low, lanes([w0, w1])) + dot_nt(low_b[...], lanes([w2, w3]))


def cross_back_norm(
    spots, q, k, v, o, lse, g, ids, rows, low_b, acc, w0, w1, w2, w3, z1, gain, o_a, o_b, so0, so1, so2, so3, sums_b,
    carried,
    sent, kept, part_q, g1_ref, gs_a, gs_b, out_t, sums, all_ref, gq_ref,
):
    low = half_back(1, q, k, v, o, lse, g, ids, rows, sent, kept, part_q, sums, gq_ref)
    up = acc[...] + dot_nt(low, lanes([w0, w1])) + dot_nt(low_b[...], lanes([w2, w3]))
    g1, row_gain, row_shift = norm_back(z1[...], gain[0:1, :], up)
    all_ref[...] = carried[...]
    all_ref[10:11, :] = row_gain
    all_ref[11:12, :] = row_shift
    all_ref[12:13, :] = column_sum(g1)
    for j in range(4):
        c = slice((j % 2) * PAIR, (j % 2 + 1) * PAIR)
        of = sums if j < 2 else sums_b
        store_shard_row(all_ref, j, 0, jnp.concatenate([of[0:1, c], of[1:2, c]], axis=1))
    g1_ref[...] = g1
    g_low = g1.astype(bf16)
    g_self = dot_nt(g_low, out_rows([so0, so1, so2, so3])).astype(bf16)
    gs_a[...] = g_self[:, : 2 * PAIR]
    gs_b[...] = g_self[:, 2 * PAIR :]
    store_blocks(out_t, dot_tn(lanes([o_a, o_b]), g_low))


def finish(first, mode, n_out, *refs):
    kept, other, rows, k_w, k_x, v_w, v_x, part_q, *refs = refs
    along, sums, refs = refs[:n_out], refs[n_out], refs[n_out + 1 :]
    outs = refs if mode == "start" else refs[1:]
    both = (kept[...] + other[...].astype(f32)).astype(bf16)
    gk, gv = both[:, : 2 * PAIR], both[:, 2 * PAIR :]
    res = dot_nt(gk, lanes([k_w, k_x])) + dot_nt(gv, lanes([v_w, v_x]))
    if mode != "start":
        res = res + refs[0][...]
    part = dot_tn(rows[...], both).astype(bf16)
    for j in range(2):
        to = outs[j]
        to[0:D, :] = part_q[j]
        to[D : 2 * D, :] = part[:, j * PAIR : (j + 1) * PAIR]
        to[2 * D : 3 * D, :] = part[:, (2 + j) * PAIR : (3 + j) * PAIR]
        for n in range(n_out):
            to[(3 + n) * D : (4 + n) * D, :] = along[n][j]
        last = (3 + n_out) * D
        to[last:, :] = jnp.zeros((to.shape[0] - last, PAIR), bf16)
        if n_out == 0:
            to[last : last + 2, :] = sums[0:2, j * PAIR : (j + 1) * PAIR].astype(bf16)
        else:
            for c in range(4):
                to[last + 16 * c : last + 16 * (c + 1), :] = sums[0:16, c * PAIR : (c + 1) * PAIR].astype(bf16)
            row = 16 + 2 * (first + j)
            blocks = [(row, 0), (row, 1), (row + 1, 0), (row + 1, 1), (row + 1, 2), (row + 1, 3)]
            shard_rows = jnp.concatenate(
                [sums[r : r + 1, c * PAIR : (c + 1) * PAIR] for r, c in blocks] + [jnp.zeros((2, PAIR), f32)], axis=0
            )
            to[last + 64 : last + 72, :] = shard_rows.astype(bf16)
    if mode == "last":
        half = res.shape[0] // 2
        outs[2][...] = res[:half]
        outs[3][...] = res[half:].astype(bf16)
    else:
        outs[2][...] = res


def own_first(ids, mine, rank):
    row = lax.dynamic_index_in_dim(ids, mine, 0, True)
    size = ids.shape[1] // 4
    parts = [
        lax.dynamic_slice_in_dim(row, (rank ^ step) * size, size, 1) for step in (0, 2, 1, 3)
    ]
    return jnp.concatenate(parts, axis=1)


def per_device(
    decoder_layer_input,
    encoder_state_rows,
    target_segments,
    source_segments,
    valid_mask,
    cotangent,
    self_input_projection,
    self_in_bias,
    self_out_proj,
    cross_input_projection,
    cross_in_bias,
    cross_out_proj,
    feed_in_proj,
    feed_in_bias,
    feed_out_proj,
    out_bias,
    norm_gain,
    norm_bias,
):
    rank = lax.axis_index("tensor")
    mine = rank // 2
    first = mine == 0
    length = decoder_layer_input.shape[1]
    own = length // 2
    width = self_out_proj.shape[0]
    units = feed_in_proj.shape[1]
    spots = jnp.stack([mine, rank, rank ^ 2, rank ^ 1, rank ^ 3]).astype(jnp.int32)

    def attention_weights(in_proj, out_proj, *more):
        blocks = [out_proj[:, j * width : (j + 1) * width] for j in range(D // width)]
        return jnp.concatenate([in_proj.reshape(-1, width), *blocks, *more], axis=0)

    biases = jnp.concatenate([self_in_bias, cross_in_bias, feed_in_bias.reshape(-1, width)], axis=0)
    high = lax.reduce_precision(biases, 8, 7)
    middle = lax.reduce_precision(biases - high, 8, 7)
    low = (biases - high - middle).astype(bf16)
    high, middle = high.astype(bf16), middle.astype(bf16)
    mask_rows = valid_mask.astype(bf16).reshape(2, -1, width)
    mask_kept = jnp.where(first, mask_rows[0], mask_rows[1])
    mask_sent = jnp.where(first, mask_rows[1], mask_rows[0])
    self_shard = attention_weights(
        self_input_projection, self_out_proj, high, middle, low, mask_sent, mask_kept, jnp.zeros((4, width), bf16)
    )
    ids = jnp.concatenate(
        [own_first(target_segments, mine, rank), own_first(source_segments, mine, rank)], axis=0
    )
    self_near = [self_shard, partner(self_shard, 1)]
    self_across = partner(self_shard, 2)

    half_shapes = [
        shape((own, 2 * PAIR), bf16), shape((length, 2 * PAIR), bf16), shape((length, 2 * PAIR), bf16),
        shape((own, 2 * PAIR), bf16), shape((own, PAIR), f32),
    ]
    full = (own, D)
    sums_shape = shape((32, D), f32)

    def parts(index, packs, at):
        return list(packs), {at + i: pack_part(index) for i in range(len(packs))}

    def tails(packs, at):
        return list(packs), {at + i: PACK_TAIL for i in range(len(packs))}

    def laid(operands, *groups):
        blocks = {}
        for group in groups:
            if isinstance(group, tuple):
                more, places = group[0](*group[1:], len(operands))
                operands = operands + more
                blocks.update(places)
            else:
                operands = operands + group
        return operands, blocks

    def sequence(array, at):
        return [array], {at: of_sequence(array)}

    def self_half(shards, x):
        operands, blocks = laid(
            [spots], (sequence, x), (parts, 0, shards), (parts, 1, shards), (parts, 2, shards), (tails, shards), [ids]
        )
        return kernel_call(self_forward, "self_forward", half_shapes, operands, blocks=blocks)

    cross_shard = attention_weights(cross_input_projection, cross_out_proj)
    cross_piece = half_here(cross_shard, 1)
    feed_piece = half_here(feed_in_proj, 1)
    q_a, k_a, v_a, o_a, lse_a = self_half(self_near, tie(decoder_layer_input, cross_piece, feed_piece))
    feed_in_1, feed_out_1, cot_1, cross_piece, feed_piece, cross_shard = tie(
        (feed_in_proj, feed_out_proj, cotangent, cross_piece, feed_piece, cross_shard), q_a
    )
    cot_sent = lax.dynamic_index_in_dim(cot_1, 1 - mine, 0, False).astype(bf16)
    self_far = [self_across, partner(tie(self_across, cot_sent), 1)]
    self_all = self_near + self_far
    cross_got, feed_got = partner(cross_piece, 2), partner(feed_piece, 2)
    q_b, k_b, v_b, o_b, lse_b = self_half(self_far, decoder_layer_input)
    cross_near = [cross_shard, partner(tie(cross_shard, self_across), 1)]
    cross_got, feed_got, cot_sent, feed_in_1, feed_out_1 = tie((cross_got, feed_got, cot_sent, feed_in_1, feed_out_1), q_b)
    cross_got_x, feed_got_x = partner_dp(cross_got, 1), partner_dp(feed_got, 1)
    cut = feed_out_1.shape[0] // 2
    out_top, cot_other = partner(feed_out_1[:cut], 2), partner(cot_sent, 2)
    operands, blocks = laid(
        [spots, o_a, tie(o_b, cross_got, feed_got)], (parts, 3, self_all), (sequence, decoder_layer_input),
        (sequence, encoder_state_rows), (parts, 0, cross_near), (parts, 1, cross_near), (parts, 2, cross_near),
        (tails, self_all[:3]), [ids, out_bias, norm_gain, norm_bias],
    )
    s1, z1, cq_a, ck_a, cv_a, co_a, clse_a, sums, x_own, e_own = kernel_call(
        cross_first,
        "cross_first",
        [shape(full, bf16), shape(full, f32), *half_shapes, sums_shape, shape(full, bf16), shape(full, bf16)],
        operands,
        blocks=blocks,
    )
    cross_got, cross_got_x, feed_got, feed_got_x, out_top, cot_other, feed_in_1, feed_out_1 = tie(
        (cross_got, cross_got_x, feed_got, feed_got_x, out_top, cot_other, feed_in_1, feed_out_1), s1
    )
    cross_across = in_order(cross_got, cross_got_x, 1)
    cross_far = [cross_across, partner(cross_across, 1)]
    cross_all = cross_near + cross_far
    feed_in_across = in_order(feed_got, feed_got_x, 1)
    out_rest = partner(feed_out_1[cut:], 2)
    feed_in_other, feed_out_other = partner(feed_in_1, 1), partner(feed_out_1, 1)
    operands, blocks = laid(
        [spots, tie(s1, feed_in_across, out_top, cot_other), co_a], (sequence, encoder_state_rows),
        (parts, 0, cross_far), (parts, 1, cross_far), (parts, 2, cross_far), (parts, 3, cross_all),
        (tails, [self_all[0], self_all[2], self_all[3]]), [ids, out_bias, norm_gain, norm_bias, sums],
    )
    cq_b, ck_b, cv_b, co_b, clse_b, s2, z2, sums = kernel_call(
        cross_second,
        "cross_second",
        [*half_shapes, shape(full, bf16), shape(full, f32), sums_shape],
        operands,
        blocks=blocks,
    )
    out_top, out_rest = tie((out_top, out_rest), s2)
    feed_out_across = jnp.concatenate([out_top, out_rest], axis=0)
    feed_in_all = [feed_in_1, feed_in_other, feed_in_across, partner(feed_in_across, 1)]
    feed_out_all = [feed_out_1, feed_out_other, feed_out_across, partner(feed_out_across, 1)]

    operands, blocks = laid(
        [spots, s2, z2, *feed_in_all, *feed_out_all], (tails, self_all), [out_bias, norm_gain, norm_bias],
        (sequence, cotangent), [cot_other], (parts, 3, cross_all), [co_a, co_b, sums],
    )
    half = (own, 2 * PAIR)
    out_kept, out_sent, feed_sent, feed_kept, g2, g_cross_a, g_cross_b, cross_out_t, sums = kernel_call(
        feed,
        "feed",
        [
            shape((own // 2, D), bf16), shape((own // 2, D), bf16),
            shape((2, D + units, D), bf16), shape((2, D + units, D), bf16),
            shape(full, f32), shape(half, bf16), shape(half, bf16), shape((4, D, PAIR), bf16), sums_shape,
        ],
        operands,
        scratch=[pltpu.VMEM((4, own, units), f32), pltpu.VMEM((4, own, units), bf16)],
        blocks=blocks,
    )
    feed_got = partner(feed_sent, 1)
    out_got = partner(out_sent, 2)

    kv_shapes = [shape(full, bf16), shape(full, f32), shape((2, D, PAIR), bf16)]

    def back_far(source, heads, g, rows):
        return kernel_call(
            lambda *refs: far_back(source, *refs),
            "attention_back",
            [*kv_shapes, shape(half, bf16), shape((8, D), f32)],
            [*heads, g, ids, rows],
            smem=0,
            scratch=[pltpu.VMEM(half, f32)],
        )

    def finished(first_pair, mode, kept, got, rows, shards, part, along, small, acc=None):
        n_out = len(along)
        last = [shape((own // 2, D), f32), shape((own // 2, D), bf16)] if mode == "last" else [shape(full, f32)]
        count = (3 + n_out) * D + (96 if n_out else 64)
        operands, blocks = laid([kept, got, rows], (parts, 1, shards), (parts, 2, shards), [part])
        if n_out:
            blocks.update(
                {len(operands) + n: ((2, D, PAIR), lambda *scalars: (first_pair // 2, 0, 0)) for n in range(n_out)}
            )
        return kernel_call(
            lambda *refs: finish(first_pair, mode, n_out, *refs),
            "finish",
            [shape((count, width), bf16), shape((count, width), bf16), *last],
            operands + list(along) + [small] + ([] if acc is None else [acc]),
            smem=0,
            blocks=blocks,
            us=2,
        )

    def added(*parts):
        total = parts[0].astype(f32)
        for part in parts[1:]:
            total = total + part.astype(f32)
        return total

    gkv_sent_b, gkv_kept_b, part_b, low_b, sums_b = back_far(1, [cq_b, ck_b, cv_b, co_b, clse_b], g_cross_b, s1)
    gkv_got_b = partner(gkv_sent_b, 1)
    feed_kept, feed_got = tie((feed_kept, feed_got), low_b)

    def half_of(rows, sent):
        cut = rows.shape[-2] // 2
        upper = (lax.axis_index("dp") & 1) != 0
        first, second = rows[..., :cut, :], rows[..., cut:, :]
        return jnp.where(upper, first, second) if sent else jnp.where(upper, second, first)

    in_y = added(feed_kept[1, :D], feed_got[1, :D]).astype(bf16)
    out_x = added(half_of(feed_kept[:, D:], True), half_of(feed_got[:, D:], True)).astype(bf16)
    in_y_got, out_x_got = partner(in_y, 2), partner_dp(out_x, 1)
    operands, blocks = laid(
        [spots, cq_a, ck_a, cv_a, co_a, clse_a, g_cross_a, ids, s1, tie(low_b, in_y, out_x, out_got), g2],
        (parts, 0, cross_all), [z1, norm_gain, o_a, o_b], (parts, 3, self_all), [sums_b, sums],
    )
    gkv_sent, gkv_kept, part_a, g1, g_self_a, g_self_b, self_out_t, sums_a, sums = kernel_call(
        cross_back_norm,
        "cross_back_norm",
        [
            *kv_shapes, shape(full, f32), shape(half, bf16), shape(half, bf16), shape((4, D, PAIR), bf16),
            shape((8, D), f32), sums_shape,
        ],
        operands,
        scratch=[pltpu.VMEM(half, f32)],
        blocks=blocks,
    )
    gkv_got = partner(gkv_sent, 1)
    cb_kept, cb_sent, enc_acc = finished(
        2, "start", gkv_kept_b, gkv_got_b, tie(e_own, g1), cross_far, part_b, [cross_out_t, self_out_t], sums
    )
    cb_got = partner(cb_sent, 1)
    in_y_got, out_x_got, feed_kept, feed_got = tie((in_y_got, out_x_got, feed_kept, feed_got), enc_acc)
    in_x = added(half_of(feed_kept[0, :D], True), half_of(feed_got[0, :D], True), half_of(in_y_got, True)).astype(bf16)
    out_y = added(half_of(feed_kept[1, D:], False), half_of(feed_got[1, D:], False), out_x_got[1]).astype(bf16)
    in_x_got, out_y_got = partner_dp(in_x, 1), partner(out_y, 2)
    cb_kept, cb_got = tie((cb_kept, cb_got), in_x, out_y)
    cross_b = added(cb_kept, cb_got).astype(bf16)
    cut = cross_b.shape[0] // 2
    cross_y = [partner(cross_b[:cut], 2), None]

    gkv_sent_b, gkv_kept_b, part_b, low_b, sums_b = back_far(
        0, [q_b, k_b, v_b, o_b, lse_b], g_self_b, tie(x_own, enc_acc, in_x, out_y, cross_b)
    )
    gkv_got_b = partner(gkv_sent_b, 1)
    in_x_got, out_y_got, cross_y[0] = tie((in_x_got, out_y_got, cross_y[0]), low_b)
    cross_y[1] = partner(tie(cross_b[cut:], cross_y[0]), 2)
    feed_total = jnp.stack(
        [
            added(half_of(feed_kept[0, :D], False), half_of(feed_got[0, :D], False), half_of(in_y_got, False), in_x_got),
            added(half_of(feed_kept[0, D:], False), half_of(feed_got[0, D:], False), out_x_got[0], out_y_got),
        ]
    )
    feed_sum = DpSum(feed_total, dp_bits()[1:])
    ca_kept, ca_sent, enc_kept, enc_sent = finished(
        0, "last", gkv_kept, gkv_got, tie(e_own, cross_y[0], feed_sum.value), cross_near, part_a,
        [cross_out_t, self_out_t], sums, enc_acc,
    )
    ca_got = partner(ca_sent, 1)
    sb_kept, sb_sent, acc = finished(
        2, "middle", gkv_kept_b, gkv_got_b, tie(x_own, enc_kept), self_far, part_b, [], sums_b, g1
    )
    sb_got = partner(sb_sent, 1)
    feed_sum.step(acc)
    self_b = added(sb_kept, sb_got).astype(bf16)
    self_y = partner(self_b, 2)
    cross_y, ca_kept, ca_got = tie((cross_y, ca_kept, ca_got), self_b, feed_sum.value)
    cross_sum = DpSum(added(ca_kept, ca_got, jnp.concatenate(cross_y, axis=0)), dp_bits())
    operands, blocks = laid(
        [q_a, k_a, v_a, o_a, lse_a, g_self_a, ids, x_own, tie(low_b, self_b, feed_sum.value, cross_sum.value), acc],
        (parts, 0, self_all),
    )
    gkv_sent, gkv_kept, part_a, acc, sums_a = kernel_call(
        self_back,
        "self_back",
        [*kv_shapes, shape(full, f32), shape((8, D), f32)],
        operands,
        smem=0,
        scratch=[pltpu.VMEM(half, f32)],
        blocks=blocks,
    )
    gkv_got = partner(gkv_sent, 1)
    feed_sum.step(acc)
    cross_sum.step(acc)
    sa_kept, sa_sent, in_kept, in_sent = finished(
        0, "last", gkv_kept, gkv_got, x_own, self_near, part_a, [], sums_a, acc
    )
    sa_got = partner(sa_sent, 1)
    self_y = tie(self_y, in_kept)
    self_sum = DpSum(added(sa_kept, sa_got, self_y), dp_bits())
    enc_sent, in_sent = tie((enc_sent, in_sent), self_sum.value)
    enc_got, in_got = partner(enc_sent, 2), partner(in_sent, 2)

    def to_owner(kept, other):
        other = other.astype(kept.dtype)
        return jnp.stack([jnp.where(first, kept, other), jnp.where(first, other, kept)])

    def in_grad(total):
        return total[: 3 * D].reshape(3, D, width).astype(f32)

    def out_grad(total):
        blocks = [total[c * width : (c + 1) * width] for c in range(D // width)]
        return jnp.concatenate(blocks, axis=1).astype(f32)

    self_sum.step()
    feed_sum.step(self_sum.value)
    cross_sum.step(feed_sum.value)
    self_sum.step()
    cross_sum.step(self_sum.value)
    feed_total = feed_sum.finish(cross_sum.value)
    layer_output = to_owner(out_kept, tie(out_got, self_sum.value))
    feed_total = tie(feed_total, self_sum.value)
    feed_in_grad, feed_out_grad = feed_total[0].astype(f32), feed_total[1].astype(f32)
    encoder_grad = to_owner(enc_kept, tie(enc_got, self_sum.value))
    self_sum.step(layer_output, feed_in_grad)
    cross_sum.step(self_sum.value, encoder_grad, feed_out_grad)
    input_grad = to_owner(in_kept, tie(in_got, self_sum.value))
    cross_total = cross_sum.finish(self_sum.value)
    self_sum.step(cross_total, input_grad)
    cross_total = tie(cross_total, self_sum.value)
    cross_in_grad, cross_out_grad = in_grad(cross_total), out_grad(cross_total[3 * D : 4 * D])
    self_out_grad = out_grad(cross_total[4 * D : 5 * D])
    common = cross_total[5 * D : 5 * D + 64].astype(f32).reshape(4, 16, PAIR).swapaxes(0, 1).reshape(16, 4 * PAIR)
    shard_sums = cross_total[5 * D + 64 : 5 * D + 72].astype(f32)
    rms_values = jnp.sqrt(jnp.sum(common[0:4], axis=1) / (jnp.sum(common[13]) * D))
    self_total = self_sum.finish(cross_in_grad, cross_out_grad, self_out_grad, common, shard_sums, rms_values)

    return (
        layer_output,
        input_grad,
        encoder_grad,
        in_grad(self_total),
        self_total[3 * D : 3 * D + 2].astype(f32),
        self_out_grad,
        cross_in_grad,
        shard_sums[0:2],
        cross_out_grad,
        feed_in_grad,
        shard_sums[2:6].reshape(units),
        feed_out_grad,
        jnp.stack([common[12], common[9], common[6]]),
        jnp.stack([common[10], common[7], common[4]]),
        jnp.stack([common[11], common[8], common[5]]),
        rms_values,
    )


def solution(mesh):
    return jax.shard_map(
        per_device,
        mesh=mesh,
        in_specs=(
            P("dp", None, None),
            P("dp", None, None),
            P("dp", None),
            P("dp", None),
            P("dp", "tensor"),
            P("dp", "tensor", None),
            P(None, None, "tensor"),
            P(None, "tensor"),
            P("tensor", None),
            P(None, None, "tensor"),
            P(None, "tensor"),
            P("tensor", None),
            P(None, "tensor"),
            P("tensor"),
            P("tensor", None),
            P(),
            P(),
            P(),
        ),
        out_specs=(
            P("dp", "tensor", None),
            P("dp", "tensor", None),
            P("dp", "tensor", None),
            P(None, None, "tensor"),
            P(None, "tensor"),
            P("tensor", None),
            P(None, None, "tensor"),
            P(None, "tensor"),
            P("tensor", None),
            P(None, "tensor"),
            P("tensor"),
            P("tensor", None),
            P(),
            P(),
            P(),
            P(),
        ),
        check_vma=False,
    )
```
